32 devices in a mesh: img: 8 (over z, x), lat: 4 (over y, core).
Axes of the slice: x: 2, y: 2, z: 4, core: 2. Of those that a mesh axis runs over, the one named last changes fastest.
Arguments:
- media: bfloat16 [64, 576, 1024], P('img', 'lat'), may hold values from -6 to 6
- latents: bfloat16 [64, 64, 1024], P('img', 'lat'), may hold values from -6 to 6
- bucket: int32 [64], P('img'), may hold values from 0 to 1, as said below
- gain_media: bfloat16 [1024], P(('img', 'lat')), may hold values from 0.099609375 to 1.8984375
- shift_media: bfloat16 [1024], P(('img', 'lat')), may hold values from -3 to 3
- gain_latent: bfloat16 [1024], P(('img', 'lat')), may hold values from 0.099609375 to 1.8984375
- shift_latent: bfloat16 [1024], P(('img', 'lat')), may hold values from -3 to 3
- gain_mlp: bfloat16 [1024], P(('img', 'lat')), may hold values from 0.099609375 to 1.8984375
- shift_mlp: bfloat16 [1024], P(('img', 'lat')), may hold values from -3 to 3
- w_query: bfloat16 [1024, 512], P(('img', 'lat')), may hold values from -0.1875 to 0.1875
- w_keyvalue: bfloat16 [1024, 1024], P(('img', 'lat')), may hold values from -0.1875 to 0.1875
- w_output: bfloat16 [512, 1024], P(('img', 'lat')), may hold values from -3 to 3
- w_up: bfloat16 [1024, 4096], P(('img', 'lat')), may hold values from -0.1875 to 0.1875
- w_down: bfloat16 [4096, 1024], P(('img', 'lat')), may hold values from -0.09375 to 0.09375
- cotangent: bfloat16 [64, 64, 1024], P('img', 'lat'), may hold values from -6 to 6
Outputs:
- latents_out: bfloat16 [64, 64, 1024], P('img', 'lat')
- grad_media: float32 [64, 576, 1024], P('img', 'lat')
- grad_latents: float32 [64, 64, 1024], P('img', 'lat')
- grad_gain_media: float32 [1024], P(('img', 'lat'))
- grad_shift_media: float32 [1024], P(('img', 'lat'))
- grad_gain_latent: float32 [1024], P(('img', 'lat'))
- grad_shift_latent: float32 [1024], P(('img', 'lat'))
- grad_gain_mlp: float32 [1024], P(('img', 'lat'))
- grad_shift_mlp: float32 [1024], P(('img', 'lat'))
- grad_w_query: float32 [1024, 512], P(('img', 'lat'))
- grad_w_keyvalue: float32 [1024, 1024], P(('img', 'lat'))
- grad_w_output: float32 [512, 1024], P(('img', 'lat'))
- grad_w_up: float32 [1024, 4096], P(('img', 'lat'))
- grad_w_down: float32 [4096, 1024], P(('img', 'lat'))
The draws below stay inside these ranges and needn't reach their ends.
Inputs may be any that keep to these rules, and one draw needn't show every extreme that they name: `bucket`: 0 marks an image of 256 patches and 1 one of 576; among the 8 images of each index of img at least one has 576 patches.
All inputs are finite; a program needn't handle non-finite values.
Results may differ from the reference program's by a relative error of at most 0.014.
Values may be sent and summed in bfloat16 or wider, within the bound.
A program may use at most 192 MiB of HBM per device.

```python
import jax
import jax.numpy as jnp
from jax import lax

D = 1024
HEADS = 8
HEAD = 64
FF = 4096
LAT = 64
SHORT = 256
LONG = 576
IMG_DEV = 8
IMAGES = 64
INNER = 512
N_IMG = 8


def draw_bucket(key, part):
    key = jax.random.fold_in(key, 11)
    first_key, second_key = jax.random.split(key)
    coins = jax.random.randint(first_key, (IMAGES,), 0, 2)
    chosen = jax.random.randint(second_key, (IMAGES // IMG_DEV, 1), 0, IMG_DEV)
    forced = (jnp.arange(IMG_DEV)[None, :] == chosen).astype(jnp.int32)
    merged = jnp.maximum(coins.reshape(IMAGES // IMG_DEV, IMG_DEV), forced)
    return merged.reshape(IMAGES).astype(jnp.int32)


def levels(stream_key, dims, pieces, low, high):
    factor_of, own = 1.0, jax.random.fold_in(stream_key, 6)
    for position, parts in pieces:
        steps = jnp.exp(jax.random.uniform(jax.random.fold_in(own, position), (parts,), jnp.float32, low / len(pieces), high / len(pieces)))
        factor_of = factor_of * jnp.repeat(steps, dims[position] // parts).reshape([-1 if axis == position else 1 for axis in range(len(dims))])
    return factor_of


def bell_draw(own_key, dims, scale, limit, shards=(), kind=jnp.bfloat16):
    loudness = levels(own_key, dims, shards, -0.22, 0.18) if shards else 1.0
    array = jax.random.normal(own_key, dims, jnp.float32) * scale * loudness
    return jnp.minimum(jnp.maximum(array, -limit), limit).astype(kind)


def setup_inputs(seed: int = 0) -> dict:
    arg_keys = jax.random.split(jax.random.key(seed), 16)
    return {
        "media": bell_draw(arg_keys[0], (IMAGES, LONG, D), 1.0, 6.0, ((0, 8), (1, 4))),
        "latents": bell_draw(arg_keys[1], (IMAGES, LAT, D), 1.0, 6.0, ((0, 8), (1, 4))),
        "bucket": draw_bucket(jax.random.fold_in(arg_keys[15], 71), 0),
        "gain_media": jnp.clip(1.0 + 0.18 * jax.random.normal(arg_keys[3], (D,), jnp.float32), 0.099609375, 1.8984375).astype(jnp.bfloat16),
        "shift_media": bell_draw(arg_keys[4], (D,), 0.5, 3.0, ((0, 32),)),
        "gain_latent": jnp.clip(1.0 + 0.18 * jax.random.normal(arg_keys[5], (D,), jnp.float32), 0.099609375, 1.8984375).astype(jnp.bfloat16),
        "shift_latent": bell_draw(arg_keys[6], (D,), 0.5, 3.0, ((0, 32),)),
        "gain_mlp": jnp.clip(1.0 + 0.18 * jax.random.normal(arg_keys[7], (D,), jnp.float32), 0.099609375, 1.8984375).astype(jnp.bfloat16),
        "shift_mlp": bell_draw(arg_keys[8], (D,), 0.5, 3.0, ((0, 32),)),
        "w_query": bell_draw(arg_keys[9], (D, INNER), D ** -0.5, 0.1875, ((0, 32),)),
        "w_keyvalue": bell_draw(arg_keys[10], (D, 2 * INNER), D ** -0.5, 0.1875, ((0, 32),)),
        "w_output": bell_draw(arg_keys[11], (INNER, D), 4 ** -0.5, 3.0, ((0, 32),)),
        "w_up": bell_draw(arg_keys[12], (D, FF), D ** -0.5, 0.1875, ((0, 32),)),
        "w_down": bell_draw(arg_keys[13], (FF, D), FF ** -0.5, 0.09375, ((0, 32),)),
        "cotangent": bell_draw(arg_keys[14], (IMAGES, LAT, D), 1.0, 6.0, ((0, 8), (1, 4))),
    }


EPS = 1e-05
SCALE = 0.125
NEG = -1e+30
HIGHEST = lax.Precision.HIGHEST

@jax.custom_vjp
def low(v):
    return lax.optimization_barrier(v.astype(jnp.bfloat16)).astype(jnp.float32)

@jax.custom_vjp
def low_back(v):
    return v

def low_keep(v):
    return (low(v), None)

def low_pass(kept, grad):
    return (grad,)

def back_keep(v):
    return (v, None)

def back_low(kept, grad):
    return (low(grad),)
low.defvjp(low_keep, low_pass)
low_back.defvjp(back_keep, back_low)

def layer_norm(values, norm_gain, norm_shift):
    row_mean = lax.optimization_barrier(jnp.mean(values, axis=-1, keepdims=True))
    centred = values - row_mean
    spread = lax.optimization_barrier(jnp.mean(centred * centred, axis=-1, keepdims=True))
    return centred * lax.rsqrt(spread + EPS) * norm_gain + norm_shift

def dense(values, weight):
    return jnp.einsum('gtd,de->gte', values, weight, precision=HIGHEST)

def layer(media_in, latent_in, lengths, weights):
    g_media, s_media, g_latent, s_latent, g_mlp, s_mlp, query_weight, pair_weight, out_weight, up_weight, down_weight = weights
    inner = query_weight.shape[1]
    groups = media_in.shape[0]
    media_low = low(layer_norm(media_in, g_media, s_media))
    latent_low = low(layer_norm(latent_in, g_latent, s_latent))
    pair_media = low_back(low(dense(media_low, pair_weight)))
    pair_latent = low_back(low(dense(latent_low, pair_weight)))
    query_low = low_back(low(dense(latent_low, query_weight)))
    pairs = jnp.concatenate([pair_media, pair_latent], axis=1)
    keys = pairs[..., :inner].reshape(groups, -1, HEADS, HEAD)
    values = pairs[..., inner:].reshape(groups, -1, HEADS, HEAD)
    queries = query_low.reshape(groups, -1, HEADS, HEAD)
    scores = low_back(jnp.einsum('gqhd,gkhd->ghqk', queries, keys, precision=HIGHEST) * SCALE)
    positions = jnp.arange(pairs.shape[1], dtype=jnp.int32)
    valid = (positions[None, :] < lengths[:, None]) | (positions[None, :] >= LONG)
    scores = jnp.where(valid[:, None, None, :], scores, NEG)
    probs = low(jax.nn.softmax(scores, axis=-1))
    mixed = jnp.einsum('ghqk,gkhd->gqhd', probs, values, precision=HIGHEST).reshape(groups, -1, inner)
    mixed = low_back(low(mixed))
    resid = latent_in + low_back(dense(mixed, out_weight))
    mlp_low = low(layer_norm(resid, g_mlp, s_mlp))
    gate = low_back(dense(mlp_low, up_weight))
    active = low(jax.nn.gelu(gate, approximate=False))
    return resid + low_back(dense(active, down_weight))

def reference(media, latents, bucket, gain_media, shift_media, gain_latent, shift_latent, gain_mlp, shift_mlp, w_query, w_keyvalue, w_output, w_up, w_down, cotangent):
    params = tuple((member.astype(jnp.float32) for member in (gain_media, shift_media, gain_latent, shift_latent, gain_mlp, shift_mlp, w_query, w_keyvalue, w_output, w_up, w_down)))
    media_groups = media.reshape(N_IMG, IMG_DEV, LONG, D)
    latent_groups = latents.reshape(N_IMG, IMG_DEV, LAT, D)
    bucket_groups = bucket.reshape(N_IMG, IMG_DEV)
    cot_groups = cotangent.reshape(N_IMG, IMG_DEV, LAT, D)

    def one_group(totals, inputs):
        media_part, latent_part, bucket_part, cot_part = inputs
        lengths = (SHORT + (LONG - SHORT) * bucket_part).astype(jnp.int32)

        def forward(media_in, latent_in, *weights):
            return layer(media_in, latent_in, lengths, weights)
        result, pull = jax.vjp(forward, media_part.astype(jnp.float32), latent_part.astype(jnp.float32), *params)
        gradients = pull(cot_part.astype(jnp.float32))
        totals = tuple((first + second for first, second in zip(totals, gradients[2:])))
        return (totals, (result.astype(jnp.bfloat16), gradients[0], gradients[1]))
    zeros_start = tuple((jnp.zeros_like(member) for member in params))
    totals, stacked = lax.scan(one_group, zeros_start, (media_groups, latent_groups, bucket_groups, cot_groups))
    latents_out = stacked[0].reshape(IMAGES, LAT, D)
    grad_media = stacked[1].reshape(IMAGES, LONG, D)
    grad_latents = stacked[2].reshape(IMAGES, LAT, D)
    return (latents_out, grad_media, grad_latents, totals[0], totals[1], totals[2], totals[3], totals[4], totals[5], totals[6], totals[7], totals[8], totals[9], totals[10])
```

```python
import jax
import jax.numpy as jnp
from jax import lax
from jax.experimental import pallas as pl
from jax.experimental.pallas import tpu as pltpu
from jax.sharding import PartitionSpec as P

MESH = pl.DeviceIdType.MESH
BF16 = jnp.bfloat16
F32 = jnp.float32

SHORT = 256
LONG = 576
HEADS = 8
EPS = 1e-05
SCALE = 0.125
NEG = -1e30

BLOCK = 8

KV = (0, 1024)
QU = (1024, 512)
GN = (1536, 128)
OUT = (1664, 512)
WIDE = 2176
URGENT = 1664


def mm(a, b):
    return lax.dot_general(a, b, (((1,), (0,)), ((), ())), preferred_element_type=F32)


def mm_nt(a, b):
    return lax.dot_general(a, b, (((1,), (1,)), ((), ())), preferred_element_type=F32)


def mm_tn(a, b):
    return lax.dot_general(a, b, (((0,), (0,)), ((), ())), preferred_element_type=F32)


def cols(span):
    return pl.ds(span[0], span[1])


def flat(values):
    return values.reshape(-1, values.shape[-1])


def normal(values):
    mean = jnp.mean(values, axis=-1, keepdims=True)
    centred = values - mean
    spread = jnp.mean(centred * centred, axis=-1, keepdims=True)
    return mean, lax.rsqrt(spread + EPS)


def norm_back(upstream, normed, rstd, gain):
    scaled = upstream * gain
    first = jnp.mean(scaled, axis=-1, keepdims=True)
    second = jnp.mean(scaled * normed, axis=-1, keepdims=True)
    return (scaled - first - normed * second) * rstd


class Place:
    def __init__(self):
        img = lax.axis_index("img")
        lat = lax.axis_index("lat")
        self.i = lax.rem(img, BLOCK)
        self.base = img - self.i
        self.z = lax.div(self.i, 2)
        self.x = lax.rem(self.i, 2)
        self.l = lat
        self.y = lax.div(lat, 2)
        self.c = lax.rem(lat, 2)
        self.z1 = self.z + 1 - 2 * lax.rem(self.z, 2)
        self.z2 = lax.rem(self.z + 2, 4)
        self.z3 = 3 - self.z
        self.mid = jnp.logical_or(self.z == 1, self.z == 2)
        self.end = jnp.logical_or(self.z == 0, self.z == 3)
        self.p = self.x * 2 + self.y
        self.q = self.z * 4 + self.p
        self.px = (1 - self.x) * 2 + self.y
        self.py = self.x * 2 + 1 - self.y
        self.pd = 3 - self.p
        self.lc = self.y * 2 + 1 - self.c
        self.ly = (1 - self.y) * 2 + self.c
        self.ld = 3 - self.l
        self.core = self.dev(self.z, self.x, self.y, 1 - self.c)
        self.xn = self.dev(self.z, 1 - self.x, self.y, self.c)
        self.yn = self.dev(self.z, self.x, 1 - self.y, self.c)
        self.diag = self.dev(self.z, 1 - self.x, 1 - self.y, self.c)
        self.ycore = self.dev(self.z, self.x, 1 - self.y, 1 - self.c)
        self.zn1 = self.dev(self.z1, self.x, self.y, self.c)
        self.zn2 = self.dev(self.z2, self.x, self.y, self.c)
        self.zn3 = self.dev(self.z3, self.x, self.y, self.c)

    def dev(self, z, x, y, c):
        return (self.base + z * 2 + x, y * 2 + c)

    def greet(self):
        barrier = pltpu.get_barrier_semaphore()
        peers = (self.core, self.xn, self.yn, self.diag, self.ycore, self.zn1, self.zn2, self.zn3)
        for peer in peers:
            pl.semaphore_signal(barrier, inc=1, device_id=peer, device_id_type=MESH)
        pl.semaphore_wait(barrier, len(peers))


def guarded(when, action):
    if when is None:
        action()
    else:
        pl.when(when)(action)


class Msg:
    def __init__(self, post, src, dst, dev, into, key=None, when=None):
        self.k = post.count
        post.count += 1
        self.key = self.k if key is None else key
        self.when = when
        self.post, self.src, self.dst, self.dev, self.into = post, src, dst, dev, into
        post.all.append(self)

    def copy(self, src, dst):
        return pltpu.make_async_remote_copy(
            src_ref=src,
            dst_ref=dst,
            send_sem=self.post.send.at[self.k],
            recv_sem=self.post.recv.at[self.key],
            device_id=self.dev,
            device_id_type=MESH,
        )

    def start(self):
        guarded(self.when, lambda: self.copy(self.src, self.dst).start())

    def arrived(self):
        self.copy(self.into, self.into).wait_recv()

    def sent(self):
        guarded(self.when, lambda: self.copy(self.src, self.dst).wait_send())


class Post:
    def __init__(self, send, recv):
        self.send = send
        self.recv = recv
        self.count = 0
        self.all = []

    def msg(self, *a, **k):
        return Msg(self, *a, **k)

    def drain(self):
        for m in self.all:
            m.sent()


class ZGather:
    def __init__(self, post, at, view):
        own = view(at.z)
        self.m1 = post.msg(own, own, at.zn1, view(at.z1))
        self.m2 = post.msg(own, own, at.zn2, view(at.z2))
        self.m3 = post.msg(own, own, at.zn3, view(at.z3), when=at.mid)
        self.relay = post.msg(view(at.z2), view(at.z2), at.zn1, view(at.z3), key=self.m3.k, when=at.mid)

    def start(self):
        self.m1.start()
        self.m2.start()
        self.m3.start()

    def near(self):
        self.m1.arrived()

    def far(self):
        self.m2.arrived()
        self.relay.start()

    def last(self):
        self.m3.arrived()


class PlaneGather:
    def __init__(self, post, at, view, half):
        own = view(at.x, at.y)
        ox, oy = 1 - at.x, 1 - at.y
        self.mx = post.msg(own, own, at.xn, view(ox, at.y))
        self.my = post.msg(own, own, at.yn, view(at.x, oy))
        self.hy = post.msg(half(ox, at.y, 0), half(ox, at.y, 0), at.yn, half(ox, oy, 0))
        self.hx = post.msg(half(at.x, oy, 1), half(at.x, oy, 1), at.xn, half(ox, oy, 1))

    def start(self):
        self.mx.start()
        self.my.start()

    def relay(self):
        self.mx.arrived()
        self.hy.start()
        self.my.arrived()
        self.hx.start()

    def last(self):
        self.hy.arrived()
        self.hx.arrived()


class LatGather:
    def __init__(self, post, at, view):
        self.mc = post.msg(view(at.l), view(at.l), at.core, view(at.lc))
        self.my = post.msg(view(at.l), view(at.l), at.yn, view(at.ly))
        self.fc = post.msg(view(at.ly), view(at.ly), at.core, view(at.ld))

    def start(self):
        self.my.start()
        self.mc.start()

    def relay(self):
        self.my.arrived()
        self.fc.start()

    def last(self):
        self.mc.arrived()
        self.fc.arrived()


class LatReduce:
    def __init__(self, post, at, parts, first, second):
        self.at, self.parts, self.first, self.second = at, parts, first, second
        self.m0 = post.msg(parts.at[at.lc], first.at[0], at.core, first.at[0])
        self.m1 = post.msg(parts.at[at.ld], first.at[1], at.core, first.at[1])
        self.m2 = post.msg(parts.at[at.ly], second, at.yn, second)

    def start(self):
        self.m1.start()
        self.m0.start()

    def relay(self):
        self.m1.arrived()
        ly = self.at.ly
        self.parts[ly] = (self.parts[ly].astype(F32) + self.first[1].astype(F32)).astype(BF16)
        self.m2.start()

    def total(self):
        self.m0.arrived()
        self.m2.arrived()
        near = self.parts[self.at.l].astype(F32) + self.first[0].astype(F32)
        return near + self.second[...].astype(F32)


class PlaneReduce:
    def __init__(self, post, at, part, by, bx, b2):
        x, y = at.x, at.y
        ox, oy = 1 - x, 1 - y
        self.part, self.by, self.bx, self.b2 = part, by, bx, b2
        self.x, self.y, self.ox, self.oy = x, y, ox, oy
        self.my1 = post.msg(part(ox, oy, 0), by.at[1], at.yn, by.at[1])
        self.mx1 = post.msg(part(ox, oy, 1), bx.at[1], at.xn, bx.at[1])
        self.my0 = post.msg(part(x, oy, 0), by.at[0], at.yn, by.at[0])
        self.mx0 = post.msg(part(ox, y, 1), bx.at[0], at.xn, bx.at[0])
        self.f0 = post.msg(part(ox, y, 0), b2.at[0], at.xn, b2.at[0])
        self.f1 = post.msg(part(x, oy, 1), b2.at[1], at.yn, b2.at[1])

    def start(self):
        self.my1.start()
        self.mx1.start()
        self.my0.start()
        self.mx0.start()

    def relay(self):
        self.my1.arrived()
        there = self.part(self.ox, self.y, 0)
        there[...] = (there[...].astype(F32) + self.by[1].astype(F32)).astype(BF16)
        self.f0.start()
        self.mx1.arrived()
        there = self.part(self.x, self.oy, 1)
        there[...] = (there[...].astype(F32) + self.bx[1].astype(F32)).astype(BF16)
        self.f1.start()

    def total(self):
        self.my0.arrived()
        self.f0.arrived()
        low = self.part(self.x, self.y, 0)[...].astype(F32) + self.by[0].astype(F32) + self.b2[0].astype(F32)
        self.mx0.arrived()
        self.f1.arrived()
        high = self.part(self.x, self.y, 1)[...].astype(F32) + self.bx[0].astype(F32) + self.b2[1].astype(F32)
        return low, high


class ZReduce:
    def __init__(self, post, at, term, bufs):
        self.at, self.term, self.bufs = at, term, bufs
        self.m1 = post.msg(term(at.z1), bufs.at[0], at.zn1, bufs.at[0])
        self.m2 = post.msg(term(at.z2), bufs.at[1], at.zn2, bufs.at[1])
        self.m3 = post.msg(term(at.z3), bufs.at[2], at.zn3, bufs.at[2], when=at.mid)
        self.rel = post.msg(term(at.z3), bufs.at[3], at.zn1, bufs.at[3], when=at.end)

    def start(self):
        self.rel.start()
        pl.when(self.at.end)(self.m2.start)
        self.m1.start()
        self.m3.start()

    def relay(self):
        @pl.when(self.at.mid)
        def _():
            self.rel.arrived()
            there = self.term(self.at.z2)
            there[...] = (there[...].astype(F32) + self.bufs[3].astype(F32)).astype(BF16)
            self.m2.start()

    def total(self, out, shape=None):
        self.m1.arrived()
        self.m2.arrived()
        value = self.term(self.at.z)[...].astype(F32) + self.bufs[0].astype(F32) + self.bufs[1].astype(F32)
        out[...] = value

        @pl.when(self.at.mid)
        def _():
            self.m3.arrived()
            out[...] += self.bufs[2].astype(F32)


def head_mask():
    rows = lax.div(lax.broadcasted_iota(jnp.int32, (256, 256), 0), 64)
    lanes = lax.div(lax.broadcasted_iota(jnp.int32, (256, 256), 1), 64)
    return (rows == lanes).astype(F32).astype(BF16)


def spread_heads(part, mask):
    rows = part.reshape(64, 256)
    return jnp.concatenate([rows, rows, rows, rows], axis=0) * mask


def gather_heads(wide):
    lane = lax.div(lax.broadcasted_iota(jnp.int32, (64, 256), 1), 64)
    out = jnp.where(lane == 0, wide[0:64], 0.0)
    for h in range(1, 4):
        out = out + jnp.where(lane == h, wide[64 * h : 64 * h + 64], 0.0)
    return out


def forward(at, post, R):
    images, per_media, _ = R.media.shape
    per_lat = R.latents.shape[1]
    rows = per_media + per_lat
    tokens = images * per_lat

    R.G[at.q, at.c] = R.wpack[...]
    R.UD[at.z, at.c] = R.w_down[...]
    for p in range(4):
        for zz in range(4):
            for cc in range(2):
                R.WS[p, :, 128 * (2 * zz + cc) : 128 * (2 * zz + cc) + 128] = R.w_up[
                    :, 128 * (8 * zz + 2 * p + cc) : 128 * (8 * zz + 2 * p + cc) + 128
                ]
    R.UU[at.q, at.c] = R.WS[at.p]
    R.CA[at.p] = R.cotangent[...].reshape(tokens, 1024)

    at.greet()

    near = pl.ds(0, URGENT)

    def g_view(zz, x, y):
        return R.G.at[zz * 4 + x * 2 + y, at.c, :, near]

    def g_half(zz, x, y, h):
        return R.G.at[zz * 4 + x * 2 + y, at.c, pl.ds(16 * h, 16), near]

    zs = (at.z, at.z1, at.z2, at.z3)
    a_z = ZGather(post, at, lambda zz: g_view(zz, at.x, at.y))
    a_xy = [
        PlaneGather(
            post, at, lambda x, y, zz=zz: g_view(zz, x, y), lambda x, y, h, zz=zz: g_half(zz, x, y, h)
        )
        for zz in zs
    ]
    a_c = [
        post.msg(
            R.G.at[pl.ds(4 * zz, 4), at.c, :, near],
            R.G.at[pl.ds(4 * zz, 4), at.c, :, near],
            at.core,
            R.G.at[pl.ds(4 * zz, 4), 1 - at.c, :, near],
        )
        for zz in zs
    ]
    a_z.start()
    a_xy[0].start()
    up = [
        post.msg(R.WS.at[there], R.UU.at[at.q, at.c], dev, R.UU.at[at.z * 4 + there, at.c])
        for there, dev in ((at.px, at.xn), (at.py, at.yn), (at.pd, at.diag))
    ]
    for m in up:
        m.start()

    def stats(g, carry):
        mean, rstd = normal(R.media[g].astype(F32))
        R.MR[g, 0:per_media, 0:1] = mean
        R.MR[g, 0:per_media, 1:2] = rstd
        mean, rstd = normal(R.latents[g].astype(F32))
        R.MR[g, per_media:rows, 0:1] = mean
        R.MR[g, per_media:rows, 1:2] = rstd
        return carry

    lax.fori_loop(0, images, stats, 0)

    a_z.near()
    a_xy[1].start()
    a_z.far()
    a_xy[2].start()
    a_z.last()
    a_xy[3].start()

    far = pl.ds(URGENT, WIDE - URGENT)

    def b_view(zz, x, y):
        return R.G.at[zz * 4 + x * 2 + y, at.c, :, far]

    def b_half(zz, x, y, h):
        return R.G.at[zz * 4 + x * 2 + y, at.c, pl.ds(16 * h, 16), far]

    b_z = ZGather(post, at, lambda zz: b_view(zz, at.x, at.y))
    b_xy = [
        PlaneGather(
            post, at, lambda x, y, zz=zz: b_view(zz, x, y), lambda x, y, h, zz=zz: b_half(zz, x, y, h)
        )
        for zz in zs
    ]
    b_c = [
        post.msg(
            R.G.at[pl.ds(4 * zz, 4), at.c, :, far],
            R.G.at[pl.ds(4 * zz, 4), at.c, :, far],
            at.core,
            R.G.at[pl.ds(4 * zz, 4), 1 - at.c, :, far],
        )
        for zz in zs
    ]
    d_z = ZGather(post, at, lambda zz: R.UD.at[zz, at.c])
    u_z = ZGather(post, at, lambda zz: R.UU.at[pl.ds(4 * zz, 4), at.c])
    d_c = [post.msg(R.UD.at[zz, at.c], R.UD.at[zz, at.c], at.core, R.UD.at[zz, 1 - at.c]) for zz in zs]
    u_c = [
        post.msg(
            R.UU.at[pl.ds(4 * zz, 4), at.c],
            R.UU.at[pl.ds(4 * zz, 4), at.c],
            at.core,
            R.UU.at[pl.ds(4 * zz, 4), 1 - at.c],
        )
        for zz in zs
    ]
    b_z.start()
    d_z.start()
    d_c[0].start()
    for m in up:
        m.arrived()
    u_z.start()
    u_c[0].start()

    for g in a_xy:
        g.relay()
    for g, m in zip(a_xy, a_c):
        g.last()
        m.start()
    b_xy[0].start()
    b_z.near()
    b_xy[1].start()
    b_z.far()
    b_xy[2].start()
    b_z.last()
    b_xy[3].start()
    cot = PlaneGather(
        post,
        at,
        lambda x, y: R.CA.at[x * 2 + y],
        lambda x, y, h: R.CA.at[x * 2 + y, pl.ds(h * (tokens // 2), tokens // 2)],
    )
    cot.start()
    for m in a_c:
        m.arrived()

    for i in range(8):
        total = jnp.zeros((16, 128), F32)
        for q in (2 * i, 2 * i + 1):
            for c in range(2):
                total = total + R.G[q, c, 0:16, GN[0] : GN[0] + GN[1]].astype(F32)
        R.VV[:, 128 * i : 128 * i + 128] = total

    def low(g, carry):
        normed = (R.media[g].astype(F32) - R.MR[g, 0:per_media, 0:1]) * R.MR[g, 0:per_media, 1:2]
        R.X[g, 0:per_media, :] = (normed * R.VV[0:1, :] + R.VV[1:2, :]).astype(BF16)
        normed = (R.latents[g].astype(F32) - R.MR[g, per_media:rows, 0:1]) * R.MR[g, per_media:rows, 1:2]
        R.X[g, per_media:rows, :] = (normed * R.VV[2:3, :] + R.VV[3:4, :]).astype(BF16)
        return carry

    lax.fori_loop(0, images, low, 0)

    latent_low = flat(R.X[:, per_media:rows, :])
    R.QA[at.l] = mm(latent_low, R.G[:, :, :, QU[0] : QU[0] + QU[1]].reshape(1024, 512)).astype(BF16)
    q_all = LatGather(post, at, lambda l: R.QA.at[l])
    q_all.start()

    def pairs(n, carry):
        weight = R.G[:, :, :, pl.ds(pl.multiple_of(n * 256, 256), 256)].reshape(1024, 256)
        made = mm(R.X[...].reshape(images * rows, 1024), weight).astype(BF16)
        R.PR[:, :, pl.ds(pl.multiple_of(n * 256, 256), 256)] = made.reshape(images, rows, 256)
        return carry

    lax.fori_loop(0, 4, pairs, 0)
    q_all.relay()
    d_z.near()
    d_c[1].start()
    u_z.near()
    u_c[1].start()
    d_z.far()
    u_z.far()
    cot.relay()
    for g in b_xy:
        g.relay()
    q_all.last()

    mask = head_mask()

    def score(g, carry):
        limit = SHORT + (LONG - SHORT) * R.bucket[g] - at.l * per_media
        row = lax.broadcasted_iota(jnp.int32, (rows, 256), 0)
        valid = jnp.logical_or(row >= per_media, row < limit)
        for half in range(2):
            span = pl.ds(256 * half, 256)
            queries = spread_heads(R.QA[:, pl.ds(pl.multiple_of(g * per_lat, per_lat), per_lat), span], mask)
            raw = mm_nt(R.PR[g, :, span], queries) * SCALE
            raw = jnp.where(valid, raw, NEG)
            top = jnp.max(raw, axis=0, keepdims=True)
            total = jnp.sum(jnp.exp(raw - top), axis=0, keepdims=True)
            R.S[2 * g + half] = raw
            R.LS[at.l, pl.ds(2 * g + half, 1), :] = top + jnp.log(total)
        return carry

    lax.fori_loop(0, images, score, 0)
    ls = [
        post.msg(R.LS.at[at.l], R.LS.at[at.l], dev, R.LS.at[there])
        for there, dev in ((at.ly, at.yn), (at.ld, at.ycore), (at.lc, at.core))
    ]
    for m in ls:
        m.start()
    for g, m in zip(b_xy, b_c):
        g.last()
        m.start()
    for m in ls:
        m.arrived()
    top = jnp.maximum(jnp.maximum(R.LS[0], R.LS[1]), jnp.maximum(R.LS[2], R.LS[3]))
    total = jnp.exp(R.LS[0] - top)
    for l in range(1, 4):
        total = total + jnp.exp(R.LS[l] - top)
    R.LG[...] = top + jnp.log(total)

    def mix(g, carry):
        for half in range(2):
            probs = jnp.exp(R.S[2 * g + half] - R.LG[pl.ds(2 * g + half, 1), :])
            R.S[2 * g + half] = probs
            wide = mm_tn(probs.astype(BF16), R.PR[g, :, pl.ds(512 + 256 * half, 256)])
            R.OP[:, pl.ds(pl.multiple_of(g * per_lat, per_lat), per_lat), pl.ds(256 * half, 256)] = (
                gather_heads(wide).reshape(4, per_lat, 256).astype(BF16)
            )
        return carry

    lax.fori_loop(0, images, mix, 0)
    mixed = LatReduce(post, at, R.OP, R.O1, R.O2)
    mixed.start()
    mixed.relay()
    d_z.last()
    u_z.last()
    for m in d_c[2:] + u_c[2:]:
        m.start()
    for m in b_c:
        m.arrived()
    R.MX[...] = mixed.total().astype(BF16)
    left = R.G[:, :, 0:16, OUT[0] : OUT[0] + OUT[1]].reshape(512, 512)
    right = R.G[:, :, 16:32, OUT[0] : OUT[0] + OUT[1]].reshape(512, 512)
    latents = R.latents[...].reshape(tokens, 1024).astype(F32)
    R.RES[:, 0:512] = latents[:, 0:512] + mm(R.MX[...], left)
    R.RES[:, 512:1024] = latents[:, 512:1024] + mm(R.MX[...], right)
    mean, rstd = normal(R.RES[...])
    R.MA[at.p] = ((R.RES[...] - mean) * rstd * R.VV[4:5, :] + R.VV[5:6, :]).astype(BF16)
    mlp = PlaneGather(
        post,
        at,
        lambda x, y: R.MA.at[x * 2 + y],
        lambda x, y, h: R.MA.at[x * 2 + y, pl.ds(h * (tokens // 2), tokens // 2)],
    )
    mlp.start()
    mlp.relay()
    cot.last()
    for m in d_c + u_c:
        m.arrived()
    mlp.last()


def backward(at, post, R):
    images, per_media, _ = R.media.shape
    per_lat = R.latents.shape[1]
    rows = per_media + per_lat
    tokens = images * per_lat
    half_rows = tokens // 2
    zs = (at.z, at.z1, at.z2, at.z3)
    at.greet()

    def gates(f, carry):
        span = pl.ds(pl.multiple_of(f * 256, 256), 256)
        gate = mm(R.MA[...].reshape(4 * tokens, 1024), R.UU[:, :, :, span].reshape(1024, 256))
        back = mm_nt(R.CA[...].reshape(4 * tokens, 1024), R.UD[f].reshape(256, 1024))
        phi = 0.5 * (1.0 + lax.erf(gate * 0.7071067811865476))
        R.ACT[:, :, span] = (gate * phi).astype(BF16).reshape(4, tokens, 256)
        slope = phi + gate * jnp.exp(-0.5 * gate * gate) * 0.3989422804014327
        R.GG[:, :, span] = (back * slope).astype(BF16).reshape(4, tokens, 256)
        return carry

    lax.fori_loop(0, 4, gates, 0)

    def norm_parts(n, carry):
        weight = R.UU[pl.ds(n * 4, 4)].reshape(256, 1024)
        made = mm_nt(R.GG[...].reshape(4 * tokens, 1024), weight)
        R.PT[:, :, pl.ds(pl.multiple_of(n * 256, 256), 256)] = made.astype(BF16).reshape(4, tokens, 256)
        return carry

    lax.fori_loop(0, 4, norm_parts, 0)
    back = PlaneReduce(
        post,
        at,
        lambda x, y, h: R.PT.at[x * 2 + y, pl.ds(h * half_rows, half_rows)],
        R.PY.at[0],
        R.PX.at[0],
        R.P2.at[0],
    )
    back.start()

    back.relay()

    def down_grads(f, carry):
        span = pl.ds(pl.multiple_of(f * 256, 256), 256)
        act = R.ACT[:, :, span].reshape(4 * tokens, 256)
        R.gD[f] = mm_tn(act, R.CA[...].reshape(4 * tokens, 1024)).astype(BF16).reshape(2, 128, 1024)
        return carry

    lax.fori_loop(0, 4, down_grads, 0)
    d_c = post.msg(R.gD.at[:, 1 - at.c], R.RD, at.core, R.RD)
    d_c.start()

    low, high = back.total()
    R.U[0:half_rows] = low
    R.U[half_rows:] = high

    mean, rstd = normal(R.RES[...])
    normed = (R.RES[...] - mean) * rstd
    upstream = R.U[...]
    cot = R.cotangent[...].reshape(tokens, 1024).astype(F32)
    R.GR[...] = cot + norm_back(upstream, normed, rstd, R.VV[4:5, :])
    R.GS[...] = jnp.zeros_like(R.GS)
    R.GS[4:5, :] = jnp.sum(upstream * normed, axis=0, keepdims=True)
    R.GS[5:6, :] = jnp.sum(upstream, axis=0, keepdims=True)
    grad_attn = R.GR[...].astype(BF16)
    left = R.G[:, :, 0:16, OUT[0] : OUT[0] + OUT[1]].reshape(512, 512)
    right = R.G[:, :, 16:32, OUT[0] : OUT[0] + OUT[1]].reshape(512, 512)
    R.GM[at.l] = (mm_nt(grad_attn[:, 0:512], left) + mm_nt(grad_attn[:, 512:1024], right)).astype(BF16)
    gm = LatGather(post, at, lambda l: R.GM.at[l])
    gm.start()
    R.gA[:, :, 0:16, OUT[0] : OUT[0] + OUT[1]] = (
        mm_tn(R.MX[...], grad_attn[:, 0:512]).astype(BF16).reshape(16, 2, 16, 512)
    )
    R.gA[:, :, 16:32, OUT[0] : OUT[0] + OUT[1]] = (
        mm_tn(R.MX[...], grad_attn[:, 512:1024]).astype(BF16).reshape(16, 2, 16, 512)
    )
    gm.relay()

    def up_grads(n, carry):
        span = pl.ds(pl.multiple_of(n * 256, 256), 256)
        low_rows = R.MA[:, :, span].reshape(4 * tokens, 256)
        made = mm_tn(low_rows, R.GG[...].reshape(4 * tokens, 1024)).astype(BF16)
        R.gU[pl.ds(n * 4, 4)] = made.reshape(4, 2, 32, 1024)
        return carry

    lax.fori_loop(0, 4, up_grads, 0)
    u_c = post.msg(R.gU.at[:, 1 - at.c], R.RU, at.core, R.RU)
    u_c.start()

    def out_parts(n, carry):
        span = pl.ds(pl.multiple_of(n * 256, 256), 256)
        made = mm(R.ACT[...].reshape(4 * tokens, 1024), R.UD[:, :, :, span].reshape(1024, 256))
        R.GG[:, :, span] = made.astype(BF16).reshape(4, tokens, 256)
        return carry

    lax.fori_loop(0, 4, out_parts, 0)
    d_c.arrived()

    def add_d(zz, carry):
        R.RD[zz] = (R.RD[zz].astype(F32) + R.gD[zz, at.c].astype(F32)).astype(BF16)
        return carry

    lax.fori_loop(0, 4, add_d, 0)
    d_z = ZReduce(post, at, lambda zz: R.RD.at[zz], R.ZD)
    d_z.start()
    out = PlaneReduce(
        post,
        at,
        lambda x, y, h: R.GG.at[x * 2 + y, pl.ds(h * half_rows, half_rows)],
        R.PY.at[1],
        R.PX.at[1],
        R.P2.at[1],
    )
    out.start()
    gm.last()

    mask = head_mask()

    def grad_probs(g, carry):
        lat_rows = pl.ds(pl.multiple_of(g * per_lat, per_lat), per_lat)
        for half in range(2):
            upper = pl.ds(512 + 256 * half, 256)
            wide = spread_heads(R.GM[:, lat_rows, pl.ds(256 * half, 256)], mask)
            made = mm_nt(R.PR[g, :, upper], wide)
            probs = R.S[2 * g + half]
            R.GP[2 * g + half] = made
            R.DL[at.l, pl.ds(2 * g + half, 1), :] = jnp.sum(probs * made, axis=0, keepdims=True)
            R.gP[g, :, upper] = mm(probs.astype(BF16), wide).astype(BF16)
        return carry

    lax.fori_loop(0, images, grad_probs, 0)
    dl = [
        post.msg(R.DL.at[at.l], R.DL.at[at.l], dev, R.DL.at[there])
        for there, dev in ((at.ly, at.yn), (at.ld, at.ycore), (at.lc, at.core))
    ]
    for m in dl:
        m.start()
    u_c.arrived()

    def add_u(zz, carry):
        span = pl.ds(zz * 4, 4)
        R.RU[span] = (R.RU[span].astype(F32) + R.gU[span, at.c].astype(F32)).astype(BF16)
        return carry

    lax.fori_loop(0, 4, add_u, 0)
    u_z = ZReduce(post, at, lambda zz: R.RU.at[pl.ds(zz * 4, 4)], R.ZU)
    u_z.start()
    out.relay()
    for m in dl:
        m.arrived()
    R.LG2[...] = R.DL[0] + R.DL[1] + R.DL[2] + R.DL[3]

    def grad_scores(g, carry):
        lat_rows = pl.ds(pl.multiple_of(g * per_lat, per_lat), per_lat)
        for half in range(2):
            span = pl.ds(256 * half, 256)
            grads = R.S[2 * g + half] * (R.GP[2 * g + half] - R.LG2[pl.ds(2 * g + half, 1), :])
            grads = grads.astype(BF16)
            wide = mm_tn(grads, R.PR[g, :, span]) * SCALE
            R.QP[:, lat_rows, span] = gather_heads(wide).reshape(4, per_lat, 256).astype(BF16)
            queries = spread_heads(R.QA[:, lat_rows, span], mask)
            R.gP[g, :, span] = (mm(grads, queries) * SCALE).astype(BF16)
        return carry

    lax.fori_loop(0, images, grad_scores, 0)
    gq = LatReduce(post, at, R.QP, R.Q1, R.Q2)
    gq.start()
    d_z.relay()
    u_z.relay()

    def kv_grads(n, carry):
        low_rows = R.X[:, :, pl.ds(pl.multiple_of(n * 256, 256), 256)].reshape(images * rows, 256)
        made = mm_tn(low_rows, R.gP[...].reshape(images * rows, 1024)).astype(BF16)
        R.gA[pl.ds(n * 4, 4), :, :, 0:1024] = made.reshape(4, 2, 32, 1024)
        return carry

    lax.fori_loop(0, 4, kv_grads, 0)
    gq.relay()

    def media_copy(h):
        return pltpu.make_async_copy(R.MG, R.grad_media.at[pl.ds(h * 2, 2)], R.local.at[0])

    def media_grads(h, carry):
        span = pl.ds(h * 2, 2)
        weight = R.G[:, :, :, 0:1024].reshape(1024, 1024)
        upstream = mm_nt(R.gP[span].reshape(2 * rows, 1024), weight).reshape(2, rows, 1024)
        R.U[pl.ds(h * 2 * per_lat, 2 * per_lat)] = upstream[:, per_media:rows, :].reshape(2 * per_lat, 1024)
        upstream = upstream[:, 0:per_media, :]
        rstd = R.MR[span, 0:per_media, 1:2]
        normed = (R.media[span].astype(F32) - R.MR[span, 0:per_media, 0:1]) * rstd
        made = norm_back(upstream, normed, rstd, R.VV[0:1, :])
        pl.when(h >= 1)(lambda: media_copy(h - 1).wait())
        R.MG[...] = made
        media_copy(h).start()
        R.GS[0:1, :] += jnp.sum(flat(upstream * normed), axis=0, keepdims=True)
        R.GS[1:2, :] += jnp.sum(flat(upstream), axis=0, keepdims=True)
        return carry

    lax.fori_loop(0, images // 2, media_grads, 0)
    media_copy(images // 2 - 1).wait()

    grad_query = gq.total().astype(BF16)
    latent_low = flat(R.X[:, per_media:rows, :])
    weight = R.G[:, :, :, QU[0] : QU[0] + QU[1]].reshape(1024, 512)
    upstream = R.U[...] + mm_nt(grad_query, weight)
    rstd = flat(R.MR[:, per_media:rows, 1:2])
    normed = (flat(R.latents[...]).astype(F32) - flat(R.MR[:, per_media:rows, 0:1])) * rstd
    R.grad_latents[...] = (R.GR[...] + norm_back(upstream, normed, rstd, R.VV[2:3, :])).reshape(
        images, per_lat, 1024
    )
    R.GS[2:3, :] = jnp.sum(upstream * normed, axis=0, keepdims=True)
    R.GS[3:4, :] = jnp.sum(upstream, axis=0, keepdims=True)
    R.gA[:, :, :, QU[0] : QU[0] + QU[1]] = (
        mm_tn(latent_low, grad_query).astype(BF16).reshape(16, 2, 32, 512)
    )
    for i in range(8):
        piece = R.GS[:, 128 * i : 128 * i + 128].astype(BF16)
        for q in (2 * i, 2 * i + 1):
            for c in range(2):
                R.gA[q, c, 0:16, GN[0] : GN[0] + GN[1]] = piece
                R.gA[q, c, 16:32, GN[0] : GN[0] + GN[1]] = jnp.zeros((16, 128), BF16)

    w_c = [
        post.msg(R.gA.at[pl.ds(4 * zz, 4), 1 - at.c], R.RA.at[pl.ds(4 * zz, 4)], at.core, R.RA.at[pl.ds(4 * zz, 4)])
        for zz in zs
    ]
    for m in w_c[::-1]:
        m.start()
    w_xy = []
    for k in (3, 2, 1, 0):
        span = pl.ds(4 * zs[k], 4)
        w_c[k].arrived()
        R.RA[span] = (R.RA[span].astype(F32) + R.gA[span, at.c].astype(F32)).astype(BF16)
        w_xy.append(
            PlaneReduce(
                post,
                at,
                lambda x, y, h, zz=zs[k]: R.RA.at[zz * 4 + x * 2 + y, pl.ds(16 * h, 16)],
                R.WY.at[k],
                R.WX.at[k],
                R.W2.at[k],
            )
        )
        w_xy[-1].start()
    low, high = out.total()
    R.latents_out[...] = jnp.concatenate([R.RES[0:half_rows] + low, R.RES[half_rows:] + high], axis=0).astype(
        BF16
    ).reshape(images, per_lat, 1024)
    d_z.total(R.grad_down)
    u_z.total(R.SF)
    R.SU[...] = R.SF[...].astype(BF16)
    R.AU[at.p] = R.SU[at.p]
    up = [
        post.msg(R.SU.at[there], R.AU.at[at.p], dev, R.AU.at[there])
        for there, dev in ((at.px, at.xn), (at.py, at.yn), (at.pd, at.diag))
    ]
    for g in w_xy:
        g.relay()
    for m in up:
        m.start()
    for k, g in zip((3, 2, 1, 0), w_xy):
        low, high = g.total()
        R.RA[zs[k] * 4 + at.p, 0:16, :] = low.astype(BF16)
        R.RA[zs[k] * 4 + at.p, 16:32, :] = high.astype(BF16)
    w_z = ZReduce(post, at, lambda zz: R.RA.at[zz * 4 + at.p], R.ZW)
    w_z.start()
    w_z.relay()
    for m in up:
        m.arrived()
    for p in range(4):
        for zz in range(4):
            for cc in range(2):
                R.grad_up[:, 128 * (8 * zz + 2 * p + cc) : 128 * (8 * zz + 2 * p + cc) + 128] = R.AU[
                    p, :, 128 * (2 * zz + cc) : 128 * (2 * zz + cc) + 128
                ].astype(F32)
    w_z.total(R.grad_pack)


class Refs:
    def __init__(self, names, refs):
        for name, ref in zip(names, refs):
            setattr(self, name, ref)


def build(kernel_body, inputs, outputs, scratch, messages, cid, name):
    in_names = [n for n, _ in inputs]
    out_names = [n for n, _, _ in outputs]
    scratch_names = [n for n, _, _ in scratch]

    def kernel(*refs):
        R = Refs(in_names + out_names + scratch_names, refs)
        at = Place()
        R.local = refs[-3]
        post = Post(refs[-2], refs[-1])
        kernel_body(at, post, R)
        post.drain()
        assert post.count == messages, post.count

    specs = [
        pl.BlockSpec(memory_space=pltpu.SMEM if n == "bucket" else pltpu.VMEM) for n in in_names
    ]
    return pl.pallas_call(
        kernel,
        out_shape=[jax.ShapeDtypeStruct(s, d) for _, s, d in outputs],
        in_specs=specs,
        out_specs=[
            pl.BlockSpec(memory_space=pl.ANY if n == "grad_media" else pltpu.VMEM) for n, _, _ in outputs
        ],
        scratch_shapes=[pltpu.VMEM(s, d) for _, s, d in scratch]
        + [pltpu.SemaphoreType.DMA((2,)), pltpu.SemaphoreType.DMA((messages,)), pltpu.SemaphoreType.DMA((messages,))],
        compiler_params=pltpu.CompilerParams(
            collective_id=cid, has_side_effects=True, vmem_limit_bytes=62 << 20
        ),
        name=name,
    )(*[v for _, v in inputs])


def layer(media, latents, bucket, cotangent, wpack, w_up, w_down):
    images, per_media, _ = media.shape
    per_lat = latents.shape[1]
    rows = per_media + per_lat
    tokens = images * per_lat
    inputs = [
        ("media", media),
        ("latents", latents),
        ("cotangent", cotangent),
        ("bucket", bucket),
        ("wpack", wpack),
        ("w_up", w_up),
        ("w_down", w_down),
    ]
    kept = [
        ("X", (images, rows, 1024), BF16),
        ("MR", (images, rows, 2), F32),
        ("PR", (images, rows, 1024), BF16),
        ("S", (2 * images, rows, 256), F32),
        ("QA", (4, tokens, 512), BF16),
        ("MX", (tokens, 512), BF16),
        ("RES", (tokens, 1024), F32),
        ("MA", (4, tokens, 1024), BF16),
        ("CA", (4, tokens, 1024), BF16),
        ("UD", (4, 2, 128, 1024), BF16),
        ("UU", (16, 2, 32, 1024), BF16),
        ("G", (16, 2, 32, WIDE), BF16),
        ("VV", (16, 1024), F32),
    ]
    scratch_a = [
        ("WS", (4, 32, 1024), BF16),
        ("LS", (4, 2 * images, 256), F32),
        ("LG", (2 * images, 256), F32),
        ("OP", (4, tokens, 512), BF16),
        ("O1", (2, tokens, 512), BF16),
        ("O2", (tokens, 512), BF16),
    ]
    outputs = [
        ("latents_out", (images, per_lat, 1024), BF16),
        ("grad_media", (images, per_media, 1024), F32),
        ("grad_latents", (images, per_lat, 1024), F32),
        ("grad_pack", (32, WIDE), F32),
        ("grad_up", (32, 4096), F32),
        ("grad_down", (128, 1024), F32),
    ]
    scratch_b = [
        ("MG", (2, per_media, 1024), F32),
        ("ACT", (4, tokens, 1024), BF16),
        ("GG", (4, tokens, 1024), BF16),
        ("PT", (4, tokens, 1024), BF16),
        ("PY", (2, 2, tokens // 2, 1024), BF16),
        ("PX", (2, 2, tokens // 2, 1024), BF16),
        ("P2", (2, 2, tokens // 2, 1024), BF16),
        ("gD", (4, 2, 128, 1024), BF16),
        ("gU", (16, 2, 32, 1024), BF16),
        ("RD", (4, 128, 1024), BF16),
        ("RU", (16, 32, 1024), BF16),
        ("ZD", (4, 128, 1024), BF16),
        ("ZU", (4, 4, 32, 1024), BF16),
        ("U", (tokens, 1024), F32),
        ("GR", (tokens, 1024), F32),
        ("GS", (16, 1024), F32),
        ("GM", (4, tokens, 512), BF16),
        ("GP", (2 * images, rows, 256), F32),
        ("gP", (images, rows, 1024), BF16),
        ("DL", (4, 2 * images, 256), F32),
        ("LG2", (2 * images, 256), F32),
        ("QP", (4, tokens, 512), BF16),
        ("Q1", (2, tokens, 512), BF16),
        ("Q2", (tokens, 512), BF16),
        ("gA", (16, 2, 32, WIDE), BF16),
        ("RA", (16, 32, WIDE), BF16),
        ("WY", (4, 2, 16, WIDE), BF16),
        ("WX", (4, 2, 16, WIDE), BF16),
        ("W2", (4, 2, 16, WIDE), BF16),
        ("ZW", (4, 32, WIDE), BF16),
        ("SF", (4, 32, 1024), F32),
        ("SU", (4, 32, 1024), BF16),
        ("AU", (4, 32, 1024), BF16),
    ]
    made = build(forward, inputs, kept, scratch_a, 84, 1, "resampler_forward")
    carried = [(n, v) for (n, _, _), v in zip(kept, made)]
    return build(backward, inputs[:3] + carried, outputs, scratch_b, 66, 2, "resampler_backward")


def solution(mesh):
    sizes = dict(mesh.shape)
    blocks = sizes["img"] // BLOCK
    names = ("img", "lat")

    def block_shard(weight):
        if blocks == 1:
            return weight
        whole = lax.all_gather(weight, names, axis=0, tiled=True)
        each = whole.shape[0] // (BLOCK * sizes["lat"])
        mine = lax.rem(lax.axis_index("img"), BLOCK) * sizes["lat"] + lax.axis_index("lat")
        return lax.dynamic_slice_in_dim(whole, mine * each, each, 0)

    def own_shard(gradient):
        if blocks == 1:
            return gradient
        each = gradient.shape[0]
        mine = lax.rem(lax.axis_index("img"), BLOCK) * sizes["lat"] + lax.axis_index("lat")
        whole = jnp.zeros((each * BLOCK * sizes["lat"],) + gradient.shape[1:], gradient.dtype)
        whole = lax.dynamic_update_slice_in_dim(whole, gradient, mine * each, 0)
        return lax.psum_scatter(whole, names, scatter_dimension=0, tiled=True)

    def on_device(
        media,
        latents,
        bucket,
        gain_media,
        shift_media,
        gain_latent,
        shift_latent,
        gain_mlp,
        shift_mlp,
        w_query,
        w_keyvalue,
        w_output,
        w_up,
        w_down,
        cotangent,
    ):
        lat = lax.axis_index("lat")
        norms = [
            block_shard(v) for v in (gain_media, shift_media, gain_latent, shift_latent, gain_mlp, shift_mlp)
        ]
        norms = jnp.pad(jnp.tile(jnp.stack(norms), (1, 4)), ((0, 26), (0, 0)))
        lanes = jnp.arange(128, dtype=jnp.int32) // 32
        norms = jnp.where(lanes[None, :] == lat, norms, jnp.zeros_like(norms))
        out_rows = block_shard(w_output)
        out_rows = jnp.concatenate([out_rows[:, 0:512], out_rows[:, 512:1024]], axis=0)
        wpack = jnp.concatenate([block_shard(w_keyvalue), block_shard(w_query), norms, out_rows], axis=1)
        latents_out, grad_media, grad_latents, grad_pack, grad_up, grad_down = layer(
            media, latents, bucket, cotangent, wpack, block_shard(w_up), block_shard(w_down)
        )
        norm_grads = lax.dynamic_slice_in_dim(grad_pack[0:6, GN[0] : GN[0] + GN[1]], lat * 32, 32, 1)
        grad_out = jnp.concatenate(
            [grad_pack[0:16, OUT[0] : OUT[0] + OUT[1]], grad_pack[16:32, OUT[0] : OUT[0] + OUT[1]]], axis=1
        )
        return (
            latents_out,
            grad_media,
            grad_latents,
            *[own_shard(norm_grads[k]) for k in range(6)],
            own_shard(grad_pack[:, QU[0] : QU[0] + QU[1]]),
            own_shard(grad_pack[:, KV[0] : KV[0] + KV[1]]),
            own_shard(grad_out),
            own_shard(grad_up),
            own_shard(grad_down),
        )

    rows = P("img", "lat", None)
    shard = P(names)
    wide = P(names, None)
    return jax.shard_map(
        on_device,
        mesh=mesh,
        in_specs=(rows, rows, P("img")) + (shard,) * 6 + (wide,) * 5 + (rows,),
        out_specs=(rows, rows, rows) + (shard,) * 6 + (wide,) * 5,
        check_vma=False,
    )
```

```python
import jax
import jax.numpy as jnp
from jax import lax
from jax.experimental import pallas as pl
from jax.experimental.pallas import tpu as pltpu
from jax.sharding import PartitionSpec as P

MESH = pl.DeviceIdType.MESH
BF16 = jnp.bfloat16
F32 = jnp.float32

SHORT = 256
LONG = 576
HEADS = 8
EPS = 1e-05
SCALE = 0.125
NEG = -1e30

BLOCK = 8

QU = (0, 512)
GN = (512, 128)
KEY = (640, 512)
VAL = (1152, 512)
KV = (640, 1024)
OUT = (1664, 512)
WIDE = 2176
GQG = (0, 640)
GOUT = (640, 512)
NARROW = 1152
MESSAGES = 183


def mm(a, b):
    return lax.dot_general(a, b, (((1,), (0,)), ((), ())), preferred_element_type=F32)


def mm_nt(a, b):
    return lax.dot_general(a, b, (((1,), (1,)), ((), ())), preferred_element_type=F32)


def mm_tn(a, b):
    return lax.dot_general(a, b, (((0,), (0,)), ((), ())), preferred_element_type=F32)


def cols(span):
    return pl.ds(span[0], span[1])


def flat(values):
    return values.reshape(-1, values.shape[-1])


def normal(values):
    mean = jnp.mean(values, axis=-1, keepdims=True)
    centred = values - mean
    spread = jnp.mean(centred * centred, axis=-1, keepdims=True)
    return mean, lax.rsqrt(spread + EPS)


def norm_back(upstream, normed, rstd, gain):
    scaled = upstream * gain
    first = jnp.mean(scaled, axis=-1, keepdims=True)
    second = jnp.mean(scaled * normed, axis=-1, keepdims=True)
    return (scaled - first - normed * second) * rstd


class Place:
    def __init__(self):
        img = lax.axis_index("img")
        lat = lax.axis_index("lat")
        self.i = lax.rem(img, BLOCK)
        self.base = img - self.i
        self.z = lax.div(self.i, 2)
        self.x = lax.rem(self.i, 2)
        self.l = lat
        self.y = lax.div(lat, 2)
        self.c = lax.rem(lat, 2)
        self.z1 = self.z + 1 - 2 * lax.rem(self.z, 2)
        self.z2 = lax.rem(self.z + 2, 4)
        self.z3 = 3 - self.z
        self.mid = jnp.logical_or(self.z == 1, self.z == 2)
        self.zs = (self.z, self.z1, self.z2, self.z3)
        self.end = jnp.logical_or(self.z == 0, self.z == 3)
        self.p = self.x * 2 + self.y
        self.q = self.z * 4 + self.p
        self.px = (1 - self.x) * 2 + self.y
        self.py = self.x * 2 + 1 - self.y
        self.pd = 3 - self.p
        self.lc = self.y * 2 + 1 - self.c
        self.ly = (1 - self.y) * 2 + self.c
        self.ld = 3 - self.l
        self.core = self.dev(self.z, self.x, self.y, 1 - self.c)
        self.xn = self.dev(self.z, 1 - self.x, self.y, self.c)
        self.yn = self.dev(self.z, self.x, 1 - self.y, self.c)
        self.diag = self.dev(self.z, 1 - self.x, 1 - self.y, self.c)
        self.ycore = self.dev(self.z, self.x, 1 - self.y, 1 - self.c)
        self.zn1 = self.dev(self.z1, self.x, self.y, self.c)
        self.zn2 = self.dev(self.z2, self.x, self.y, self.c)
        self.zn3 = self.dev(self.z3, self.x, self.y, self.c)

    def dev(self, z, x, y, c):
        return (self.base + z * 2 + x, y * 2 + c)

    def greet(self):
        barrier = pltpu.get_barrier_semaphore()
        peers = (self.core, self.xn, self.yn, self.diag, self.ycore, self.zn1, self.zn2, self.zn3)
        for peer in peers:
            pl.semaphore_signal(barrier, inc=1, device_id=peer, device_id_type=MESH)
        pl.semaphore_wait(barrier, len(peers))


def guarded(when, action):
    if when is None:
        action()
    else:
        pl.when(when)(action)


class Msg:
    def __init__(self, post, src, dst, dev, into, key=None, when=None):
        self.k = post.count
        post.count += 1
        self.key = self.k if key is None else key
        self.when = when
        self.post, self.src, self.dst, self.dev, self.into = post, src, dst, dev, into
        self.done = False
        post.all.append(self)

    def copy(self, src, dst):
        return pltpu.make_async_remote_copy(
            src_ref=src,
            dst_ref=dst,
            send_sem=self.post.send.at[self.k],
            recv_sem=self.post.recv.at[self.key],
            device_id=self.dev,
            device_id_type=MESH,
        )

    def start(self):
        guarded(self.when, lambda: self.copy(self.src, self.dst).start())

    def arrived(self):
        self.copy(self.into, self.into).wait_recv()

    def sent(self):
        if self.done:
            return
        self.done = True
        guarded(self.when, lambda: self.copy(self.src, self.dst).wait_send())


class Post:
    def __init__(self, send, recv):
        self.send = send
        self.recv = recv
        self.count = 0
        self.all = []

    def msg(self, *a, **k):
        return Msg(self, *a, **k)

    def drain(self):
        for m in self.all:
            m.sent()


class ZGather:
    def __init__(self, post, at, view):
        own = view(at.z)
        self.m1 = post.msg(own, own, at.zn1, view(at.z1))
        self.m2 = post.msg(own, own, at.zn2, view(at.z2))
        self.m3 = post.msg(own, own, at.zn3, view(at.z3), when=at.mid)
        self.relay = post.msg(view(at.z2), view(at.z2), at.zn1, view(at.z3), key=self.m3.k, when=at.mid)

    def start(self):
        self.m1.start()
        self.m2.start()
        self.m3.start()

    def near(self):
        self.m1.arrived()

    def far(self):
        self.m2.arrived()
        self.relay.start()

    def last(self):
        self.m3.arrived()


class PlaneGather:
    def __init__(self, post, at, view, half):
        own = view(at.x, at.y)
        ox, oy = 1 - at.x, 1 - at.y
        self.mx = post.msg(own, own, at.xn, view(ox, at.y))
        self.my = post.msg(own, own, at.yn, view(at.x, oy))
        self.hy = post.msg(half(ox, at.y, 0), half(ox, at.y, 0), at.yn, half(ox, oy, 0))
        self.hx = post.msg(half(at.x, oy, 1), half(at.x, oy, 1), at.xn, half(ox, oy, 1))

    def start(self):
        self.mx.start()
        self.my.start()

    def relay(self):
        self.mx.arrived()
        self.hy.start()
        self.my.arrived()
        self.hx.start()

    def last(self):
        self.hy.arrived()
        self.hx.arrived()


class Spread:
    def __init__(self, post, at, G, span):
        lanes = cols(span)

        def view(zz, x, y):
            return G.at[zz, x * 2 + y, at.c, :, lanes]

        def half(zz, x, y, h):
            return G.at[zz, x * 2 + y, at.c, pl.ds(16 * h, 16), lanes]

        own = view(at.z, at.x, at.y)
        self.z = [
            post.msg(own, own, dev, view(zz, at.x, at.y))
            for zz, dev in ((at.z1, at.zn1), (at.z2, at.zn2), (at.z3, at.zn3))
        ]
        self.plane = [
            PlaneGather(
                post, at, lambda x, y, zz=zz: view(zz, x, y), lambda x, y, h, zz=zz: half(zz, x, y, h)
            )
            for zz in at.zs
        ]
        self.core = [
            post.msg(
                G.at[zz, :, at.c, :, lanes], G.at[zz, :, at.c, :, lanes], at.core, G.at[zz, :, 1 - at.c, :, lanes]
            )
            for zz in at.zs
        ]

    def start(self):
        for m in self.z:
            m.start()

    def into_plane(self):
        for k in range(3):
            self.z[k].arrived()
            self.plane[k + 1].start()

    def relay(self):
        for g in self.plane:
            g.relay()

    def to_core(self):
        for g, m in zip(self.plane, self.core):
            g.last()
            m.start()

    def arrived(self):
        for m in self.core:
            m.arrived()


class LatGather:
    def __init__(self, post, at, view):
        self.mc = post.msg(view(at.l), view(at.l), at.core, view(at.lc))
        self.my = post.msg(view(at.l), view(at.l), at.yn, view(at.ly))
        self.fc = post.msg(view(at.ly), view(at.ly), at.core, view(at.ld))

    def start(self):
        self.my.start()
        self.mc.start()

    def relay(self):
        self.my.arrived()
        self.fc.start()

    def last(self):
        self.mc.arrived()
        self.fc.arrived()


class LatReduce:
    def __init__(self, post, at, parts, first, second):
        self.at, self.parts, self.first, self.second = at, parts, first, second
        self.m0 = post.msg(parts.at[at.lc], first.at[0], at.core, first.at[0])
        self.m1 = post.msg(parts.at[at.ld], first.at[1], at.core, first.at[1])
        self.m2 = post.msg(parts.at[at.ly], second, at.yn, second)

    def start(self):
        self.m1.start()
        self.m0.start()

    def relay(self):
        self.m1.arrived()
        ly = self.at.ly
        self.parts[ly] = (self.parts[ly].astype(F32) + self.first[1].astype(F32)).astype(BF16)
        self.m2.start()

    def total(self):
        self.m0.arrived()
        self.m2.arrived()
        near = self.parts[self.at.l].astype(F32) + self.first[0].astype(F32)
        return near + self.second[...].astype(F32)


class PlaneReduce:
    def __init__(self, post, at, part, by, bx, b2):
        x, y = at.x, at.y
        ox, oy = 1 - x, 1 - y
        self.part, self.by, self.bx, self.b2 = part, by, bx, b2
        self.x, self.y, self.ox, self.oy = x, y, ox, oy
        self.my1 = post.msg(part(ox, oy, 0), by(1), at.yn, by(1))
        self.mx1 = post.msg(part(ox, oy, 1), bx(1), at.xn, bx(1))
        self.my0 = post.msg(part(x, oy, 0), by(0), at.yn, by(0))
        self.mx0 = post.msg(part(ox, y, 1), bx(0), at.xn, bx(0))
        self.f0 = post.msg(part(ox, y, 0), b2(0), at.xn, b2(0))
        self.f1 = post.msg(part(x, oy, 1), b2(1), at.yn, b2(1))

    def start(self):
        self.my1.start()
        self.mx1.start()

    def relay(self):
        self.my1.arrived()
        there = self.part(self.ox, self.y, 0)
        there[...] = (there[...].astype(F32) + self.by(1)[...].astype(F32)).astype(BF16)
        self.f0.start()
        self.mx1.arrived()
        there = self.part(self.x, self.oy, 1)
        there[...] = (there[...].astype(F32) + self.bx(1)[...].astype(F32)).astype(BF16)
        self.f1.start()
        self.my0.start()
        self.mx0.start()

    def total(self):
        self.my0.arrived()
        self.f0.arrived()
        low = self.part(self.x, self.y, 0)[...].astype(F32) + self.by(0)[...].astype(F32)
        low = low + self.b2(0)[...].astype(F32)
        self.mx0.arrived()
        self.f1.arrived()
        high = self.part(self.x, self.y, 1)[...].astype(F32) + self.bx(0)[...].astype(F32)
        return low, high + self.b2(1)[...].astype(F32)


class ZReduce:
    def __init__(self, post, at, term, buf):
        self.at, self.term, self.buf = at, term, buf
        self.m1 = post.msg(term(at.z1), buf(0), at.zn1, buf(0))
        self.m2 = post.msg(term(at.z2), buf(1), at.zn2, buf(1))
        self.m3 = post.msg(term(at.z3), buf(2), at.zn3, buf(2), when=at.mid)
        self.rel = post.msg(term(at.z3), buf(3), at.zn1, buf(3), when=at.end)

    def start(self):
        self.rel.start()
        pl.when(self.at.end)(self.m2.start)
        self.m1.start()
        self.m3.start()

    def relay(self):
        @pl.when(self.at.mid)
        def _():
            self.rel.arrived()
            there = self.term(self.at.z2)
            there[...] = (there[...].astype(F32) + self.buf(3)[...].astype(F32)).astype(BF16)
            self.m2.start()

    def total(self, out):
        self.m1.arrived()
        self.m2.arrived()
        value = self.term(self.at.z)[...].astype(F32) + self.buf(0)[...].astype(F32)
        out[...] = value + self.buf(1)[...].astype(F32)

        @pl.when(self.at.mid)
        def _():
            self.m3.arrived()
            out[...] += self.buf(2)[...].astype(F32)


class Collect:
    def __init__(self, post, at, grads, near, by, bx, b2, bz, src, dst):
        self.at, self.grads, self.near, self.src = at, grads, near, src
        self.lanes, self.there = cols(src), cols(dst)
        self.core = post.msg(
            grads.at[:, :, 1 - at.c, :, self.lanes], near.at[:, :, :, self.lanes], at.core,
            near.at[:, :, :, self.lanes],
        )
        self.plane = PlaneReduce(
            post,
            at,
            lambda x, y, h: near.at[:, x * 2 + y, pl.ds(16 * h, 16), self.lanes],
            lambda k: by.at[k, :, :, self.there],
            lambda k: bx.at[k, :, :, self.there],
            lambda k: b2.at[k, :, :, self.there],
        )
        self.z = ZReduce(
            post, at, lambda zz: near.at[zz, at.p, :, self.lanes], lambda k: bz.at[k, :, self.there]
        )

    def start(self):
        self.core.start()

    def into_plane(self):
        self.core.arrived()

        def add(zz, carry):
            mine = self.grads[zz, :, self.at.c, :, self.lanes].astype(F32)
            self.near[zz, :, :, self.lanes] = (self.near[zz, :, :, self.lanes].astype(F32) + mine).astype(BF16)
            return carry

        lax.fori_loop(0, 4, add, 0)
        self.plane.start()

    def relay(self):
        self.plane.relay()

    def into_z(self):
        low, high = self.plane.total()
        self.near[:, self.at.p, 0:16, self.lanes] = low.astype(BF16)
        self.near[:, self.at.p, 16:32, self.lanes] = high.astype(BF16)
        self.z.start()

    def z_relay(self):
        self.z.relay()

    def total(self, out):
        self.z.total(out)


def head_mask():
    rows = lax.div(lax.broadcasted_iota(jnp.int32, (256, 256), 0), 64)
    lanes = lax.div(lax.broadcasted_iota(jnp.int32, (256, 256), 1), 64)
    return (rows == lanes).astype(F32).astype(BF16)


def spread_heads(part, mask):
    rows = part.reshape(64, 256)
    return jnp.concatenate([rows, rows, rows, rows], axis=0) * mask


def gather_heads(wide):
    lane = lax.div(lax.broadcasted_iota(jnp.int32, (64, 256), 1), 64)
    out = jnp.where(lane == 0, wide[0:64], 0.0)
    for h in range(1, 4):
        out = out + jnp.where(lane == h, wide[64 * h : 64 * h + 64], 0.0)
    return out


def span256(n):
    return pl.ds(pl.multiple_of(n * 256, 256), 256)


def kernel_body(at, post, R):
    images, per_media, _ = R.MED.shape
    per_lat = R.latents.shape[1]
    rows = per_media + per_lat
    tokens = images * per_lat
    half_rows = tokens // 2
    zs = at.zs

    media_in = pltpu.make_async_copy(R.media, R.MED, R.local.at[0])
    media_in.start()
    R.G[at.z, at.p, at.c, :, cols(QU)] = R.w_query[...]
    R.G[at.z, at.p, at.c, :, cols(KV)] = R.w_keyvalue[...]
    R.G[at.z, at.p, at.c, 0:16, cols(OUT)] = R.w_output[:, 0:512]
    R.G[at.z, at.p, at.c, 16:32, cols(OUT)] = R.w_output[:, 512:1024]
    norms = R.norms[...].astype(F32)
    norms = jnp.concatenate([norms, norms, norms, norms], axis=1)
    lanes = lax.div(lax.broadcasted_iota(jnp.int32, (16, 128), 1), 32)
    R.G[at.z, at.p, at.c, 0:16, cols(GN)] = jnp.where(lanes == at.l, norms, 0.0).astype(BF16)
    R.G[at.z, at.p, at.c, 16:32, cols(GN)] = jnp.zeros((16, 128), BF16)
    R.UD[at.z, at.c] = R.w_down[...]
    for p in range(4):
        for zz in range(4):
            for cc in range(2):
                R.WS[p, :, 128 * (2 * zz + cc) : 128 * (2 * zz + cc) + 128] = R.w_up[
                    :, 128 * (8 * zz + 2 * p + cc) : 128 * (8 * zz + 2 * p + cc) + 128
                ]
    R.UU[at.z, at.p, at.c] = R.WS[at.p]
    R.CA[at.p] = R.cotangent[...].reshape(tokens, 1024)

    with jax.named_scope("greet"):
        at.greet()

    first = Spread(post, at, R.G, (0, 1152))
    second = Spread(post, at, R.G, VAL)
    third = Spread(post, at, R.G, OUT)
    up = [
        post.msg(R.WS.at[there], R.UU.at[at.z, at.p, at.c], dev, R.UU.at[at.z, there, at.c])
        for there, dev in ((at.px, at.xn), (at.py, at.yn), (at.pd, at.diag))
    ]
    d_z = ZGather(post, at, lambda zz: R.UD.at[zz, at.c])
    u_z = ZGather(post, at, lambda zz: R.UU.at[zz, :, at.c])
    d_c = [post.msg(R.UD.at[zz, at.c], R.UD.at[zz, at.c], at.core, R.UD.at[zz, 1 - at.c]) for zz in zs]
    u_c = [
        post.msg(R.UU.at[zz, :, at.c], R.UU.at[zz, :, at.c], at.core, R.UU.at[zz, :, 1 - at.c]) for zz in zs
    ]
    cot = PlaneGather(
        post,
        at,
        lambda x, y: R.CA.at[x * 2 + y],
        lambda x, y, h: R.CA.at[x * 2 + y, pl.ds(h * half_rows, half_rows)],
    )

    first.start()
    first.plane[0].start()
    for m in up:
        m.start()

    def stats(g, carry):
        mean, rstd = normal(R.MED[g].astype(F32))
        R.MR[g, 0:per_media, 0:1] = mean
        R.MR[g, 0:per_media, 1:2] = rstd
        mean, rstd = normal(R.latents[g].astype(F32))
        R.MR[g, per_media:rows, 0:1] = mean
        R.MR[g, per_media:rows, 1:2] = rstd
        return carry

    media_in.wait()
    loop(images, stats)
    first.into_plane()
    second.start()
    d_z.start()
    d_c[0].start()
    first.relay()
    for m in up:
        m.arrived()
    u_z.start()
    u_c[0].start()
    first.to_core()
    second.plane[0].start()
    second.into_plane()
    third.start()
    first.arrived()

    for i in range(8):
        total = jnp.zeros((16, 128), F32)
        for p in (2 * (i % 2), 2 * (i % 2) + 1):
            for c in range(2):
                total = total + R.G[i // 2, p, c, 0:16, cols(GN)].astype(F32)
        R.VV[:, 128 * i : 128 * i + 128] = total

    latents = flat(R.latents[...]).astype(F32)
    normed = (latents - flat(R.MR[:, per_media:rows, 0:1])) * flat(R.MR[:, per_media:rows, 1:2])
    latent_low = (normed * R.VV[2:3, :] + R.VV[3:4, :]).astype(BF16)
    R.X[:, per_media:rows, :] = latent_low.reshape(images, per_lat, 1024)
    R.QA[at.l] = mm(latent_low, R.G[:, :, :, :, cols(QU)].reshape(1024, 512)).astype(BF16)
    q_all = LatGather(post, at, lambda l: R.QA.at[l])
    q_all.start()

    def low(g, carry):
        normed = (R.MED[g].astype(F32) - R.MR[g, 0:per_media, 0:1]) * R.MR[g, 0:per_media, 1:2]
        R.X[g, 0:per_media, :] = (normed * R.VV[0:1, :] + R.VV[1:2, :]).astype(BF16)
        return carry

    loop(images, low)
    second.relay()

    def pairs(n, carry):
        weight = R.G[:, :, :, :, pl.ds(pl.multiple_of(KV[0] + n * 256, 128), 256)].reshape(1024, 256)
        made = mm(R.X[...].reshape(images * rows, 1024), weight).astype(BF16)
        R.PR[:, :, span256(n)] = made.reshape(images, rows, 256)
        return carry

    loop((0, 2), pairs)
    q_all.relay()
    second.to_core()
    third.plane[0].start()
    third.into_plane()
    q_all.last()

    mask = head_mask()

    def score(g, carry):
        limit = SHORT + (LONG - SHORT) * R.bucket[g] - at.l * per_media
        row = lax.broadcasted_iota(jnp.int32, (rows, 256), 0)
        valid = jnp.logical_or(row >= per_media, row < limit)
        for half in range(2):
            span = pl.ds(256 * half, 256)
            queries = spread_heads(R.QA[:, pl.ds(pl.multiple_of(g * per_lat, per_lat), per_lat), span], mask)
            raw = mm_nt(R.PR[g, :, span], queries) * SCALE
            raw = jnp.where(valid, raw, NEG)
            top = jnp.max(raw, axis=0, keepdims=True)
            total = jnp.sum(jnp.exp(raw - top), axis=0, keepdims=True)
            R.S[2 * g + half] = raw
            R.LS[at.l, pl.ds(2 * g + half, 1), :] = top + jnp.log(total)
        return carry

    loop(images, score)
    ls = [
        post.msg(R.LS.at[at.l], R.LS.at[at.l], dev, R.LS.at[there])
        for there, dev in ((at.ly, at.yn), (at.ld, at.ycore), (at.lc, at.core))
    ]
    for m in ls:
        m.start()
    second.arrived()
    loop((2, 4), pairs)
    third.relay()
    cot.start()
    for m in ls:
        m.arrived()
    top = jnp.maximum(jnp.maximum(R.LS[0], R.LS[1]), jnp.maximum(R.LS[2], R.LS[3]))
    total = jnp.exp(R.LS[0] - top)
    for l in range(1, 4):
        total = total + jnp.exp(R.LS[l] - top)
    R.LG[...] = top + jnp.log(total)

    def mix(g, carry):
        for half in range(2):
            probs = jnp.exp(R.S[2 * g + half] - R.LG[pl.ds(2 * g + half, 1), :]).astype(BF16)
            R.PB[2 * g + half] = probs
            wide = mm_tn(probs, R.PR[g, :, pl.ds(512 + 256 * half, 256)])
            R.OP[:, pl.ds(pl.multiple_of(g * per_lat, per_lat), per_lat), pl.ds(256 * half, 256)] = (
                gather_heads(wide).reshape(4, per_lat, 256).astype(BF16)
            )
        return carry

    loop(images, mix)
    mixed = LatReduce(post, at, R.OP, R.O1, R.O2)
    mixed.start()
    d_z.near()
    d_c[1].start()
    u_z.near()
    u_c[1].start()
    mixed.relay()
    third.to_core()
    d_z.far()
    d_c[2].start()
    u_z.far()
    u_c[2].start()
    cot.relay()
    third.arrived()
    R.MX[...] = mixed.total().astype(BF16)
    left = R.G[:, :, :, 0:16, cols(OUT)].reshape(512, 512)
    right = R.G[:, :, :, 16:32, cols(OUT)].reshape(512, 512)
    latents = flat(R.latents[...]).astype(F32)
    R.RES[:, 0:512] = latents[:, 0:512] + mm(R.MX[...], left)
    R.RES[:, 512:1024] = latents[:, 512:1024] + mm(R.MX[...], right)
    mean, rstd = normal(R.RES[...])
    R.MA[at.p] = ((R.RES[...] - mean) * rstd * R.VV[4:5, :] + R.VV[5:6, :]).astype(BF16)
    mlp = PlaneGather(
        post,
        at,
        lambda x, y: R.MA.at[x * 2 + y],
        lambda x, y, h: R.MA.at[x * 2 + y, pl.ds(h * half_rows, half_rows)],
    )
    mlp.start()
    mlp.relay()
    cot.last()
    d_z.last()
    u_z.last()
    d_c[3].start()
    u_c[3].start()
    for m in d_c + u_c:
        m.arrived()
    mlp.last()

    def gates(f, carry):
        gate = mm(R.MA[...].reshape(4 * tokens, 1024), R.UU[:, :, :, :, span256(f)].reshape(1024, 256))
        back = mm_nt(R.CA[...].reshape(4 * tokens, 1024), R.UD[f].reshape(256, 1024))
        phi = 0.5 * (1.0 + lax.erf(gate * 0.7071067811865476))
        R.ACT[:, :, span256(f)] = (gate * phi).astype(BF16).reshape(4, tokens, 256)
        slope = phi + gate * jnp.exp(-0.5 * gate * gate) * 0.3989422804014327
        R.GG[:, :, span256(f)] = (back * slope).astype(BF16).reshape(4, tokens, 256)
        return carry

    loop(4, gates)

    def norm_parts(n, carry):
        made = mm_nt(R.GG[...].reshape(4 * tokens, 1024), R.UU[n].reshape(256, 1024))
        R.PT[:, :, span256(n)] = made.astype(BF16).reshape(4, tokens, 256)
        return carry

    loop(4, norm_parts)
    back = PlaneReduce(
        post,
        at,
        lambda x, y, h: R.PT.at[x * 2 + y, pl.ds(h * half_rows, half_rows)],
        lambda k: R.PY.at[0, k],
        lambda k: R.PX.at[0, k],
        lambda k: R.P2.at[0, k],
    )
    back.start()

    def down_grads(f, carry):
        act = R.ACT[:, :, span256(f)].reshape(4 * tokens, 256)
        R.gD[f] = mm_tn(act, R.CA[...].reshape(4 * tokens, 1024)).astype(BF16).reshape(2, 128, 1024)
        return carry

    loop(4, down_grads)
    gd_c = post.msg(R.gD.at[:, 1 - at.c], R.RD, at.core, R.RD)
    gd_c.start()
    back.relay()

    def up_grads(n, carry):
        low_rows = R.MA[:, :, span256(n)].reshape(4 * tokens, 256)
        made = mm_tn(low_rows, R.GG[...].reshape(4 * tokens, 1024)).astype(BF16)
        R.gU[n] = made.reshape(4, 2, 32, 1024)
        return carry

    loop(4, up_grads)
    gu_c = post.msg(R.gU.at[:, :, 1 - at.c], R.RU, at.core, R.RU)
    gu_c.start()
    gd_c.arrived()

    def add_d(zz, carry):
        R.RD[zz] = (R.RD[zz].astype(F32) + R.gD[zz, at.c].astype(F32)).astype(BF16)
        return carry

    loop(4, add_d)
    gd_z = ZReduce(post, at, lambda zz: R.RD.at[zz], lambda k: R.ZD.at[k])
    gd_z.start()

    def out_parts(n, carry):
        made = mm(R.ACT[...].reshape(4 * tokens, 1024), R.UD[:, :, :, span256(n)].reshape(1024, 256))
        R.GG[:, :, span256(n)] = made.astype(BF16).reshape(4, tokens, 256)
        return carry

    loop(4, out_parts)
    gu_c.arrived()

    def add_u(zz, carry):
        R.RU[zz] = (R.RU[zz].astype(F32) + R.gU[zz, :, at.c].astype(F32)).astype(BF16)
        return carry

    loop(4, add_u)
    gu_z = ZReduce(post, at, lambda zz: R.RU.at[zz], lambda k: R.ZU.at[k])
    gu_z.start()
    out = PlaneReduce(
        post,
        at,
        lambda x, y, h: R.GG.at[x * 2 + y, pl.ds(h * half_rows, half_rows)],
        lambda k: R.PY.at[1, k],
        lambda k: R.PX.at[1, k],
        lambda k: R.P2.at[1, k],
    )
    low_part, high_part = back.total()
    R.U[0:half_rows] = low_part
    R.U[half_rows:] = high_part

    mean, rstd = normal(R.RES[...])
    normed = (R.RES[...] - mean) * rstd
    upstream = R.U[...]
    R.GR[...] = flat(R.cotangent[...]).astype(F32) + norm_back(upstream, normed, rstd, R.VV[4:5, :])
    R.GS[...] = jnp.zeros_like(R.GS)
    R.GS[4:5, :] = jnp.sum(upstream * normed, axis=0, keepdims=True)
    R.GS[5:6, :] = jnp.sum(upstream, axis=0, keepdims=True)
    grad_attn = R.GR[...].astype(BF16)
    left = R.G[:, :, :, 0:16, cols(OUT)].reshape(512, 512)
    right = R.G[:, :, :, 16:32, cols(OUT)].reshape(512, 512)
    R.GM[at.l] = (mm_nt(grad_attn[:, 0:512], left) + mm_nt(grad_attn[:, 512:1024], right)).astype(BF16)
    gm = LatGather(post, at, lambda l: R.GM.at[l])
    gm.start()
    grad_attn = R.GR[...].astype(BF16)
    made = mm_tn(R.MX[...], grad_attn[:, 0:512]).astype(BF16)
    R.gA[:, :, :, 0:16, cols(GOUT)] = made.reshape(4, 4, 2, 16, 512)
    made = mm_tn(R.MX[...], grad_attn[:, 512:1024]).astype(BF16)
    R.gA[:, :, :, 16:32, cols(GOUT)] = made.reshape(4, 4, 2, 16, 512)
    w_out = Collect(post, at, R.gA, R.RA, R.WY, R.WX, R.W2, R.ZW, GOUT, OUT)
    w_out.start()
    gm.relay()
    gm.last()

    def grad_probs(g, carry):
        lat_rows = pl.ds(pl.multiple_of(g * per_lat, per_lat), per_lat)
        for half in range(2):
            upper = pl.ds(512 + 256 * half, 256)
            wide = spread_heads(R.GM[:, lat_rows, pl.ds(256 * half, 256)], mask)
            made = mm_nt(R.PR[g, :, upper], wide)
            probs = R.PB[2 * g + half]
            R.S[2 * g + half] = made
            R.DL[at.l, pl.ds(2 * g + half, 1), :] = jnp.sum(probs.astype(F32) * made, axis=0, keepdims=True)
            R.gP[g, :, upper] = mm(probs, wide).astype(BF16)
        return carry

    loop(images, grad_probs)
    dl = [
        post.msg(R.DL.at[at.l], R.DL.at[at.l], dev, R.DL.at[there])
        for there, dev in ((at.ly, at.yn), (at.ld, at.ycore), (at.lc, at.core))
    ]
    for m in dl:
        m.start()
    w_out.into_plane()

    def kv_grads(n, carry):
        low_rows = R.X[:, :, span256(lax.rem(n, 4))].reshape(images * rows, 256)
        lanes = pl.ds(pl.multiple_of(lax.div(n, 4) * 512, 512), 512)
        made = mm_tn(low_rows, R.gP[:, :, lanes].reshape(images * rows, 512)).astype(BF16)
        R.gU[lax.rem(n, 4), :, :, :, lanes] = made.reshape(4, 2, 32, 512)
        return carry

    gu_c.sent()
    loop((4, 8), kv_grads)
    w_val = Collect(post, at, R.gU, R.RK, R.WY, R.WX, R.W2, R.ZW, (512, 512), VAL)
    w_val.start()
    for m in dl:
        m.arrived()
    R.LG[...] = R.DL[0] + R.DL[1] + R.DL[2] + R.DL[3]

    def grad_scores(g, carry):
        lat_rows = pl.ds(pl.multiple_of(g * per_lat, per_lat), per_lat)
        for half in range(2):
            span = pl.ds(256 * half, 256)
            grads = R.PB[2 * g + half].astype(F32) * (R.S[2 * g + half] - R.LG[pl.ds(2 * g + half, 1), :])
            grads = grads.astype(BF16)
            wide = mm_tn(grads, R.PR[g, :, span]) * SCALE
            R.QP[:, lat_rows, span] = gather_heads(wide).reshape(4, per_lat, 256).astype(BF16)
            queries = spread_heads(R.QA[:, lat_rows, span], mask)
            R.gP[g, :, span] = (mm(grads, queries) * SCALE).astype(BF16)
        return carry

    loop(images, grad_scores)
    gq = LatReduce(post, at, R.QP, R.Q1, R.Q2)
    gq.start()
    w_out.relay()
    w_val.into_plane()
    loop((0, 4), kv_grads)
    w_key = Collect(post, at, R.gU, R.RK, R.WY, R.WX, R.W2, R.ZW, (0, 512), KEY)
    w_key.start()
    gq.relay()
    gd_z.relay()
    gu_z.relay()
    w_out.into_z()
    w_val.relay()
    w_key.into_plane()

    def media_copy(h):
        return pltpu.make_async_copy(R.MG, R.grad_media.at[pl.ds(h * 2, 2)], R.local.at[0])

    def media_grads(h, carry):
        span = pl.ds(h * 2, 2)
        weight = R.G[:, :, :, :, cols(KV)].reshape(1024, 1024)
        upstream = mm_nt(R.gP[span].reshape(2 * rows, 1024), weight).reshape(2, rows, 1024)
        R.U[pl.ds(h * 2 * per_lat, 2 * per_lat)] = upstream[:, per_media:rows, :].reshape(2 * per_lat, 1024)
        upstream = upstream[:, 0:per_media, :]
        rstd = R.MR[span, 0:per_media, 1:2]
        normed = (R.MED[span].astype(F32) - R.MR[span, 0:per_media, 0:1]) * rstd
        made = norm_back(upstream, normed, rstd, R.VV[0:1, :]).astype(R.MG.dtype)
        pl.when(h >= 1)(lambda: media_copy(h - 1).wait())
        R.MG[...] = made
        media_copy(h).start()
        R.GS[0:1, :] += jnp.sum(flat(upstream * normed), axis=0, keepdims=True)
        R.GS[1:2, :] += jnp.sum(flat(upstream), axis=0, keepdims=True)
        return carry

    loop((0, images // 4), media_grads)
    w_val.into_z()
    w_key.relay()
    w_out.z_relay()
    loop((images // 4, images // 2), media_grads)
    media_copy(images // 2 - 1).wait()
    w_val.z_relay()

    grad_query = gq.total().astype(BF16)
    latent_low = flat(R.X[:, per_media:rows, :])
    upstream = R.U[...] + mm_nt(grad_query, R.G[:, :, :, :, cols(QU)].reshape(1024, 512))
    rstd = flat(R.MR[:, per_media:rows, 1:2])
    normed = (flat(R.latents[...]).astype(F32) - flat(R.MR[:, per_media:rows, 0:1])) * rstd
    R.grad_latents[...] = (R.GR[...] + norm_back(upstream, normed, rstd, R.VV[2:3, :])).reshape(
        images, per_lat, 1024
    )
    R.GS[2:3, :] = jnp.sum(upstream * normed, axis=0, keepdims=True)
    R.GS[3:4, :] = jnp.sum(upstream, axis=0, keepdims=True)
    R.gA[:, :, :, :, cols(QU)] = mm_tn(latent_low, grad_query).astype(BF16).reshape(4, 4, 2, 32, 512)
    for i in range(8):
        piece = R.GS[:, 128 * i : 128 * i + 128].astype(BF16)
        for p in (2 * (i % 2), 2 * (i % 2) + 1):
            for c in range(2):
                R.gA[i // 2, p, c, 0:16, cols(GN)] = piece
                R.gA[i // 2, p, c, 16:32, cols(GN)] = jnp.zeros((16, 128), BF16)
    w_qg = Collect(post, at, R.gA, R.RA, R.WY, R.WX, R.W2, R.ZW, GQG, GQG)
    w_qg.start()
    w_key.into_z()
    w_qg.into_plane()
    out.start()
    gd_z.total(R.grad_down)
    gu_z.total(R.SF)
    R.SU[...] = R.SF[...].astype(BF16)
    R.AU[at.p] = R.SU[at.p]
    up = [
        post.msg(R.SU.at[there], R.AU.at[at.p], dev, R.AU.at[there])
        for there, dev in ((at.px, at.xn), (at.py, at.yn), (at.pd, at.diag))
    ]
    for m in up:
        m.start()
    w_qg.relay()
    out.relay()
    w_key.z_relay()
    w_out.total(R.grad_pack.at[:, cols(OUT)])
    w_val.total(R.grad_pack.at[:, cols(VAL)])
    w_qg.into_z()
    w_qg.z_relay()
    low_part, high_part = out.total()
    R.latents_out[...] = jnp.concatenate(
        [R.RES[0:half_rows] + low_part, R.RES[half_rows:] + high_part], axis=0
    ).astype(BF16).reshape(images, per_lat, 1024)
    w_key.total(R.grad_pack.at[:, cols(KEY)])
    for m in up:
        m.arrived()
    for p in range(4):
        for zz in range(4):
            for cc in range(2):
                R.grad_up[:, 128 * (8 * zz + 2 * p + cc) : 128 * (8 * zz + 2 * p + cc) + 128] = R.AU[
                    p, :, 128 * (2 * zz + cc) : 128 * (2 * zz + cc) + 128
                ].astype(F32)
    w_qg.total(R.grad_pack.at[:, cols(GQG)])


def loop(bounds, step):
    first, last = bounds if isinstance(bounds, tuple) else (0, bounds)
    with jax.named_scope(step.__name__):
        lax.fori_loop(first, last, step, 0)


PLACES = {"bucket": pltpu.SMEM, "media": pl.ANY, "grad_media": pl.ANY}


class Refs:
    def __init__(self, names, refs):
        for name, ref in zip(names, refs):
            setattr(self, name, ref)


def build(kernel_body, inputs, outputs, scratch, messages, cid, name):
    in_names = [n for n, _ in inputs]
    out_names = [n for n, _, _ in outputs]
    scratch_names = [n for n, _, _ in scratch]

    def kernel(*refs):
        R = Refs(in_names + out_names + scratch_names, refs)
        at = Place()
        R.local = refs[-3]
        post = Post(refs[-2], refs[-1])
        kernel_body(at, post, R)
        post.drain()
        assert post.count == messages, post.count

    specs = [
        pl.BlockSpec(memory_space=PLACES.get(n, pltpu.VMEM)) for n in in_names
    ]
    return pl.pallas_call(
        kernel,
        out_shape=[jax.ShapeDtypeStruct(s, d) for _, s, d in outputs],
        in_specs=specs,
        out_specs=[
            pl.BlockSpec(memory_space=PLACES.get(n, pltpu.VMEM)) for n, _, _ in outputs
        ],
        scratch_shapes=[pltpu.VMEM(s, d) for _, s, d in scratch]
        + [pltpu.SemaphoreType.DMA((2,)), pltpu.SemaphoreType.DMA((messages,)), pltpu.SemaphoreType.DMA((messages,))],
        compiler_params=pltpu.CompilerParams(
            collective_id=cid, has_side_effects=True, vmem_limit_bytes=62 << 20
        ),
        name=name,
    )(*[v for _, v in inputs])


def layer(media, latents, bucket, cotangent, norms, w_query, w_keyvalue, w_output, w_up, w_down):
    images, per_media, _ = media.shape
    per_lat = latents.shape[1]
    rows = per_media + per_lat
    tokens = images * per_lat
    inputs = [
        ("media", media),
        ("latents", latents),
        ("cotangent", cotangent),
        ("bucket", bucket),
        ("norms", norms),
        ("w_query", w_query),
        ("w_keyvalue", w_keyvalue),
        ("w_output", w_output),
        ("w_up", w_up),
        ("w_down", w_down),
    ]
    outputs = [
        ("latents_out", (images, per_lat, 1024), BF16),
        ("grad_media", (images, per_media, 1024), BF16),
        ("grad_latents", (images, per_lat, 1024), F32),
        ("grad_pack", (32, WIDE), F32),
        ("grad_up", (32, 4096), F32),
        ("grad_down", (128, 1024), F32),
    ]
    scratch = [
        ("MED", (images, per_media, 1024), BF16),
        ("X", (images, rows, 1024), BF16),
        ("MR", (images, rows, 2), F32),
        ("PR", (images, rows, 1024), BF16),
        ("S", (2 * images, rows, 256), F32),
        ("PB", (2 * images, rows, 256), BF16),
        ("QA", (4, tokens, 512), BF16),
        ("MX", (tokens, 512), BF16),
        ("RES", (tokens, 1024), F32),
        ("MA", (4, tokens, 1024), BF16),
        ("CA", (4, tokens, 1024), BF16),
        ("UD", (4, 2, 128, 1024), BF16),
        ("UU", (4, 4, 2, 32, 1024), BF16),
        ("G", (4, 4, 2, 32, WIDE), BF16),
        ("VV", (16, 1024), F32),
        ("WS", (4, 32, 1024), BF16),
        ("LS", (4, 2 * images, 256), F32),
        ("LG", (2 * images, 256), F32),
        ("OP", (4, tokens, 512), BF16),
        ("O1", (2, tokens, 512), BF16),
        ("O2", (tokens, 512), BF16),
        ("MG", (2, per_media, 1024), BF16),
        ("ACT", (4, tokens, 1024), BF16),
        ("GG", (4, tokens, 1024), BF16),
        ("PT", (4, tokens, 1024), BF16),
        ("PY", (2, 2, tokens // 2, 1024), BF16),
        ("PX", (2, 2, tokens // 2, 1024), BF16),
        ("P2", (2, 2, tokens // 2, 1024), BF16),
        ("gD", (4, 2, 128, 1024), BF16),
        ("gU", (4, 4, 2, 32, 1024), BF16),
        ("RD", (4, 128, 1024), BF16),
        ("RU", (4, 4, 32, 1024), BF16),
        ("ZD", (4, 128, 1024), BF16),
        ("ZU", (4, 4, 32, 1024), BF16),
        ("U", (tokens, 1024), F32),
        ("GR", (tokens, 1024), F32),
        ("GS", (16, 1024), F32),
        ("GM", (4, tokens, 512), BF16),
        ("gP", (images, rows, 1024), BF16),
        ("DL", (4, 2 * images, 256), F32),
        ("QP", (4, tokens, 512), BF16),
        ("Q1", (2, tokens, 512), BF16),
        ("Q2", (tokens, 512), BF16),
        ("gA", (4, 4, 2, 32, NARROW), BF16),
        ("RA", (4, 4, 32, NARROW), BF16),
        ("RK", (4, 4, 32, 1024), BF16),
        ("WY", (2, 4, 16, WIDE), BF16),
        ("WX", (2, 4, 16, WIDE), BF16),
        ("W2", (2, 4, 16, WIDE), BF16),
        ("ZW", (4, 32, WIDE), BF16),
        ("SF", (4, 32, 1024), F32),
        ("SU", (4, 32, 1024), BF16),
        ("AU", (4, 32, 1024), BF16),
    ]
    return build(kernel_body, inputs, outputs, scratch, MESSAGES, 1, "resampler")


def solution(mesh):
    sizes = dict(mesh.shape)
    blocks = sizes["img"] // BLOCK
    names = ("img", "lat")

    def block_shard(weight):
        if blocks == 1:
            return weight
        whole = lax.all_gather(weight, names, axis=0, tiled=True)
        each = whole.shape[0] // (BLOCK * sizes["lat"])
        mine = lax.rem(lax.axis_index("img"), BLOCK) * sizes["lat"] + lax.axis_index("lat")
        return lax.dynamic_slice_in_dim(whole, mine * each, each, 0)

    def own_shard(gradient):
        if blocks == 1:
            return gradient
        each = gradient.shape[0]
        mine = lax.rem(lax.axis_index("img"), BLOCK) * sizes["lat"] + lax.axis_index("lat")
        whole = jnp.zeros((each * BLOCK * sizes["lat"],) + gradient.shape[1:], gradient.dtype)
        whole = lax.dynamic_update_slice_in_dim(whole, gradient, mine * each, 0)
        return lax.psum_scatter(whole, names, scatter_dimension=0, tiled=True)

    def on_device(
        media,
        latents,
        bucket,
        gain_media,
        shift_media,
        gain_latent,
        shift_latent,
        gain_mlp,
        shift_mlp,
        w_query,
        w_keyvalue,
        w_output,
        w_up,
        w_down,
        cotangent,
    ):
        lat = lax.axis_index("lat")
        norms = [
            block_shard(v) for v in (gain_media, shift_media, gain_latent, shift_latent, gain_mlp, shift_mlp)
        ]
        norms = jnp.pad(jnp.stack(norms), ((0, 10), (0, 0)))
        latents_out, grad_media, grad_latents, grad_pack, grad_up, grad_down = layer(
            media,
            latents,
            bucket,
            cotangent,
            norms,
            *[block_shard(v) for v in (w_query, w_keyvalue, w_output, w_up, w_down)],
        )
        norm_grads = lax.dynamic_slice_in_dim(grad_pack[0:6, GN[0] : GN[0] + GN[1]], lat * 32, 32, 1)
        grad_out = jnp.concatenate(
            [grad_pack[0:16, OUT[0] : OUT[0] + OUT[1]], grad_pack[16:32, OUT[0] : OUT[0] + OUT[1]]], axis=1
        )
        return (
            latents_out,
            grad_media.astype(F32),
            grad_latents,
            *[own_shard(norm_grads[k]) for k in range(6)],
            own_shard(grad_pack[:, QU[0] : QU[0] + QU[1]]),
            own_shard(grad_pack[:, KV[0] : KV[0] + KV[1]]),
            own_shard(grad_out),
            own_shard(grad_up),
            own_shard(grad_down),
        )

    rows = P("img", "lat", None)
    shard = P(names)
    wide = P(names, None)
    return jax.shard_map(
        on_device,
        mesh=mesh,
        in_specs=(rows, rows, P("img")) + (shard,) * 6 + (wide,) * 5 + (rows,),
        out_specs=(rows, rows, rows) + (shard,) * 6 + (wide,) * 5,
        check_vma=False,
    )
```

```python
import jax
import jax.numpy as jnp
from jax import lax
from jax.experimental import pallas as pl
from jax.experimental.pallas import tpu as pltpu
from jax.sharding import PartitionSpec as P

MESH = pl.DeviceIdType.MESH
BF16 = jnp.bfloat16
F32 = jnp.float32

SHORT = 256
LONG = 576
HEADS = 8
EPS = 1e-05
SCALE = 0.125
NEG = -1e30

BLOCK = 8

QU = (0, 512)
GN = (512, 128)
KEY = (640, 512)
VAL = (1152, 512)
KV = (640, 1024)
OUT = (1664, 512)
WIDE = 2176
GOUT = (640, 512)
NARROW = 1152
MESSAGES = 256


def mm(a, b):
    return lax.dot_general(a, b, (((1,), (0,)), ((), ())), preferred_element_type=F32)


def mm_nt(a, b):
    return lax.dot_general(a, b, (((1,), (1,)), ((), ())), preferred_element_type=F32)


def mm_tn(a, b):
    return lax.dot_general(a, b, (((0,), (0,)), ((), ())), preferred_element_type=F32)


def cols(span):
    return pl.ds(span[0], span[1])


def flat(values):
    return values.reshape(-1, values.shape[-1])


def normal(values):
    mean = jnp.mean(values, axis=-1, keepdims=True)
    centred = values - mean
    spread = jnp.mean(centred * centred, axis=-1, keepdims=True)
    return mean, lax.rsqrt(spread + EPS)


def norm_back(upstream, normed, rstd, gain):
    scaled = upstream * gain
    first = jnp.mean(scaled, axis=-1, keepdims=True)
    second = jnp.mean(scaled * normed, axis=-1, keepdims=True)
    return (scaled - first - normed * second) * rstd


class Place:
    def __init__(self):
        img = lax.axis_index("img")
        lat = lax.axis_index("lat")
        self.i = lax.rem(img, BLOCK)
        self.base = img - self.i
        self.z = lax.div(self.i, 2)
        self.x = lax.rem(self.i, 2)
        self.l = lat
        self.y = lax.div(lat, 2)
        self.c = lax.rem(lat, 2)
        self.z1 = self.z + 1 - 2 * lax.rem(self.z, 2)
        self.z2 = lax.rem(self.z + 2, 4)
        self.z3 = 3 - self.z
        self.mid = jnp.logical_or(self.z == 1, self.z == 2)
        self.zs = (self.z, self.z1, self.z2, self.z3)
        self.end = jnp.logical_or(self.z == 0, self.z == 3)
        self.p = self.x * 2 + self.y
        self.q = self.z * 4 + self.p
        self.px = (1 - self.x) * 2 + self.y
        self.py = self.x * 2 + 1 - self.y
        self.pd = 3 - self.p
        self.lc = self.y * 2 + 1 - self.c
        self.ly = (1 - self.y) * 2 + self.c
        self.ld = 3 - self.l
        self.core = self.dev(self.z, self.x, self.y, 1 - self.c)
        self.xn = self.dev(self.z, 1 - self.x, self.y, self.c)
        self.yn = self.dev(self.z, self.x, 1 - self.y, self.c)
        self.diag = self.dev(self.z, 1 - self.x, 1 - self.y, self.c)
        self.ycore = self.dev(self.z, self.x, 1 - self.y, 1 - self.c)
        self.zn1 = self.dev(self.z1, self.x, self.y, self.c)
        self.zn2 = self.dev(self.z2, self.x, self.y, self.c)
        self.zn3 = self.dev(self.z3, self.x, self.y, self.c)

    def dev(self, z, x, y, c):
        return (self.base + z * 2 + x, y * 2 + c)

    def greet(self):
        barrier = pltpu.get_barrier_semaphore()
        peers = (self.core, self.xn, self.yn, self.diag, self.ycore, self.zn1, self.zn2, self.zn3)
        for peer in peers:
            pl.semaphore_signal(barrier, inc=1, device_id=peer, device_id_type=MESH)
        pl.semaphore_wait(barrier, len(peers))


def guarded(when, action):
    if when is None:
        action()
    else:
        pl.when(when)(action)


class Msg:
    def __init__(self, post, src, dst, dev, into, key=None, when=None):
        self.k = post.count
        post.count += 1
        self.key = self.k if key is None else key
        self.when = when
        self.post, self.src, self.dst, self.dev, self.into = post, src, dst, dev, into
        self.done = False
        post.all.append(self)

    def copy(self, src, dst):
        return pltpu.make_async_remote_copy(
            src_ref=src,
            dst_ref=dst,
            send_sem=self.post.send.at[self.k],
            recv_sem=self.post.recv.at[self.key],
            device_id=self.dev,
            device_id_type=MESH,
        )

    def start(self):
        guarded(self.when, lambda: self.copy(self.src, self.dst).start())

    def arrived(self):
        self.copy(self.into, self.into).wait_recv()

    def sent(self):
        if self.done:
            return
        self.done = True
        with jax.named_scope('S_%d' % self.k):
            guarded(self.when, lambda: self.copy(self.src, self.dst).wait_send())


class Post:
    def __init__(self, send, recv):
        self.send = send
        self.recv = recv
        self.count = 0
        self.all = []

    def msg(self, *a, **k):
        return Msg(self, *a, **k)

    def drain(self):
        for m in self.all:
            m.sent()


class ZGather:
    def __init__(self, post, at, view, core):
        own = view(at.z)
        self.at = at
        self.m1 = post.msg(own, own, at.zn1, view(at.z1))
        self.m2 = post.msg(own, own, at.zn2, view(at.z2))
        self.m3 = post.msg(own, own, at.zn3, view(at.z3), when=at.mid)
        self.relay = post.msg(view(at.z2), view(at.z2), at.zn1, view(at.z3), key=self.m3.k, when=at.mid)
        early = jnp.where(at.mid, at.z2, at.z1)
        late = jnp.where(at.mid, at.z1, at.z2)
        self.core = [core(zz) for zz in (at.z, early, late, at.z3)]

    def start(self):
        pl.when(self.at.mid)(self.m1.start)
        pl.when(self.at.end)(self.m2.start)
        self.core[0].start()

    def far(self):
        @pl.when(self.at.mid)
        def _():
            self.m2.arrived()
            self.relay.start()
            self.m3.start()
            self.m2.start()

        pl.when(self.at.end)(self.m1.start)

    def last(self):
        pl.when(self.at.end)(self.m1.arrived)
        self.core[1].start()
        pl.when(self.at.mid)(self.m1.arrived)
        pl.when(self.at.end)(self.m2.arrived)
        self.core[2].start()
        self.m3.arrived()
        self.core[3].start()

    def all(self):
        for m in self.core:
            m.arrived()


class PlaneGather:
    def __init__(self, post, at, view, half):
        own = view(at.x, at.y)
        ox, oy = 1 - at.x, 1 - at.y
        self.mx = post.msg(own, own, at.xn, view(ox, at.y))
        self.my = post.msg(own, own, at.yn, view(at.x, oy))
        self.hy = post.msg(half(ox, at.y, 0), half(ox, at.y, 0), at.yn, half(ox, oy, 0))
        self.hx = post.msg(half(at.x, oy, 1), half(at.x, oy, 1), at.xn, half(ox, oy, 1))

    def start(self):
        self.mx.start()
        self.my.start()

    def relay(self):
        self.mx.arrived()
        self.hy.start()
        self.my.arrived()
        self.hx.start()

    def last(self):
        self.hy.arrived()
        self.hx.arrived()


class HalfGather:
    def __init__(self, post, at, half):
        x, y = at.x, at.y
        ox, oy = 1 - x, 1 - y

        def msg(part, dev, into):
            return post.msg(part, part, dev, into)

        self.x0 = msg(half(x, y, 0), at.xn, half(ox, y, 0))
        self.y1 = msg(half(x, y, 1), at.yn, half(x, oy, 1))
        self.x1 = msg(half(x, y, 1), at.xn, half(ox, y, 1))
        self.y0 = msg(half(x, y, 0), at.yn, half(x, oy, 0))
        self.hy = msg(half(ox, y, 0), at.yn, half(ox, oy, 0))
        self.hx = msg(half(x, oy, 1), at.xn, half(ox, oy, 1))

    def start(self):
        self.x0.start()
        self.y1.start()

    def relay(self):
        self.x0.arrived()
        self.hy.start()
        self.y1.arrived()
        self.hx.start()

    def rest(self):
        self.x1.start()
        self.y0.start()

    def last(self):
        for m in (self.x1, self.y0, self.hy, self.hx):
            m.arrived()


class Spread:
    def __init__(self, post, at, G, span):
        lanes = cols(span)

        def view(zz, x, y):
            return G.at[zz, x * 2 + y, at.c, :, lanes]

        def half(zz, x, y, h):
            return G.at[zz, x * 2 + y, at.c, pl.ds(16 * h, 16), lanes]

        own = view(at.z, at.x, at.y)
        self.z = [
            post.msg(own, own, dev, view(zz, at.x, at.y))
            for zz, dev in ((at.z1, at.zn1), (at.z2, at.zn2), (at.z3, at.zn3))
        ]
        self.plane = [
            PlaneGather(
                post, at, lambda x, y, zz=zz: view(zz, x, y), lambda x, y, h, zz=zz: half(zz, x, y, h)
            )
            for zz in at.zs
        ]
        self.core = [
            post.msg(
                G.at[zz, :, at.c, :, lanes], G.at[zz, :, at.c, :, lanes], at.core, G.at[zz, :, 1 - at.c, :, lanes]
            )
            for zz in at.zs
        ]

    def start(self):
        for m in self.z:
            m.start()

    def into_plane(self):
        for k in range(3):
            self.z[k].arrived()
            self.plane[k + 1].start()

    def along_z(self):
        for m in self.z:
            m.arrived()

    def over_plane(self):
        for g in self.plane:
            g.start()

    def relay(self):
        for g in self.plane:
            g.relay()

    def to_core(self):
        for g, m in zip(self.plane, self.core):
            g.last()
            m.start()

    def arrived(self):
        for m in self.core:
            m.arrived()


class LatGather:
    def __init__(self, post, at, view):
        self.mc = post.msg(view(at.l), view(at.l), at.core, view(at.lc))
        self.my = post.msg(view(at.l), view(at.l), at.yn, view(at.ly))
        self.fc = post.msg(view(at.ly), view(at.ly), at.core, view(at.ld))

    def start(self):
        self.my.start()
        self.mc.start()

    def relay(self):
        self.my.arrived()
        self.fc.start()

    def last(self):
        self.mc.arrived()
        self.fc.arrived()


class LatReduce:
    def __init__(self, post, at, parts, first, second):
        self.at, self.parts, self.first, self.second = at, parts, first, second
        self.m0 = post.msg(parts.at[at.lc], first.at[0], at.core, first.at[0])
        self.m1 = post.msg(parts.at[at.ld], first.at[1], at.core, first.at[1])
        self.m2 = post.msg(parts.at[at.ly], second, at.yn, second)

    def start(self):
        self.m1.start()
        self.m0.start()

    def relay(self):
        self.m1.arrived()
        ly = self.at.ly
        self.parts[ly] = (self.parts[ly].astype(F32) + self.first[1].astype(F32)).astype(BF16)
        self.m2.start()

    def total(self):
        self.m0.arrived()
        self.m2.arrived()
        near = self.parts[self.at.l].astype(F32) + self.first[0].astype(F32)
        return near + self.second[...].astype(F32)


class PlaneReduce:
    def __init__(self, post, at, part, by, bx, b2):
        x, y = at.x, at.y
        ox, oy = 1 - x, 1 - y
        self.part, self.by, self.bx, self.b2 = part, by, bx, b2
        self.x, self.y, self.ox, self.oy = x, y, ox, oy
        self.my1 = post.msg(part(ox, oy, 0), by(1), at.yn, by(1))
        self.mx1 = post.msg(part(ox, oy, 1), bx(1), at.xn, bx(1))
        self.my0 = post.msg(part(x, oy, 0), by(0), at.yn, by(0))
        self.mx0 = post.msg(part(ox, y, 1), bx(0), at.xn, bx(0))
        self.f0 = post.msg(part(ox, y, 0), b2(0), at.xn, b2(0))
        self.f1 = post.msg(part(x, oy, 1), b2(1), at.yn, b2(1))

    def start(self):
        self.my1.start()
        self.mx1.start()

    def rest(self):
        self.my0.start()
        self.mx0.start()

    def relay(self):
        self.my1.arrived()
        there = self.part(self.ox, self.y, 0)
        there[...] = (there[...].astype(F32) + self.by(1)[...].astype(F32)).astype(BF16)
        self.f0.start()
        self.mx1.arrived()
        there = self.part(self.x, self.oy, 1)
        there[...] = (there[...].astype(F32) + self.bx(1)[...].astype(F32)).astype(BF16)
        self.f1.start()

    def total(self):
        self.my0.arrived()
        self.f0.arrived()
        low = self.part(self.x, self.y, 0)[...].astype(F32) + self.by(0)[...].astype(F32)
        low = low + self.b2(0)[...].astype(F32)
        self.mx0.arrived()
        self.f1.arrived()
        high = self.part(self.x, self.y, 1)[...].astype(F32) + self.bx(0)[...].astype(F32)
        return low, high + self.b2(1)[...].astype(F32)


class ZReduce:
    def __init__(self, post, at, term, buf):
        self.at, self.term, self.buf = at, term, buf
        self.m1 = post.msg(term(at.z1), buf(0), at.zn1, buf(0))
        self.m2 = post.msg(term(at.z2), buf(1), at.zn2, buf(1))
        self.m3 = post.msg(term(at.z3), buf(2), at.zn3, buf(2), when=at.mid)
        self.rel = post.msg(term(at.z3), buf(3), at.zn1, buf(3), when=at.end)

    def start_last(self):
        self.rel.start()
        self.m3.start()

    def start_far(self):
        pl.when(self.at.end)(self.m2.start)

    def start_near(self):
        self.m1.start()

    def relay(self):
        @pl.when(self.at.mid)
        def _():
            self.rel.arrived()
            there = self.term(self.at.z2)
            there[...] = (there[...].astype(F32) + self.buf(3)[...].astype(F32)).astype(BF16)
            self.m2.start()

    def total(self, out):
        self.m1.arrived()
        self.m2.arrived()
        value = self.term(self.at.z)[...].astype(F32) + self.buf(0)[...].astype(F32)
        out[...] = value + self.buf(1)[...].astype(F32)

        @pl.when(self.at.mid)
        def _():
            self.m3.arrived()
            out[...] += self.buf(2)[...].astype(F32)


class ZDirect:
    def __init__(self, post, at, term, buf):
        self.at, self.term, self.buf = at, term, buf
        self.msgs = [
            post.msg(term(zz), buf(k), dev, buf(k))
            for k, (zz, dev) in enumerate(((at.z1, at.zn1), (at.z2, at.zn2), (at.z3, at.zn3)))
        ]

    def start(self):
        for m in self.msgs[::-1]:
            m.start()

    def total(self, out):
        value = self.term(self.at.z)[...].astype(F32)
        for k, m in enumerate(self.msgs):
            m.arrived()
            value = value + self.buf(k)[...].astype(F32)
        out[...] = value


class Collect:
    def __init__(self, post, at, grads, near, by, bx, b2, bz, src, dst):
        self.at, self.grads, self.near, self.src = at, grads, near, src
        self.lanes, self.there = cols(src), cols(dst)
        self.core = post.msg(
            grads.at[:, :, 1 - at.c, :, self.lanes], near.at[:, :, :, self.lanes], at.core,
            near.at[:, :, :, self.lanes],
        )
        self.plane = PlaneReduce(
            post,
            at,
            lambda x, y, h: near.at[:, x * 2 + y, pl.ds(16 * h, 16), self.lanes],
            lambda k: by.at[k, :, :, self.there],
            lambda k: bx.at[k, :, :, self.there],
            lambda k: b2.at[k, :, :, self.there],
        )
        self.z = ZDirect(
            post, at, lambda zz: near.at[zz, at.p, :, self.lanes], lambda k: bz.at[k, :, self.there]
        )

    def start(self):
        self.core.start()

    def into_plane(self):
        self.core.arrived()

        def add(zz, carry):
            mine = self.grads[zz, :, self.at.c, :, self.lanes].astype(F32)
            self.near[zz, :, :, self.lanes] = (self.near[zz, :, :, self.lanes].astype(F32) + mine).astype(BF16)
            return carry

        lax.fori_loop(0, 4, add, 0)
        self.plane.start()
        self.plane.rest()

    def relay(self):
        self.plane.relay()

    def into_z(self):
        low, high = self.plane.total()
        self.near[:, self.at.p, 0:16, self.lanes] = low.astype(BF16)
        self.near[:, self.at.p, 16:32, self.lanes] = high.astype(BF16)
        self.z.start()

    def total(self, out):
        self.z.total(out)


class CollectNorms:
    def __init__(self, post, at, grads, near, by, bx, b2, bz, span):
        self.at, self.grads, self.near, self.lanes = at, grads, near, cols(span)
        low = pl.ds(0, 16)

        def part(p):
            return near.at[:, p, low, self.lanes]

        theirs = grads.at[:, :, 1 - at.c, low, self.lanes]
        here = near.at[:, :, low, self.lanes]
        self.core = post.msg(theirs, here, at.core, here)
        self.bufs = [b.at[0, :, :, self.lanes] for b in (bx, by, b2)]
        self.plane = [
            post.msg(part(p), buf, dev, buf)
            for p, buf, dev in zip((at.px, at.py, at.pd), self.bufs, (at.xn, at.yn, at.diag))
        ]
        self.z = ZDirect(
            post, at, lambda zz: near.at[zz, at.p, low, self.lanes], lambda k: bz.at[k, low, self.lanes]
        )

    def start(self):
        self.core.start()

    def into_plane(self):
        self.core.arrived()
        mine = self.grads[:, :, self.at.c, 0:16, self.lanes].astype(F32)
        self.near[:, :, 0:16, self.lanes] = (self.near[:, :, 0:16, self.lanes].astype(F32) + mine).astype(BF16)
        for m in self.plane:
            m.start()

    def into_z(self):
        total = self.near[:, self.at.p, 0:16, self.lanes].astype(F32)
        for m, buf in zip(self.plane, self.bufs):
            m.arrived()
            total = total + buf[...].astype(F32)
        self.near[:, self.at.p, 0:16, self.lanes] = total.astype(BF16)
        self.z.start()

    def total(self, out):
        self.z.total(out)


def head_mask():
    rows = lax.div(lax.broadcasted_iota(jnp.int32, (256, 256), 0), 64)
    lanes = lax.div(lax.broadcasted_iota(jnp.int32, (256, 256), 1), 64)
    return (rows == lanes).astype(F32).astype(BF16)


def spread_heads(part, mask):
    rows = part.reshape(64, 256)
    return jnp.concatenate([rows, rows, rows, rows], axis=0) * mask


def gather_heads(wide):
    lane = lax.div(lax.broadcasted_iota(jnp.int32, (64, 256), 1), 64)
    out = jnp.where(lane == 0, wide[0:64], 0.0)
    for h in range(1, 4):
        out = out + jnp.where(lane == h, wide[64 * h : 64 * h + 64], 0.0)
    return out


def pick(values, k):
    out = values[-1]
    for i in range(len(values) - 2, -1, -1):
        out = jnp.where(k == i, values[i], out)
    return out


def span256(n):
    return pl.ds(pl.multiple_of(n * 256, 256), 256)


def kernel_body(at, post, R):
    images, per_media, _ = R.MED.shape
    per_lat = R.latents.shape[1]
    rows = per_media + per_lat
    tokens = images * per_lat
    half_rows = tokens // 2
    zs = at.zs

    media_in = pltpu.make_async_copy(R.media, R.MED, R.local.at[0])
    media_in.start()
    R.G[at.z, at.p, at.c, :, cols(QU)] = R.w_query[...]
    R.G[at.z, at.p, at.c, :, cols(KV)] = R.w_keyvalue[...]
    R.G[at.z, at.p, at.c, 0:16, cols(OUT)] = R.w_output[:, 0:512]
    R.G[at.z, at.p, at.c, 16:32, cols(OUT)] = R.w_output[:, 512:1024]
    norms = [ref[...].astype(F32).reshape(1, 32) for ref in (R.n0, R.n1, R.n2, R.n3, R.n4, R.n5)]
    norms = jnp.concatenate(norms + [jnp.zeros((10, 32), F32)], axis=0)
    norms = jnp.concatenate([norms, norms, norms, norms], axis=1)
    lanes = lax.div(lax.broadcasted_iota(jnp.int32, (16, 128), 1), 32)
    R.G[at.z, at.p, at.c, 0:16, cols(GN)] = jnp.where(lanes == at.l, norms, 0.0).astype(BF16)
    R.G[at.z, at.p, at.c, 16:32, cols(GN)] = jnp.zeros((16, 128), BF16)
    R.UD[at.z, at.c] = R.w_down[...]
    for p in range(4):
        for zz in range(4):
            for cc in range(2):
                R.WS[p, :, 128 * (2 * zz + cc) : 128 * (2 * zz + cc) + 128] = R.w_up[
                    :, 128 * (8 * zz + 2 * p + cc) : 128 * (8 * zz + 2 * p + cc) + 128
                ]
    R.UU[at.z, at.p, at.c] = R.WS[at.p]
    R.CA[at.p] = R.cotangent[...].reshape(tokens, 1024)

    with jax.named_scope("greet"):
        at.greet()

    first = Spread(post, at, R.G, (0, 640))
    keys = Spread(post, at, R.G, KEY)
    second = Spread(post, at, R.G, VAL)
    third = Spread(post, at, R.G, OUT)
    up = [
        post.msg(R.WS.at[there], R.UU.at[at.z, at.p, at.c], dev, R.UU.at[at.z, there, at.c])
        for there, dev in ((at.px, at.xn), (at.py, at.yn), (at.pd, at.diag))
    ]
    d_z = ZGather(
        post,
        at,
        lambda zz: R.UD.at[zz, at.c],
        lambda zz: post.msg(R.UD.at[zz, at.c], R.UD.at[zz, at.c], at.core, R.UD.at[zz, 1 - at.c]),
    )
    u_z = ZGather(
        post,
        at,
        lambda zz: R.UU.at[zz, :, at.c],
        lambda zz: post.msg(R.UU.at[zz, :, at.c], R.UU.at[zz, :, at.c], at.core, R.UU.at[zz, :, 1 - at.c]),
    )
    cot = HalfGather(post, at, lambda x, y, h: R.CA.at[x * 2 + y, pl.ds(h * half_rows, half_rows)])

    first.start()
    first.plane[0].start()
    keys.plane[0].start()
    for m in up:
        m.start()

    def stats(g, carry):
        mean, rstd = normal(R.MED[g].astype(F32))
        R.MR[g, 0:per_media, 0:1] = mean
        R.MR[g, 0:per_media, 1:2] = rstd
        mean, rstd = normal(R.latents[g].astype(F32))
        R.MR[g, per_media:rows, 0:1] = mean
        R.MR[g, per_media:rows, 1:2] = rstd
        return carry

    media_in.wait()
    loop(images, stats)
    keys.start()
    first.into_plane()
    second.start()
    first.relay()
    keys.into_plane()
    third.start()
    first.to_core()
    d_z.start()
    keys.relay()
    first.arrived()

    for i in range(8):
        total = jnp.zeros((16, 128), F32)
        for p in (2 * (i % 2), 2 * (i % 2) + 1):
            for c in range(2):
                total = total + R.G[i // 2, p, c, 0:16, cols(GN)].astype(F32)
        R.VV[:, 128 * i : 128 * i + 128] = total

    latents = flat(R.latents[...]).astype(F32)
    normed = (latents - flat(R.MR[:, per_media:rows, 0:1])) * flat(R.MR[:, per_media:rows, 1:2])
    latent_low = (normed * R.VV[2:3, :] + R.VV[3:4, :]).astype(BF16)
    R.X[:, per_media:rows, :] = latent_low.reshape(images, per_lat, 1024)
    R.QA[at.l] = mm(latent_low, R.G[:, :, :, :, cols(QU)].reshape(1024, 512)).astype(BF16)
    q_all = LatGather(post, at, lambda l: R.QA.at[l])
    q_all.start()
    second.plane[0].mx.start()

    def low(g, carry):
        normed = (R.MED[g].astype(F32) - R.MR[g, 0:per_media, 0:1]) * R.MR[g, 0:per_media, 1:2]
        R.X[g, 0:per_media, :] = (normed * R.VV[0:1, :] + R.VV[1:2, :]).astype(BF16)
        return carry

    keys.to_core()
    loop(images, low)
    keys.arrived()

    def pairs(n, carry):
        weight = R.G[:, :, :, :, pl.ds(pl.multiple_of(KV[0] + n * 256, 128), 256)].reshape(1024, 256)
        made = mm(R.X[...].reshape(images * rows, 1024), weight).astype(BF16)
        R.PR[:, :, span256(n)] = made.reshape(images, rows, 256)
        return carry

    loop((0, 2), pairs)
    q_all.relay()
    second.along_z()
    second.plane[0].my.start()
    for g in second.plane[1:]:
        g.start()
    for m in up:
        m.arrived()
    u_z.start()
    d_z.far()
    q_all.last()

    mask = head_mask()

    def score(g, carry):
        limit = SHORT + (LONG - SHORT) * R.bucket[g] - at.l * per_media
        row = lax.broadcasted_iota(jnp.int32, (rows, 256), 0)
        valid = jnp.logical_or(row >= per_media, row < limit)
        for half in range(2):
            span = pl.ds(256 * half, 256)
            queries = spread_heads(R.QA[:, pl.ds(pl.multiple_of(g * per_lat, per_lat), per_lat), span], mask)
            raw = mm_nt(R.PR[g, :, span], queries) * SCALE
            raw = jnp.where(valid, raw, NEG)
            top = jnp.max(raw, axis=0, keepdims=True)
            total = jnp.sum(jnp.exp(raw - top), axis=0, keepdims=True)
            R.S[2 * g + half] = raw
            R.LS[at.l, pl.ds(2 * g + half, 1), :] = top + jnp.log(total)
        return carry

    loop(images, score)
    second.relay()
    ls = [
        post.msg(R.LS.at[at.l], R.LS.at[at.l], dev, R.LS.at[there])
        for there, dev in ((at.ly, at.yn), (at.ld, at.ycore), (at.lc, at.core))
    ]
    for m in ls:
        m.start()
    third.along_z()
    third.over_plane()
    second.to_core()
    second.arrived()
    loop((2, 4), pairs)
    third.relay()
    cot.start()
    cot.rest()
    u_z.far()
    for m in ls:
        m.arrived()
    top = jnp.maximum(jnp.maximum(R.LS[0], R.LS[1]), jnp.maximum(R.LS[2], R.LS[3]))
    total = jnp.exp(R.LS[0] - top)
    for l in range(1, 4):
        total = total + jnp.exp(R.LS[l] - top)
    R.LG[...] = top + jnp.log(total)

    def mix(g, carry):
        for half in range(2):
            probs = jnp.exp(R.S[2 * g + half] - R.LG[pl.ds(2 * g + half, 1), :]).astype(BF16)
            R.PB[2 * g + half] = probs
            wide = mm_tn(probs, R.PR[g, :, pl.ds(512 + 256 * half, 256)])
            R.OP[:, pl.ds(pl.multiple_of(g * per_lat, per_lat), per_lat), pl.ds(256 * half, 256)] = (
                gather_heads(wide).reshape(4, per_lat, 256).astype(BF16)
            )
        return carry

    loop(images, mix)
    mixed = LatReduce(post, at, R.OP, R.O1, R.O2)
    mixed.start()
    mixed.relay()
    third.to_core()
    cot.relay()
    third.arrived()
    R.MX[...] = mixed.total().astype(BF16)
    left = R.G[:, :, :, 0:16, cols(OUT)].reshape(512, 512)
    right = R.G[:, :, :, 16:32, cols(OUT)].reshape(512, 512)
    latents = flat(R.latents[...]).astype(F32)
    R.RES[:, 0:512] = latents[:, 0:512] + mm(R.MX[...], left)
    R.RES[:, 512:1024] = latents[:, 512:1024] + mm(R.MX[...], right)
    mean, rstd = normal(R.RES[...])
    R.MA[at.p] = ((R.RES[...] - mean) * rstd * R.VV[4:5, :] + R.VV[5:6, :]).astype(BF16)
    mlp = HalfGather(post, at, lambda x, y, h: R.MA.at[x * 2 + y, pl.ds(h * half_rows, half_rows)])
    mlp.start()
    mlp.rest()
    mlp.relay()
    cot.last()
    d_z.last()
    u_z.last()
    d_z.all()

    def cot_back(f, carry):
        made = mm_nt(R.CA[...].reshape(4 * tokens, 1024), R.UD[f].reshape(256, 1024))
        R.S[pl.ds(4 * f, 4), 0:tokens, :] = made.reshape(4, tokens, 256)
        return carry

    loop(4, cot_back)
    u_z.all()
    mlp.last()

    def gates(k, carry):
        f = pick(zs, k)
        gate = mm(R.MA[...].reshape(4 * tokens, 1024), R.UU[:, :, :, :, span256(f)].reshape(1024, 256))
        back = R.S[pl.ds(4 * f, 4), 0:tokens, :].reshape(4 * tokens, 256)
        phi = 0.5 * (1.0 + lax.erf(gate * 0.7071067811865476))
        R.ACT[:, :, span256(f)] = (gate * phi).astype(BF16).reshape(4, tokens, 256)
        slope = phi + gate * jnp.exp(-0.5 * gate * gate) * 0.3989422804014327
        R.GG[:, :, span256(f)] = (back * slope).astype(BF16).reshape(4, tokens, 256)
        return carry

    def norm_parts(n, carry):
        made = mm_nt(R.GG[...].reshape(4 * tokens, 1024), R.UU[n].reshape(256, 1024))
        R.PT[:, :, span256(n)] = made.astype(BF16).reshape(4, tokens, 256)
        return carry

    gd_c = [post.msg(R.gD.at[zz, 1 - at.c], R.RD.at[zz], at.core, R.RD.at[zz]) for zz in zs]
    gu_c = [post.msg(R.gU.at[zz, :, 1 - at.c], R.RU.at[zz], at.core, R.RU.at[zz]) for zz in zs]
    gd_z = ZReduce(post, at, lambda zz: R.RD.at[zz], lambda k: R.ZD.at[k])
    gu_z = ZReduce(post, at, lambda zz: R.RU.at[zz], lambda k: R.ZU.at[k])

    def down_grads(k, carry):
        f = pick(zs, k)
        act = R.ACT[:, :, span256(f)].reshape(4 * tokens, 256)
        R.gD[f] = mm_tn(act, R.CA[...].reshape(4 * tokens, 1024)).astype(BF16).reshape(2, 128, 1024)
        return carry

    def up_grads(k, carry):
        n = pick(zs, k)
        low_rows = R.MA[:, :, span256(n)].reshape(4 * tokens, 256)
        made = mm_tn(low_rows, R.GG[...].reshape(4 * tokens, 1024)).astype(BF16)
        R.gU[n] = made.reshape(4, 2, 32, 1024)
        return carry

    def add_d(k):
        gd_c[k].arrived()
        R.RD[zs[k]] = (R.RD[zs[k]].astype(F32) + R.gD[zs[k], at.c].astype(F32)).astype(BF16)

    def add_u(k):
        gu_c[k].arrived()
        R.RU[zs[k]] = (R.RU[zs[k]].astype(F32) + R.gU[zs[k], :, at.c].astype(F32)).astype(BF16)

    loop((3, 4), gates)
    loop((3, 4), down_grads)
    gd_c[3].start()
    loop((0, 3), gates)
    loop((3, 4), up_grads)
    gu_c[3].start()
    add_d(3)
    gd_z.start_last()
    loop(4, norm_parts)
    back = PlaneReduce(
        post,
        at,
        lambda x, y, h: R.PT.at[x * 2 + y, pl.ds(h * half_rows, half_rows)],
        lambda k: R.PY.at[0, k],
        lambda k: R.PX.at[0, k],
        lambda k: R.P2.at[0, k],
    )
    back.start()

    add_u(3)
    gu_z.start_last()
    loop((2, 3), down_grads)
    gd_c[2].start()
    loop((2, 3), up_grads)
    gu_c[2].start()
    back.rest()
    loop((0, 2), down_grads)
    gd_c[1].start()
    gd_c[0].start()
    add_d(2)
    gd_z.start_far()
    add_u(2)
    gu_z.start_far()
    back.relay()
    loop((0, 2), up_grads)
    gu_c[1].start()
    gu_c[0].start()
    add_d(1)
    gd_z.start_near()
    add_d(0)

    def out_parts(n, carry):
        made = mm(R.ACT[...].reshape(4 * tokens, 1024), R.UD[:, :, :, span256(n)].reshape(1024, 256))
        R.GG[:, :, span256(n)] = made.astype(BF16).reshape(4, tokens, 256)
        return carry

    loop(4, out_parts)
    add_u(1)
    gu_z.start_near()
    add_u(0)

    out = PlaneReduce(
        post,
        at,
        lambda x, y, h: R.GG.at[x * 2 + y, pl.ds(h * half_rows, half_rows)],
        lambda k: R.PY.at[1, k],
        lambda k: R.PX.at[1, k],
        lambda k: R.P2.at[1, k],
    )
    low_part, high_part = back.total()
    R.U[0:half_rows] = low_part
    R.U[half_rows:] = high_part

    mean, rstd = normal(R.RES[...])
    normed = (R.RES[...] - mean) * rstd
    upstream = R.U[...]
    R.GR[...] = flat(R.cotangent[...]).astype(F32) + norm_back(upstream, normed, rstd, R.VV[4:5, :])
    R.GS[...] = jnp.zeros_like(R.GS)
    R.GS[4:5, :] = jnp.sum(upstream * normed, axis=0, keepdims=True)
    R.GS[5:6, :] = jnp.sum(upstream, axis=0, keepdims=True)
    grad_attn = R.GR[...].astype(BF16)
    left = R.G[:, :, :, 0:16, cols(OUT)].reshape(512, 512)
    right = R.G[:, :, :, 16:32, cols(OUT)].reshape(512, 512)
    R.GM[at.l] = (mm_nt(grad_attn[:, 0:512], left) + mm_nt(grad_attn[:, 512:1024], right)).astype(BF16)
    gm = LatGather(post, at, lambda l: R.GM.at[l])
    gm.start()
    out.mx1.start()
    out.mx0.start()
    grad_attn = R.GR[...].astype(BF16)
    made = mm_tn(R.MX[...], grad_attn[:, 0:512]).astype(BF16)
    R.gA[:, :, :, 0:16, cols(GOUT)] = made.reshape(4, 4, 2, 16, 512)
    made = mm_tn(R.MX[...], grad_attn[:, 512:1024]).astype(BF16)
    R.gA[:, :, :, 16:32, cols(GOUT)] = made.reshape(4, 4, 2, 16, 512)
    w_out = Collect(post, at, R.gA, R.RA, R.WY, R.WX, R.W2, R.ZW, GOUT, OUT)
    w_out.start()
    gm.relay()
    gm.last()
    out.my1.start()
    out.my0.start()

    def grad_probs(g, carry):
        lat_rows = pl.ds(pl.multiple_of(g * per_lat, per_lat), per_lat)
        for half in range(2):
            upper = pl.ds(512 + 256 * half, 256)
            wide = spread_heads(R.GM[:, lat_rows, pl.ds(256 * half, 256)], mask)
            made = mm_nt(R.PR[g, :, upper], wide)
            probs = R.PB[2 * g + half]
            R.S[2 * g + half] = made
            R.DL[at.l, pl.ds(2 * g + half, 1), :] = jnp.sum(probs.astype(F32) * made, axis=0, keepdims=True)
            R.gP[g, :, upper] = mm(probs, wide).astype(BF16)
        return carry

    loop(images, grad_probs)
    dl = [
        post.msg(R.DL.at[at.l], R.DL.at[at.l], dev, R.DL.at[there])
        for there, dev in ((at.ly, at.yn), (at.ld, at.ycore), (at.lc, at.core))
    ]
    for m in dl:
        m.start()
    w_out.into_plane()

    def kv_grads(n, carry):
        low_rows = R.X[:, :, span256(lax.rem(n, 4))].reshape(images * rows, 256)
        lanes = pl.ds(pl.multiple_of(lax.div(n, 4) * 512, 512), 512)
        made = mm_tn(low_rows, R.gP[:, :, lanes].reshape(images * rows, 512)).astype(BF16)
        R.gU[lax.rem(n, 4), :, :, :, lanes] = made.reshape(4, 2, 32, 512)
        return carry

    for m in gu_c:
        m.sent()
    loop((4, 8), kv_grads)
    w_val = Collect(post, at, R.gU, R.RK, R.WY, R.WX, R.W2, R.ZW, (512, 512), VAL)
    w_val.start()
    gd_z.relay()
    gu_z.relay()
    out.relay()
    for m in dl:
        m.arrived()
    R.LG[...] = R.DL[0] + R.DL[1] + R.DL[2] + R.DL[3]

    def grad_scores(g, carry):
        lat_rows = pl.ds(pl.multiple_of(g * per_lat, per_lat), per_lat)
        for half in range(2):
            span = pl.ds(256 * half, 256)
            grads = R.PB[2 * g + half].astype(F32) * (R.S[2 * g + half] - R.LG[pl.ds(2 * g + half, 1), :])
            grads = grads.astype(BF16)
            wide = mm_tn(grads, R.PR[g, :, span]) * SCALE
            R.QP[:, lat_rows, span] = gather_heads(wide).reshape(4, per_lat, 256).astype(BF16)
            queries = spread_heads(R.QA[:, lat_rows, span], mask)
            R.gP[g, :, span] = (mm(grads, queries) * SCALE).astype(BF16)
        return carry

    loop(images, grad_scores)
    gq = LatReduce(post, at, R.QP, R.Q1, R.Q2)
    gq.start()
    w_out.relay()
    w_val.into_plane()
    loop((0, 4), kv_grads)
    w_key = Collect(post, at, R.gU, R.RK, R.WY, R.WX, R.W2, R.ZW, (0, 512), KEY)
    w_key.start()
    gq.relay()

    def media_copy(h):
        return pltpu.make_async_copy(R.MG, R.grad_media.at[pl.ds(h * 2, 2)], R.local.at[0])

    def media_grads(h, carry):
        span = pl.ds(h * 2, 2)
        weight = R.G[:, :, :, :, cols(KV)].reshape(1024, 1024)
        upstream = mm_nt(R.gP[span].reshape(2 * rows, 1024), weight).reshape(2, rows, 1024)
        R.U[pl.ds(h * 2 * per_lat, 2 * per_lat)] = upstream[:, per_media:rows, :].reshape(2 * per_lat, 1024)
        upstream = upstream[:, 0:per_media, :]
        rstd = R.MR[span, 0:per_media, 1:2]
        normed = (R.MED[span].astype(F32) - R.MR[span, 0:per_media, 0:1]) * rstd
        made = norm_back(upstream, normed, rstd, R.VV[0:1, :]).astype(R.MG.dtype)
        pl.when(h >= 1)(lambda: media_copy(h - 1).wait())
        R.MG[...] = made
        media_copy(h).start()
        R.GS[0:1, :] += jnp.sum(flat(upstream * normed), axis=0, keepdims=True)
        R.GS[1:2, :] += jnp.sum(flat(upstream), axis=0, keepdims=True)
        return carry

    loop((0, 1), media_grads)
    w_key.into_plane()
    loop((1, 2), media_grads)
    w_val.relay()
    w_out.into_z()
    loop((2, 3), media_grads)
    with jax.named_scope("query"):
        grad_query = gq.total().astype(BF16)
        latent_low = flat(R.X[:, per_media:rows, :])
        R.gA[:, :, :, :, cols(QU)] = mm_tn(latent_low, grad_query).astype(BF16).reshape(4, 4, 2, 32, 512)
        R.GQ[...] = grad_query
    w_que = Collect(post, at, R.gA, R.RA, R.WY, R.WX, R.W2, R.ZW, QU, QU)
    w_que.start()
    loop((3, 4), media_grads)
    w_key.relay()
    w_que.into_plane()
    media_copy(images // 2 - 1).wait()

    upstream = R.U[...] + mm_nt(R.GQ[...], R.G[:, :, :, :, cols(QU)].reshape(1024, 512))
    rstd = flat(R.MR[:, per_media:rows, 1:2])
    normed = (flat(R.latents[...]).astype(F32) - flat(R.MR[:, per_media:rows, 0:1])) * rstd
    R.GS[2:3, :] = jnp.sum(upstream * normed, axis=0, keepdims=True)
    R.GS[3:4, :] = jnp.sum(upstream, axis=0, keepdims=True)
    for i in range(8):
        piece = R.GS[:, 128 * i : 128 * i + 128].astype(BF16)
        for p in (2 * (i % 2), 2 * (i % 2) + 1):
            for c in range(2):
                R.gA[i // 2, p, c, 0:16, cols(GN)] = piece
                R.gA[i // 2, p, c, 16:32, cols(GN)] = jnp.zeros((16, 128), BF16)
    w_nrm = CollectNorms(post, at, R.gA, R.RA, R.WY, R.WX, R.W2, R.ZW, GN)
    w_nrm.start()
    w_que.relay()
    with jax.named_scope('T_w_val_into_z'):
        w_val.into_z()
    w_nrm.into_plane()
    with jax.named_scope('T_w_key_into_z'):
        w_key.into_z()
    R.grad_latents[...] = (R.GR[...] + norm_back(upstream, normed, rstd, R.VV[2:3, :])).reshape(
        images, per_lat, 1024
    )
    with jax.named_scope('T_gd_z_total'):
        gd_z.total(R.grad_down)
    gu_z.total(R.SF)
    R.SU[...] = R.SF[...].astype(BF16)
    R.AU[at.p] = R.SU[at.p]
    up = [
        post.msg(R.SU.at[there], R.AU.at[at.p], dev, R.AU.at[there])
        for there, dev in ((at.px, at.xn), (at.py, at.yn), (at.pd, at.diag))
    ]
    for m in up:
        m.start()
    with jax.named_scope('T_w_nrm_into_z'):
        w_nrm.into_z()
    low_part, high_part = out.total()
    R.latents_out[...] = jnp.concatenate(
        [R.RES[0:half_rows] + low_part, R.RES[half_rows:] + high_part], axis=0
    ).astype(BF16).reshape(images, per_lat, 1024)
    with jax.named_scope('T_w_que_into_z'):
        w_que.into_z()
    with jax.named_scope('T_w_out_total'):
        w_out.total(R.grad_pack.at[:, cols(OUT)])
    with jax.named_scope('T_w_val_total'):
        w_val.total(R.grad_pack.at[:, cols(VAL)])
    with jax.named_scope('T_w_key_total'):
        w_key.total(R.grad_pack.at[:, cols(KEY)])
    with jax.named_scope('T_w_nrm_total'):
        w_nrm.total(R.grad_pack.at[0:16, cols(GN)])
    for m in up:
        m.arrived()
    for p in range(4):
        for zz in range(4):
            for cc in range(2):
                R.grad_up[:, 128 * (8 * zz + 2 * p + cc) : 128 * (8 * zz + 2 * p + cc) + 128] = R.AU[
                    p, :, 128 * (2 * zz + cc) : 128 * (2 * zz + cc) + 128
                ].astype(F32)
    with jax.named_scope('T_w_que_total'):
        w_que.total(R.grad_pack.at[:, cols(QU)])


def loop(bounds, step):
    first, last = bounds if isinstance(bounds, tuple) else (0, bounds)
    with jax.named_scope(step.__name__):
        lax.fori_loop(first, last, step, 0)


PLACES = {"bucket": pltpu.SMEM, "media": pl.ANY, "grad_media": pl.ANY}


class Refs:
    def __init__(self, names, refs):
        for name, ref in zip(names, refs):
            setattr(self, name, ref)


def build(kernel_body, inputs, outputs, scratch, messages, cid, name):
    in_names = [n for n, _ in inputs]
    out_names = [n for n, _, _ in outputs]
    scratch_names = [n for n, _, _ in scratch]

    def kernel(*refs):
        R = Refs(in_names + out_names + scratch_names, refs)
        at = Place()
        R.local = refs[-3]
        post = Post(refs[-2], refs[-1])
        kernel_body(at, post, R)
        post.drain()
        assert post.count <= messages, post.count

    specs = [
        pl.BlockSpec(memory_space=PLACES.get(n, pltpu.VMEM)) for n in in_names
    ]
    return pl.pallas_call(
        kernel,
        out_shape=[jax.ShapeDtypeStruct(s, d) for _, s, d in outputs],
        in_specs=specs,
        out_specs=[
            pl.BlockSpec(memory_space=PLACES.get(n, pltpu.VMEM)) for n, _, _ in outputs
        ],
        scratch_shapes=[pltpu.VMEM(s, d) for _, s, d in scratch]
        + [pltpu.SemaphoreType.DMA((2,)), pltpu.SemaphoreType.DMA((messages,)), pltpu.SemaphoreType.DMA((messages,))],
        compiler_params=pltpu.CompilerParams(
            collective_id=cid, has_side_effects=True, vmem_limit_bytes=62 << 20
        ),
        name=name,
    )(*[v for _, v in inputs])


def layer(media, latents, bucket, cotangent, n0, n1, n2, n3, n4, n5, w_query, w_keyvalue, w_output, w_up, w_down):
    images, per_media, _ = media.shape
    per_lat = latents.shape[1]
    rows = per_media + per_lat
    tokens = images * per_lat
    inputs = [
        ("media", media),
        ("latents", latents),
        ("cotangent", cotangent),
        ("bucket", bucket),
        ("n0", n0),
        ("n1", n1),
        ("n2", n2),
        ("n3", n3),
        ("n4", n4),
        ("n5", n5),
        ("w_query", w_query),
        ("w_keyvalue", w_keyvalue),
        ("w_output", w_output),
        ("w_up", w_up),
        ("w_down", w_down),
    ]
    outputs = [
        ("latents_out", (images, per_lat, 1024), BF16),
        ("grad_media", (images, per_media, 1024), BF16),
        ("grad_latents", (images, per_lat, 1024), F32),
        ("grad_pack", (32, WIDE), F32),
        ("grad_up", (32, 4096), F32),
        ("grad_down", (128, 1024), F32),
    ]
    scratch = [
        ("MED", (images, per_media, 1024), BF16),
        ("X", (images, rows, 1024), BF16),
        ("MR", (images, rows, 2), F32),
        ("PR", (images, rows, 1024), BF16),
        ("S", (2 * images, rows, 256), F32),
        ("PB", (2 * images, rows, 256), BF16),
        ("QA", (4, tokens, 512), BF16),
        ("MX", (tokens, 512), BF16),
        ("RES", (tokens, 1024), F32),
        ("MA", (4, tokens, 1024), BF16),
        ("CA", (4, tokens, 1024), BF16),
        ("UD", (4, 2, 128, 1024), BF16),
        ("UU", (4, 4, 2, 32, 1024), BF16),
        ("G", (4, 4, 2, 32, WIDE), BF16),
        ("VV", (16, 1024), F32),
        ("WS", (4, 32, 1024), BF16),
        ("LS", (4, 2 * images, 256), F32),
        ("LG", (2 * images, 256), F32),
        ("OP", (4, tokens, 512), BF16),
        ("O1", (2, tokens, 512), BF16),
        ("O2", (tokens, 512), BF16),
        ("MG", (2, per_media, 1024), BF16),
        ("ACT", (4, tokens, 1024), BF16),
        ("GG", (4, tokens, 1024), BF16),
        ("PT", (4, tokens, 1024), BF16),
        ("PY", (2, 2, tokens // 2, 1024), BF16),
        ("PX", (2, 2, tokens // 2, 1024), BF16),
        ("P2", (2, 2, tokens // 2, 1024), BF16),
        ("gD", (4, 2, 128, 1024), BF16),
        ("gU", (4, 4, 2, 32, 1024), BF16),
        ("RD", (4, 128, 1024), BF16),
        ("RU", (4, 4, 32, 1024), BF16),
        ("ZD", (4, 128, 1024), BF16),
        ("ZU", (4, 4, 32, 1024), BF16),
        ("U", (tokens, 1024), F32),
        ("GR", (tokens, 1024), F32),
        ("GS", (16, 1024), F32),
        ("GM", (4, tokens, 512), BF16),
        ("gP", (images, rows, 1024), BF16),
        ("DL", (4, 2 * images, 256), F32),
        ("QP", (4, tokens, 512), BF16),
        ("Q1", (2, tokens, 512), BF16),
        ("Q2", (tokens, 512), BF16),
        ("GQ", (tokens, 512), BF16),
        ("gA", (4, 4, 2, 32, NARROW), BF16),
        ("RA", (4, 4, 32, NARROW), BF16),
        ("RK", (4, 4, 32, 1024), BF16),
        ("WY", (2, 4, 16, WIDE), BF16),
        ("WX", (2, 4, 16, WIDE), BF16),
        ("W2", (2, 4, 16, WIDE), BF16),
        ("ZW", (3, 32, WIDE), BF16),
        ("SF", (4, 32, 1024), F32),
        ("SU", (4, 32, 1024), BF16),
        ("AU", (4, 32, 1024), BF16),
    ]
    return build(kernel_body, inputs, outputs, scratch, MESSAGES, 1, "resampler")


def finish_body(
    out_in, media_in, latents_in, pack, up_in, down_in, out, media, latents, n0, n1, n2, n3, n4, n5, wq, wkv, wo, wu, wd
):
    rows = wo.shape[0]
    media[...] = media_in[...].astype(F32)

    @pl.when(pl.program_id(0) == 0)
    def _():
        out[...] = out_in[...]
        latents[...] = latents_in[...]
        wu[...] = up_in[...]
        wd[...] = down_in[...]
        wq[...] = pack[:, cols(QU)]
        wkv[...] = pack[:, cols(KV)]
        wo[:, 0:512] = pack[0:rows, cols(OUT)]
        wo[:, 512:1024] = pack[rows : 2 * rows, cols(OUT)]
        mine = pltpu.roll(pack[0:8, cols(GN)], lax.rem(128 - 32 * lax.axis_index("lat"), 128), 1)
        for k, ref in enumerate((n0, n1, n2, n3, n4, n5)):
            ref[...] = mine[k, 0:32]


def finish(latents_out, grad_media, grad_latents, grad_pack, grad_up, grad_down):
    images, per_media, width = grad_media.shape
    block = pl.BlockSpec((2, per_media, width), lambda g: (g, 0, 0))

    def whole(shape):
        return pl.BlockSpec(shape, lambda g: (0,) * len(shape))

    shapes = [
        jax.ShapeDtypeStruct(latents_out.shape, BF16),
        jax.ShapeDtypeStruct(grad_media.shape, F32),
        jax.ShapeDtypeStruct(grad_latents.shape, F32),
    ] + [
        jax.ShapeDtypeStruct(shape, F32)
        for shape in ((32,),) * 6 + ((32, 512), (32, 1024), (16, 1024), grad_up.shape, grad_down.shape)
    ]
    values = (latents_out, grad_media, grad_latents, grad_pack, grad_up, grad_down)
    return pl.pallas_call(
        finish_body,
        grid=(images // 2,),
        out_shape=shapes,
        in_specs=[block if k == 1 else whole(v.shape) for k, v in enumerate(values)],
        out_specs=[block if k == 1 else whole(v.shape) for k, v in enumerate(shapes)],
        name="finish",
    )(*values)


def solution(mesh):
    sizes = dict(mesh.shape)
    blocks = sizes["img"] // BLOCK
    names = ("img", "lat")

    def block_shard(weight):
        if blocks == 1:
            return weight
        whole = lax.all_gather(weight, names, axis=0, tiled=True)
        each = whole.shape[0] // (BLOCK * sizes["lat"])
        mine = lax.rem(lax.axis_index("img"), BLOCK) * sizes["lat"] + lax.axis_index("lat")
        return lax.dynamic_slice_in_dim(whole, mine * each, each, 0)

    def own_shard(gradient):
        if blocks == 1:
            return gradient
        each = gradient.shape[0]
        mine = lax.rem(lax.axis_index("img"), BLOCK) * sizes["lat"] + lax.axis_index("lat")
        whole = jnp.zeros((each * BLOCK * sizes["lat"],) + gradient.shape[1:], gradient.dtype)
        whole = lax.dynamic_update_slice_in_dim(whole, gradient, mine * each, 0)
        return lax.psum_scatter(whole, names, scatter_dimension=0, tiled=True)

    def on_device(
        media,
        latents,
        bucket,
        gain_media,
        shift_media,
        gain_latent,
        shift_latent,
        gain_mlp,
        shift_mlp,
        w_query,
        w_keyvalue,
        w_output,
        w_up,
        w_down,
        cotangent,
    ):
        norms = (gain_media, shift_media, gain_latent, shift_latent, gain_mlp, shift_mlp)
        weights = (w_query, w_keyvalue, w_output, w_up, w_down)
        made = layer(media, latents, bucket, cotangent, *[block_shard(v) for v in norms + weights])
        made = finish(*made)
        return (*made[:3], *[own_shard(v) for v in made[3:]])

    rows = P("img", "lat", None)
    shard = P(names)
    wide = P(names, None)
    return jax.shard_map(
        on_device,
        mesh=mesh,
        in_specs=(rows, rows, P("img")) + (shard,) * 6 + (wide,) * 5 + (rows,),
        out_specs=(rows, rows, rows) + (shard,) * 6 + (wide,) * 5,
        check_vma=False,
    )
```

```python
import jax
import jax.numpy as jnp
from jax import lax
from jax.experimental import pallas as pl
from jax.experimental.pallas import tpu as pltpu
from jax.sharding import PartitionSpec as P

MESH = pl.DeviceIdType.MESH
BF16 = jnp.bfloat16
F32 = jnp.float32

SHORT = 256
LONG = 576
HEADS = 8
EPS = 1e-05
SCALE = 0.125
NEG = -1e30

BLOCK = 8

QU = (0, 512)
GN = (512, 128)
KEY = (640, 512)
VAL = (1152, 512)
KV = (640, 1024)
OUT = (1664, 512)
WIDE = 2176
GOUT = (640, 512)
NARROW = 1152
MESSAGES = (106, 132)


def mm(a, b):
    return lax.dot_general(a, b, (((1,), (0,)), ((), ())), preferred_element_type=F32)


def mm_nt(a, b):
    return lax.dot_general(a, b, (((1,), (1,)), ((), ())), preferred_element_type=F32)


def mm_tn(a, b):
    return lax.dot_general(a, b, (((0,), (0,)), ((), ())), preferred_element_type=F32)


def cols(span):
    return pl.ds(span[0], span[1])


def flat(values):
    return values.reshape(-1, values.shape[-1])


def normal(values):
    mean = jnp.mean(values, axis=-1, keepdims=True)
    centred = values - mean
    spread = jnp.mean(centred * centred, axis=-1, keepdims=True)
    return mean, lax.rsqrt(spread + EPS)


def norm_back(upstream, normed, rstd, gain):
    scaled = upstream * gain
    first = jnp.mean(scaled, axis=-1, keepdims=True)
    second = jnp.mean(scaled * normed, axis=-1, keepdims=True)
    return (scaled - first - normed * second) * rstd


class Place:
    def __init__(self):
        img = lax.axis_index("img")
        lat = lax.axis_index("lat")
        self.i = lax.rem(img, BLOCK)
        self.base = img - self.i
        self.z = lax.div(self.i, 2)
        self.x = lax.rem(self.i, 2)
        self.l = lat
        self.y = lax.div(lat, 2)
        self.c = lax.rem(lat, 2)
        self.z1 = self.z + 1 - 2 * lax.rem(self.z, 2)
        self.z2 = lax.rem(self.z + 2, 4)
        self.z3 = 3 - self.z
        self.mid = jnp.logical_or(self.z == 1, self.z == 2)
        self.zs = (self.z, self.z1, self.z2, self.z3)
        self.end = jnp.logical_or(self.z == 0, self.z == 3)
        self.p = self.x * 2 + self.y
        self.q = self.z * 4 + self.p
        self.px = (1 - self.x) * 2 + self.y
        self.py = self.x * 2 + 1 - self.y
        self.pd = 3 - self.p
        self.lc = self.y * 2 + 1 - self.c
        self.ly = (1 - self.y) * 2 + self.c
        self.ld = 3 - self.l
        self.core = self.dev(self.z, self.x, self.y, 1 - self.c)
        self.xn = self.dev(self.z, 1 - self.x, self.y, self.c)
        self.yn = self.dev(self.z, self.x, 1 - self.y, self.c)
        self.diag = self.dev(self.z, 1 - self.x, 1 - self.y, self.c)
        self.ycore = self.dev(self.z, self.x, 1 - self.y, 1 - self.c)
        self.zn1 = self.dev(self.z1, self.x, self.y, self.c)
        self.zn2 = self.dev(self.z2, self.x, self.y, self.c)
        self.zn3 = self.dev(self.z3, self.x, self.y, self.c)

    def dev(self, z, x, y, c):
        return (self.base + z * 2 + x, y * 2 + c)

    def greet(self):
        barrier = pltpu.get_barrier_semaphore()
        peers = (self.core, self.xn, self.yn, self.diag, self.ycore, self.zn1, self.zn2, self.zn3)
        for peer in peers:
            pl.semaphore_signal(barrier, inc=1, device_id=peer, device_id_type=MESH)
        pl.semaphore_wait(barrier, len(peers))


def guarded(when, action):
    if when is None:
        action()
    else:
        pl.when(when)(action)


class Msg:
    def __init__(self, post, src, dst, dev, into, key=None, when=None):
        self.k = post.sends
        post.sends += 1
        self.key = post.key() if key is None else key
        self.when = when
        self.post, self.src, self.dst, self.dev, self.into = post, src, dst, dev, into
        self.done = False
        post.group.append(self)

    def copy(self, src, dst):
        return pltpu.make_async_remote_copy(
            src_ref=src,
            dst_ref=dst,
            send_sem=self.post.send.at[self.k],
            recv_sem=self.post.recv.at[self.key],
            device_id=self.dev,
            device_id_type=MESH,
        )

    def start(self):
        guarded(self.when, lambda: self.copy(self.src, self.dst).start())

    def arrived(self):
        self.copy(self.into, self.into).wait_recv()

    def sent(self):
        if self.done:
            return
        self.done = True
        guarded(self.when, lambda: self.copy(self.src, self.dst).wait_send())


class Post:
    def __init__(self, send, recv):
        self.send, self.recv = send, recv
        self.sends = self.most = self.keys = 0
        self.group, self.spare = [], []

    def key(self):
        if self.spare:
            return self.spare.pop(0)
        self.keys += 1
        return self.keys - 1

    def msg(self, *a, **k):
        return Msg(self, *a, **k)

    def recycle(self):
        group, self.group = self.group, []
        self.most, self.sends = max(self.most, self.sends), 0
        return group

    def drain(self):
        for m in self.recycle():
            m.sent()


class ZGather:
    def __init__(self, post, at, view, core):
        own = view(at.z)
        self.at = at
        self.m1 = post.msg(own, own, at.zn1, view(at.z1))
        self.m2 = post.msg(own, own, at.zn2, view(at.z2))
        self.m3 = post.msg(own, own, at.zn3, view(at.z3), when=at.mid)
        self.relay = post.msg(view(at.z2), view(at.z2), at.zn1, view(at.z3), key=self.m3.key, when=at.mid)
        early = jnp.where(at.mid, at.z2, at.z1)
        late = jnp.where(at.mid, at.z1, at.z2)
        self.core = [core(zz) for zz in (at.z, early, late, at.z3)]

    def start(self):
        pl.when(self.at.mid)(self.m1.start)
        pl.when(self.at.end)(self.m2.start)
        self.core[0].start()

    def far(self):
        @pl.when(self.at.mid)
        def _():
            self.m2.arrived()
            self.relay.start()
            self.m3.start()
            self.m2.start()

        pl.when(self.at.end)(self.m1.start)

    def early(self):
        pl.when(self.at.end)(self.m1.arrived)
        self.core[1].start()

    def last(self):
        pl.when(self.at.mid)(self.m1.arrived)
        pl.when(self.at.end)(self.m2.arrived)
        self.core[2].start()
        self.m3.arrived()
        self.core[3].start()

    def all(self):
        for m in self.core:
            m.arrived()


class PlaneGather:
    def __init__(self, post, at, view, half):
        own = view(at.x, at.y)
        ox, oy = 1 - at.x, 1 - at.y
        self.mx = post.msg(own, own, at.xn, view(ox, at.y))
        self.my = post.msg(own, own, at.yn, view(at.x, oy))
        self.hy = post.msg(half(ox, at.y, 0), half(ox, at.y, 0), at.yn, half(ox, oy, 0))
        self.hx = post.msg(half(at.x, oy, 1), half(at.x, oy, 1), at.xn, half(ox, oy, 1))

    def start(self):
        self.mx.start()
        self.my.start()

    def relay(self):
        self.mx.arrived()
        self.hy.start()
        self.my.arrived()
        self.hx.start()

    def last(self):
        self.hy.arrived()
        self.hx.arrived()


class HalfGather:
    def __init__(self, post, at, half):
        x, y = at.x, at.y
        ox, oy = 1 - x, 1 - y

        def msg(part, dev, into):
            return post.msg(part, part, dev, into)

        self.x0 = msg(half(x, y, 0), at.xn, half(ox, y, 0))
        self.y1 = msg(half(x, y, 1), at.yn, half(x, oy, 1))
        self.x1 = msg(half(x, y, 1), at.xn, half(ox, y, 1))
        self.y0 = msg(half(x, y, 0), at.yn, half(x, oy, 0))
        self.hy = msg(half(ox, y, 0), at.yn, half(ox, oy, 0))
        self.hx = msg(half(x, oy, 1), at.xn, half(ox, oy, 1))

    def start(self):
        self.x0.start()
        self.y1.start()

    def relay0(self):
        self.x0.arrived()
        self.hy.start()

    def relay1(self):
        self.y1.arrived()
        self.hx.start()

    def relay(self):
        self.relay0()
        self.relay1()

    def rest(self):
        self.y0.start()
        self.x1.start()

    def last0(self):
        self.y0.arrived()
        self.hy.arrived()

    def last1(self):
        self.x1.arrived()
        self.hx.arrived()

    def last(self):
        self.last0()
        self.last1()


class Spread:
    def __init__(self, post, at, G, span):
        lanes = cols(span)

        def view(zz, x, y):
            return G.at[zz, x * 2 + y, at.c, :, lanes]

        def half(zz, x, y, h):
            return G.at[zz, x * 2 + y, at.c, pl.ds(16 * h, 16), lanes]

        own = view(at.z, at.x, at.y)
        self.z = [
            post.msg(own, own, dev, view(zz, at.x, at.y))
            for zz, dev in ((at.z1, at.zn1), (at.z2, at.zn2), (at.z3, at.zn3))
        ]
        self.plane = [
            PlaneGather(
                post, at, lambda x, y, zz=zz: view(zz, x, y), lambda x, y, h, zz=zz: half(zz, x, y, h)
            )
            for zz in at.zs
        ]
        self.core = [
            post.msg(
                G.at[zz, :, at.c, :, lanes], G.at[zz, :, at.c, :, lanes], at.core, G.at[zz, :, 1 - at.c, :, lanes]
            )
            for zz in at.zs
        ]

    def start(self):
        for m in self.z:
            m.start()

    def into_plane(self):
        for k in range(3):
            self.z[k].arrived()
            self.plane[k + 1].start()

    def relay(self):
        for g in self.plane:
            g.relay()

    def to_core(self):
        for g, m in zip(self.plane, self.core):
            g.last()
            m.start()

    def arrived(self):
        for m in self.core:
            m.arrived()


class SpreadWide:
    def __init__(self, post, at, G, span, along_x):
        lanes = cols(span)

        def block(zz):
            return G.at[zz, at.p, at.c, :, lanes]

        def column(p):
            return G.at[:, p, at.c, :, lanes]

        own = block(at.z)
        self.z = [
            post.msg(own, own, dev, block(zz))
            for zz, dev in ((at.z1, at.zn1), (at.z2, at.zn2), (at.z3, at.zn3))
        ]
        near, far = ((at.px, at.xn), (at.py, at.yn)) if along_x else ((at.py, at.yn), (at.px, at.xn))
        self.one = post.msg(column(at.p), column(at.p), near[1], column(near[0]))
        self.two = post.msg(column(at.p), column(at.p), far[1], column(far[0]))
        self.on = post.msg(column(near[0]), column(near[0]), far[1], column(at.pd))
        self.core = post.msg(
            G.at[:, :, at.c, :, lanes], G.at[:, :, at.c, :, lanes], at.core, G.at[:, :, 1 - at.c, :, lanes]
        )

    def start(self):
        for m in self.z:
            m.start()

    def along_z(self):
        for m in self.z:
            m.arrived()

    def relay(self):
        self.one.arrived()
        self.on.start()

    def to_core(self):
        self.two.arrived()
        self.on.arrived()
        self.core.start()

    def arrived(self):
        self.core.arrived()


class LatGather:
    def __init__(self, post, at, view):
        self.mc = post.msg(view(at.l), view(at.l), at.core, view(at.lc))
        self.my = post.msg(view(at.l), view(at.l), at.yn, view(at.ly))
        self.fc = post.msg(view(at.ly), view(at.ly), at.core, view(at.ld))

    def start(self):
        self.my.start()
        self.mc.start()

    def relay(self):
        self.my.arrived()
        self.fc.start()

    def last(self):
        self.mc.arrived()
        self.fc.arrived()


class LatReduce:
    def __init__(self, post, at, parts, first, second):
        self.at, self.parts, self.first, self.second = at, parts, first, second
        self.m0 = post.msg(parts.at[at.lc], first.at[0], at.core, first.at[0])
        self.m1 = post.msg(parts.at[at.ld], first.at[1], at.core, first.at[1])
        self.m2 = post.msg(parts.at[at.ly], second, at.yn, second)

    def start(self):
        self.m1.start()
        self.m0.start()

    def relay(self):
        self.m1.arrived()
        ly = self.at.ly
        self.parts[ly] = (self.parts[ly].astype(F32) + self.first[1].astype(F32)).astype(BF16)
        self.m2.start()

    def total(self):
        self.m0.arrived()
        self.m2.arrived()
        near = self.parts[self.at.l].astype(F32) + self.first[0].astype(F32)
        return near + self.second[...].astype(F32)


class HalfReduce:
    def __init__(self, post, at, half, part, near, other, last):
        x, y = at.x, at.y
        ox, oy = 1 - x, 1 - y
        self.near, self.other, self.end = near, other, last
        self.own = part(x, y)
        first, second = (at.yn, at.xn) if half == 0 else (at.xn, at.yn)
        self.there = part(ox, y) if half == 0 else part(x, oy)
        beside = part(x, oy) if half == 0 else part(ox, y)
        self.m1 = post.msg(part(ox, oy), other, first, other)
        self.m0 = post.msg(beside, near, first, near)
        self.f = post.msg(self.there, last, second, last)

    def start(self):
        self.m1.start()
        self.m0.start()

    def relay(self):
        self.m1.arrived()
        self.there[...] = (self.there[...].astype(F32) + self.other[...].astype(F32)).astype(BF16)
        self.f.start()

    def total(self):
        self.m0.arrived()
        self.f.arrived()
        return self.own[...].astype(F32) + self.near[...].astype(F32) + self.end[...].astype(F32)


class PlaneReduceX:
    def __init__(self, post, at, part, mine, other, last, pieces):
        ox, oy = 1 - at.x, 1 - at.y
        self.mine, self.other, self.end = mine, other, last
        self.own, self.there = part(at.x, at.y), part(at.x, oy)
        self.m1 = post.msg(part(ox, oy), other, at.xn, other)
        self.m0 = post.msg(part(ox, at.y), mine, at.xn, mine)
        size = self.there.shape[0] // pieces
        self.f = []
        for k in range(pieces):
            piece = last.at[pl.ds(k * size, size)]
            self.f.append(post.msg(self.there.at[pl.ds(k * size, size)], piece, at.yn, piece))

    def start(self):
        self.m1.start()
        self.m0.start()

    def relay(self):
        self.m1.arrived()
        self.there[...] = (self.there[...].astype(F32) + self.other[...].astype(F32)).astype(BF16)
        self.f[0].start()

    def rest(self):
        self.f[1].start()

    def total(self):
        self.m0.arrived()
        for m in self.f:
            m.arrived()
        total = self.own[...].astype(F32) + self.mine[...].astype(F32)
        return total + self.end[...].astype(F32)


class ZReduce:
    def __init__(self, post, at, term, buf):
        self.at, self.term, self.buf = at, term, buf
        self.m1 = post.msg(term(at.z1), buf(0), at.zn1, buf(0))
        self.m2 = post.msg(term(at.z2), buf(1), at.zn2, buf(1))
        self.m3 = post.msg(term(at.z3), buf(2), at.zn3, buf(2), when=at.mid)
        self.rel = post.msg(term(at.z3), buf(3), at.zn1, buf(3), when=at.end)

    def start_last(self):
        self.rel.start()
        self.m3.start()

    def start_far(self):
        pl.when(self.at.end)(self.m2.start)

    def start_near(self):
        self.m1.start()

    def relay(self):
        @pl.when(self.at.mid)
        def _():
            self.rel.arrived()
            there = self.term(self.at.z2)
            there[...] = (there[...].astype(F32) + self.buf(3)[...].astype(F32)).astype(BF16)
            self.m2.start()

    def total(self, out):
        self.m1.arrived()
        self.m2.arrived()
        value = self.term(self.at.z)[...].astype(F32) + self.buf(0)[...].astype(F32)
        out[...] = value + self.buf(1)[...].astype(F32)

        @pl.when(self.at.mid)
        def _():
            self.m3.arrived()
            out[...] += self.buf(2)[...].astype(F32)


class ZDirect:
    def __init__(self, post, at, term, buf):
        self.at, self.term, self.buf = at, term, buf
        self.msgs = [
            post.msg(term(zz), buf(k), dev, buf(k))
            for k, (zz, dev) in enumerate(((at.z1, at.zn1), (at.z2, at.zn2), (at.z3, at.zn3)))
        ]

    def start(self):
        for m in self.msgs[::-1]:
            m.start()

    def total(self, out):
        value = self.term(self.at.z)[...].astype(F32)
        for k, m in enumerate(self.msgs):
            m.arrived()
            value = value + self.buf(k)[...].astype(F32)
        out[...] = value


class Collect:
    def __init__(self, post, at, grads, near, bufs, bz, src, dst, buf, spare):
        self.at, self.grads, self.near, self.src = at, grads, near, src
        post.spare = list(spare)
        self.lanes, self.there = cols(src), cols(dst)
        into = pl.ds(buf, src[1])
        self.core = post.msg(
            grads.at[:, :, 1 - at.c, :, self.lanes], near.at[:, :, :, self.lanes], at.core,
            near.at[:, :, :, self.lanes],
        )
        self.plane = [
            HalfReduce(
                post,
                at,
                h,
                lambda x, y, h=h: near.at[:, x * 2 + y, pl.ds(16 * h, 16), self.lanes],
                *[b.at[h, :, :, into] for b in bufs],
            )
            for h in range(2)
        ]
        post.spare = []
        self.z = ZDirect(
            post, at, lambda zz: near.at[zz, at.p, :, self.lanes], lambda k: bz.at[k, :, self.there]
        )

    def start(self):
        self.core.start()

    def into_plane(self):
        self.core.arrived()

        def add(zz, carry):
            mine = self.grads[zz, :, self.at.c, :, self.lanes].astype(F32)
            self.near[zz, :, :, self.lanes] = (self.near[zz, :, :, self.lanes].astype(F32) + mine).astype(BF16)
            return carry

        lax.fori_loop(0, 4, add, 0)
        for h in self.plane:
            h.start()

    def relay(self):
        for h in self.plane:
            h.relay()

    def into_z(self):
        for k, h in enumerate(self.plane):
            self.near[:, self.at.p, 16 * k : 16 * k + 16, self.lanes] = h.total().astype(BF16)
        self.z.start()

    def total(self, out):
        self.z.total(out)


class CollectNorms:
    def __init__(self, post, at, grads, near, by, bx, b2, bz, span, spare):
        self.at, self.grads, self.near, self.lanes = at, grads, near, cols(span)
        post.spare = list(spare)
        low = pl.ds(0, 16)

        def part(p):
            return near.at[:, p, low, self.lanes]

        theirs = grads.at[:, :, 1 - at.c, low, self.lanes]
        here = near.at[:, :, low, self.lanes]
        self.core = post.msg(theirs, here, at.core, here)
        self.bufs = [b.at[0, :, :, self.lanes] for b in (bx, by, b2)]
        self.plane = [
            post.msg(part(p), buf, dev, buf)
            for p, buf, dev in zip((at.px, at.py, at.pd), self.bufs, (at.xn, at.yn, at.diag))
        ]
        post.spare = []
        self.z = ZDirect(
            post, at, lambda zz: near.at[zz, at.p, low, self.lanes], lambda k: bz.at[k, low, self.lanes]
        )

    def start(self):
        self.core.start()

    def into_plane(self):
        self.core.arrived()
        mine = self.grads[:, :, self.at.c, 0:16, self.lanes].astype(F32)
        self.near[:, :, 0:16, self.lanes] = (self.near[:, :, 0:16, self.lanes].astype(F32) + mine).astype(BF16)
        for m in self.plane:
            m.start()

    def into_z(self):
        total = self.near[:, self.at.p, 0:16, self.lanes].astype(F32)
        for m, buf in zip(self.plane, self.bufs):
            m.arrived()
            total = total + buf[...].astype(F32)
        self.near[:, self.at.p, 0:16, self.lanes] = total.astype(BF16)
        self.z.start()

    def total(self, out):
        self.z.total(out)


def head_mask():
    rows = lax.div(lax.broadcasted_iota(jnp.int32, (256, 256), 0), 64)
    lanes = lax.div(lax.broadcasted_iota(jnp.int32, (256, 256), 1), 64)
    return (rows == lanes).astype(F32).astype(BF16)


def spread_heads(part, mask):
    rows = part.reshape(64, 256)
    return jnp.concatenate([rows, rows, rows, rows], axis=0) * mask


def gather_heads(wide):
    lane = lax.div(lax.broadcasted_iota(jnp.int32, (64, 256), 1), 64)
    out = jnp.where(lane == 0, wide[0:64], 0.0)
    for h in range(1, 4):
        out = out + jnp.where(lane == h, wide[64 * h : 64 * h + 64], 0.0)
    return out


def pick(values, k):
    out = values[-1]
    for i in range(len(values) - 2, -1, -1):
        out = jnp.where(k == i, values[i], out)
    return out


def span256(n):
    return pl.ds(pl.multiple_of(n * 256, 256), 256)


class Names:
    def __getattr__(self, name):
        return name


class Steps:
    def __init__(self):
        self.made = {}

    def __getattr__(self, name):
        def keep(*actions):
            assert name not in self.made, name
            self.made[name] = actions

        return keep


def order(s):
    return (
        s.load, s.greet, s.staged, s.first_z, s.first_0, s.keys_0, s.cot_a, s.up_a, s.stats, s.keys_z, s.first_1,
        s.first_2, s.first_3, s.second_z, s.first_r0, s.first_r1, s.first_r2, s.first_r3, s.keys_1, s.keys_2,
        s.keys_3, s.third_z, s.first_c0, s.first_c1, s.first_c2, s.first_c3, s.down_a, s.up_in, s.up_z, s.keys_r0,
        s.keys_r1, s.keys_r2, s.keys_r3, s.first_in, s.query, s.q_a, s.second_in, s.second_a, s.keys_c0, s.keys_c1,
        s.keys_c2, s.keys_c3, s.low, s.second_b, s.keys_in, s.pairs_k, s.q_b, s.second_r, s.q_in, s.down_far,
        s.up_far, s.third_in, s.third_a, s.third_b, s.cot_b, s.score_0, s.ls_0, s.cot_r, s.score_1, s.ls_1,
        s.second_c, s.third_r, s.second_done, s.pairs_v, s.ls_in0, s.mix_0, s.mixed_a0, s.ls_in1, s.mix_1,
        s.mixed_a1, s.mixed_b0, s.mixed_b1, s.third_c, s.third_done, s.mixed_in0, s.mixed_in1, s.resid, s.mlp_a,
        s.mlp_b, s.mlp_r0, s.mlp_r1, s.cot_in, s.down_early, s.up_early, s.down_last, s.up_mid, s.down_done,
        s.cot_back, s.up_end, s.up_done, s.mlp_in0, s.gates_0, s.parts_0, s.recycle, s.back_a0, s.mlp_in1, s.gates_1,
        s.parts_1, s.back_a1, s.grad_d3, s.grad_u3, s.grad_d2, s.add_d3, s.grad_u2, s.add_u3, s.back_r0, s.grad_d1,
        s.grad_d0, s.back_r1, s.add_d2, s.add_u2, s.grad_u1, s.grad_u0, s.add_d1, s.add_d0, s.out_parts, s.add_u1,
        s.add_u0, s.back_in0, s.norm_0, s.gm_a0, s.back_in1, s.norm_1, s.gm_a1, s.out_a, s.w_out, s.out_core,
        s.gm_b0, s.gm_in0, s.gm_b1, s.probs_0, s.dl_0, s.gm_in1, s.probs_1, s.dl_1, s.value_0, s.dl_in0, s.out_plane,
        s.scores_0, s.gq_a0, s.dl_in1, s.scores_1, s.gq_a1, s.value_1, s.value_core, s.far_d, s.far_u, s.gq_b0,
        s.gq_b1, s.key_0, s.value_plane, s.out_relay, s.key_1, s.key_core, s.key_plane, s.media_0, s.media_1,
        s.value_relay, s.media_2, s.out_r, s.media_3, s.gq_in, s.query_core, s.norms, s.norms_core, s.key_relay,
        s.out_z, s.value_z, s.grad_latents, s.norms_plane, s.query_plane, s.key_z, s.query_relay, s.out_b, s.sum_d,
        s.sum_u, s.norms_z, s.query_z, s.out_sum, s.value_sum, s.key_sum, s.norms_sum, s.up_out, s.out_in,
        s.query_sum,
    )


def kernel_body(at, post, R):
    images, per_media, _ = R.MED.shape
    per_lat = R.latents.shape[1]
    rows = per_media + per_lat
    tokens = images * per_lat
    half_rows = tokens // 2
    each = images // 2
    zs = at.zs
    halves = (pl.ds(0, half_rows), pl.ds(half_rows, half_rows))
    do = Steps()

    own = R.G.at[at.z, at.p, at.c]
    loads = [
        pltpu.make_async_copy(src, dst, R.local.at[k])
        for k, (src, dst) in enumerate(
            (
                (R.in_media, R.MED),
                (R.in_latents, R.latents),
                (R.in_cotangent, R.cotangent),
                (R.in_query, own.at[:, cols(QU)]),
                (R.in_keyvalue, own.at[:, cols(KV)]),
                (R.in_output.at[:, pl.ds(0, 512)], own.at[pl.ds(0, 16), cols(OUT)]),
                (R.in_output.at[:, pl.ds(512, 512)], own.at[pl.ds(16, 16), cols(OUT)]),
                (R.in_up, R.w_up),
                (R.in_down, R.UD.at[at.z, at.c]),
            )
        )
    ]

    @do.load
    def _():
        for c in loads[3:] + loads[2:3] + loads[:2]:
            c.start()
        norms = [ref[...].astype(F32).reshape(1, 32) for ref in (R.n0, R.n1, R.n2, R.n3, R.n4, R.n5)]
        norms = jnp.concatenate(norms + [jnp.zeros((10, 32), F32)], axis=0)
        norms = jnp.concatenate([norms, norms, norms, norms], axis=1)
        lanes = lax.div(lax.broadcasted_iota(jnp.int32, (16, 128), 1), 32)
        R.G[at.z, at.p, at.c, 0:16, cols(GN)] = jnp.where(lanes == at.l, norms, 0.0).astype(BF16)
        R.G[at.z, at.p, at.c, 16:32, cols(GN)] = jnp.zeros((16, 128), BF16)

    do.greet(at.greet)

    @do.staged
    def _():
        for c in loads[3:]:
            c.wait()
        for p in range(4):
            for zz in range(4):
                for cc in range(2):
                    R.WS[p, :, 128 * (2 * zz + cc) : 128 * (2 * zz + cc) + 128] = R.w_up[
                        :, 128 * (8 * zz + 2 * p + cc) : 128 * (8 * zz + 2 * p + cc) + 128
                    ]
        R.UU[at.z, at.p, at.c] = R.WS[at.p]
        loads[2].wait()
        R.CA[at.p] = R.cotangent[...].reshape(tokens, 1024)

    first = Spread(post, at, R.G, (0, 640))
    keys = Spread(post, at, R.G, KEY)
    second = SpreadWide(post, at, R.G, VAL, True)
    third = SpreadWide(post, at, R.G, OUT, False)
    for name, stream in (("first", first), ("keys", keys)):
        getattr(do, name + "_z")(stream.start)
        getattr(do, name + "_0")(stream.plane[0].start)
        for k in range(1, 4):
            getattr(do, "%s_%d" % (name, k))(stream.z[k - 1].arrived, stream.plane[k].start)
        for k in range(4):
            getattr(do, "%s_r%d" % (name, k))(stream.plane[k].relay)
            getattr(do, "%s_c%d" % (name, k))(stream.plane[k].last, stream.core[k].start)
        getattr(do, name + "_in")(stream.arrived)
    for name, stream in (("second", second), ("third", third)):
        getattr(do, name + "_z")(stream.start)
        getattr(do, name + "_in")(stream.along_z)
        getattr(do, name + "_a")(stream.one.start)
        getattr(do, name + "_b")(stream.two.start)
        getattr(do, name + "_r")(stream.relay)
        getattr(do, name + "_c")(stream.to_core)
        getattr(do, name + "_done")(stream.arrived)

    up = [
        post.msg(R.WS.at[there], R.UU.at[at.z, at.p, at.c], dev, R.UU.at[at.z, there, at.c])
        for there, dev in ((at.px, at.xn), (at.py, at.yn), (at.pd, at.diag))
    ]
    do.up_a(*[m.start for m in up])
    do.up_in(*[m.arrived for m in up])
    d_z = ZGather(
        post,
        at,
        lambda zz: R.UD.at[zz, at.c],
        lambda zz: post.msg(R.UD.at[zz, at.c], R.UD.at[zz, at.c], at.core, R.UD.at[zz, 1 - at.c]),
    )
    u_z = ZGather(
        post,
        at,
        lambda zz: R.UU.at[zz, :, at.c],
        lambda zz: post.msg(R.UU.at[zz, :, at.c], R.UU.at[zz, :, at.c], at.core, R.UU.at[zz, :, 1 - at.c]),
    )
    do.down_a(d_z.start)
    do.down_far(d_z.far)
    do.down_early(d_z.early)
    do.down_last(d_z.last)
    do.down_done(d_z.all)
    do.up_z(u_z.start)
    do.up_far(u_z.far)
    do.up_early(u_z.early)
    do.up_mid(lambda: pl.when(at.mid)(u_z.last))
    do.up_end(lambda: pl.when(at.end)(u_z.last))
    do.up_done(u_z.all)

    cot = HalfGather(post, at, lambda x, y, h: R.CA.at[x * 2 + y, halves[h]])
    do.cot_a(cot.start)
    do.cot_b(cot.rest)
    do.cot_r(cot.relay)
    do.cot_in(cot.last)

    @do.stats
    def _():
        def stats(g, carry):
            mean, rstd = normal(R.MED[g].astype(F32))
            R.MR[g, 0:per_media, 0:1] = mean
            R.MR[g, 0:per_media, 1:2] = rstd
            mean, rstd = normal(R.latents[g].astype(F32))
            R.MR[g, per_media:rows, 0:1] = mean
            R.MR[g, per_media:rows, 1:2] = rstd
            return carry

        loads[0].wait()
        loads[1].wait()
        loop(images, stats)

    @do.query
    def _():
        for i in range(8):
            total = jnp.zeros((16, 128), F32)
            for p in (2 * (i % 2), 2 * (i % 2) + 1):
                for c in range(2):
                    total = total + R.G[i // 2, p, c, 0:16, cols(GN)].astype(F32)
            R.VV[:, 128 * i : 128 * i + 128] = total
        latents = flat(R.latents[...]).astype(F32)
        normed = (latents - flat(R.MR[:, per_media:rows, 0:1])) * flat(R.MR[:, per_media:rows, 1:2])
        latent_low = (normed * R.VV[2:3, :] + R.VV[3:4, :]).astype(BF16)
        R.X[:, per_media:rows, :] = latent_low.reshape(images, per_lat, 1024)
        R.QA[at.l] = mm(latent_low, R.G[:, :, :, :, cols(QU)].reshape(1024, 512)).astype(BF16)

    q_all = LatGather(post, at, lambda l: R.QA.at[l])
    do.q_a(q_all.start)
    do.q_b(q_all.relay)
    do.q_in(q_all.last)

    @do.low
    def _():
        def low(g, carry):
            normed = (R.MED[g].astype(F32) - R.MR[g, 0:per_media, 0:1]) * R.MR[g, 0:per_media, 1:2]
            R.X[g, 0:per_media, :] = (normed * R.VV[0:1, :] + R.VV[1:2, :]).astype(BF16)
            return carry

        loop(images, low)

    def pairs(n, carry):
        weight = R.G[:, :, :, :, pl.ds(pl.multiple_of(KV[0] + n * 256, 128), 256)].reshape(1024, 256)
        made = mm(R.X[...].reshape(images * rows, 1024), weight).astype(BF16)
        R.PR[:, :, span256(n)] = made.reshape(images, rows, 256)
        return carry

    do.pairs_k(lambda: loop((0, 2), pairs))
    do.pairs_v(lambda: loop((2, 4), pairs))

    mask = head_mask()

    def lat_rows(g):
        return pl.ds(pl.multiple_of(g * per_lat, per_lat), per_lat)

    def score(g, carry):
        limit = SHORT + (LONG - SHORT) * R.bucket[g] - at.l * per_media
        row = lax.broadcasted_iota(jnp.int32, (rows, 256), 0)
        valid = jnp.logical_or(row >= per_media, row < limit)
        for half in range(2):
            span = pl.ds(256 * half, 256)
            raw = mm_nt(R.PR[g, :, span], spread_heads(R.QA[:, lat_rows(g), span], mask)) * SCALE
            raw = jnp.where(valid, raw, NEG)
            top = jnp.max(raw, axis=0, keepdims=True)
            total = jnp.sum(jnp.exp(raw - top), axis=0, keepdims=True)
            R.S[2 * g + half] = raw
            R.LS[at.l, pl.ds(2 * g + half, 1), :] = top + jnp.log(total)
        return carry

    def mix(g, carry):
        for half in range(2):
            probs = jnp.exp(R.S[2 * g + half] - R.LG[pl.ds(2 * g + half, 1), :]).astype(BF16)
            R.PB[2 * g + half] = probs
            wide = mm_tn(probs, R.PR[g, :, pl.ds(512 + 256 * half, 256)])
            R.OP[:, lat_rows(g), pl.ds(256 * half, 256)] = (
                gather_heads(wide).reshape(4, per_lat, 256).astype(BF16)
            )
        return carry

    def exchange(ref, span):
        return [
            post.msg(ref.at[at.l, span], ref.at[at.l, span], dev, ref.at[there, span])
            for there, dev in ((at.ly, at.yn), (at.ld, at.ycore), (at.lc, at.core))
        ]

    def log_total(span):
        parts = [R.LS[l, span, :] for l in range(4)]
        top = jnp.maximum(jnp.maximum(parts[0], parts[1]), jnp.maximum(parts[2], parts[3]))
        total = sum(jnp.exp(part - top) for part in parts)
        R.LG[span, :] = top + jnp.log(total)

    lat_keys = []
    for h in range(2):
        here = (each * h, each * h + each)
        span = pl.ds(2 * each * h, 2 * each)
        getattr(do, "score_%d" % h)(lambda here=here: loop(here, score))
        ls = exchange(R.LS, span)
        getattr(do, "ls_%d" % h)(*[m.start for m in ls])
        getattr(do, "ls_in%d" % h)(*[m.arrived for m in ls], lambda span=span: log_total(span))
        getattr(do, "mix_%d" % h)(lambda here=here: loop(here, mix))
        mixed = LatReduce(post, at, R.OP.at[:, halves[h]], R.O1.at[:, halves[h]], R.O2.at[halves[h]])
        lat_keys.append([m.key for m in ls + [mixed.m0, mixed.m1, mixed.m2]])
        getattr(do, "mixed_a%d" % h)(mixed.start)
        getattr(do, "mixed_b%d" % h)(mixed.relay)

        @getattr(do, "mixed_in%d" % h)
        def _(mixed=mixed, h=h):
            R.MX[halves[h], :] = mixed.total().astype(BF16)

    def out_weight():
        left = R.G[:, :, :, 0:16, cols(OUT)].reshape(512, 512)
        return left, R.G[:, :, :, 16:32, cols(OUT)].reshape(512, 512)

    @do.resid
    def _():
        left, right = out_weight()
        latents = flat(R.latents[...]).astype(F32)
        R.RES[:, 0:512] = latents[:, 0:512] + mm(R.MX[...], left)
        R.RES[:, 512:1024] = latents[:, 512:1024] + mm(R.MX[...], right)
        mean, rstd = normal(R.RES[...])
        R.RN[:, 0:1] = mean
        R.RN[:, 1:2] = rstd
        R.MA[at.p] = ((R.RES[...] - mean) * rstd * R.VV[4:5, :] + R.VV[5:6, :]).astype(BF16)

    mlp = HalfGather(post, at, lambda x, y, h: R.MA.at[x * 2 + y, halves[h]])
    do.mlp_a(mlp.start)
    do.mlp_b(mlp.rest)
    do.mlp_r0(mlp.relay0)
    do.mlp_r1(mlp.relay1)
    do.mlp_in0(mlp.last0)
    do.mlp_in1(mlp.last1)

    do.recycle(*[m.sent for m in post.recycle()])
    planes = [m.key for w in (first, keys) for g in w.plane for m in (g.mx, g.my, g.hy, g.hx)]
    cores = [m.key for w in (first, keys) for m in w.core]

    @do.cot_back
    def _():
        def cot_back(f, carry):
            made = mm_nt(R.CA[...].reshape(4 * tokens, 1024), R.UD[f].reshape(256, 1024))
            R.S[pl.ds(4 * f, 4), 0:tokens, :] = made.reshape(4, tokens, 256)
            return carry

        loop(4, cot_back)

    def gates(h):
        part = halves[h]

        def gates(f, carry):
            weight = R.UU[:, :, :, :, span256(f)].reshape(1024, 256)
            gate = mm(R.MA[:, part, :].reshape(4 * half_rows, 1024), weight)
            back = R.S[pl.ds(4 * f, 4), part, :].reshape(4 * half_rows, 256)
            phi = 0.5 * (1.0 + lax.erf(gate * 0.7071067811865476))
            R.ACT[:, part, span256(f)] = (gate * phi).astype(BF16).reshape(4, half_rows, 256)
            slope = phi + gate * jnp.exp(-0.5 * gate * gate) * 0.3989422804014327
            R.GG[:, part, span256(f)] = (back * slope).astype(BF16).reshape(4, half_rows, 256)
            return carry

        loop(4, gates)

    def norm_parts(h):
        part = halves[h]

        def norm_parts(n, carry):
            made = mm_nt(R.GG[:, part, :].reshape(4 * half_rows, 1024), R.UU[n].reshape(256, 1024))
            R.PT[:, part, span256(n)] = made.astype(BF16).reshape(4, half_rows, 256)
            return carry

        loop(4, norm_parts)

    post.spare = [m.key for w in (second, third) for m in (w.one, w.two, w.on)]
    for h in range(2):
        getattr(do, "gates_%d" % h)(lambda h=h: gates(h))
        getattr(do, "parts_%d" % h)(lambda h=h: norm_parts(h))
        back = HalfReduce(
            post, at, h, lambda x, y, h=h: R.PT.at[x * 2 + y, halves[h]], R.PY.at[h], R.PX.at[h], R.P2.at[h]
        )
        getattr(do, "back_a%d" % h)(back.start)
        getattr(do, "back_r%d" % h)(back.relay)

        @getattr(do, "back_in%d" % h)
        def _(back=back, h=h):
            R.U[halves[h], :] = back.total()

    def down_grads(k, carry):
        f = pick(zs, k)
        act = R.ACT[:, :, span256(f)].reshape(4 * tokens, 256)
        R.gD[f] = mm_tn(act, R.CA[...].reshape(4 * tokens, 1024)).astype(BF16).reshape(2, 128, 1024)
        return carry

    def up_grads(k, carry):
        n = pick(zs, k)
        low_rows = R.MA[:, :, span256(n)].reshape(4 * tokens, 256)
        made = mm_tn(low_rows, R.GG[...].reshape(4 * tokens, 1024)).astype(BF16)
        R.gU[n] = made.reshape(4, 2, 32, 1024)
        return carry

    gd_z = ZReduce(post, at, lambda zz: R.RD.at[zz], lambda k: R.ZD.at[k])
    gu_z = ZReduce(post, at, lambda zz: R.RU.at[zz], lambda k: R.ZU.at[k])
    nothing = lambda: None
    gu_c = []
    post.spare = cores
    for k in range(4):
        zz = zs[k]
        gd = post.msg(R.gD.at[zz, 1 - at.c], R.RD.at[zz], at.core, R.RD.at[zz])
        gu = post.msg(R.gU.at[zz, :, 1 - at.c], R.RU.at[zz], at.core, R.RU.at[zz])
        gu_c.append(gu)
        getattr(do, "grad_d%d" % k)(lambda k=k: loop((k, k + 1), down_grads), gd.start)
        getattr(do, "grad_u%d" % k)(lambda k=k: loop((k, k + 1), up_grads), gu.start)

        def add_d(zz=zz):
            R.RD[zz] = (R.RD[zz].astype(F32) + R.gD[zz, at.c].astype(F32)).astype(BF16)

        def add_u(zz=zz):
            R.RU[zz] = (R.RU[zz].astype(F32) + R.gU[zz, :, at.c].astype(F32)).astype(BF16)

        send = (nothing, "start_near", "start_far", "start_last")[k]
        getattr(do, "add_d%d" % k)(gd.arrived, add_d, getattr(gd_z, send) if k else nothing)
        getattr(do, "add_u%d" % k)(gu.arrived, add_u, getattr(gu_z, send) if k else nothing)
    do.far_d(gd_z.relay)
    do.far_u(gu_z.relay)

    @do.out_parts
    def _():
        def out_parts(n, carry):
            made = mm(R.ACT[...].reshape(4 * tokens, 1024), R.UD[:, :, :, span256(n)].reshape(1024, 256))
            R.GG[:, :, span256(n)] = made.astype(BF16).reshape(4, tokens, 256)
            return carry

        loop(4, out_parts)

    out = PlaneReduceX(post, at, lambda x, y: R.GG.at[x * 2 + y], R.OX.at[0], R.OX.at[1], R.OY, 2)
    do.out_a(out.start)
    do.out_r(out.relay)
    do.out_b(out.rest)

    post.spare = [m.key for m in (q_all.mc, q_all.my, q_all.fc, second.core, third.core)]
    for h in range(2):

        @getattr(do, "norm_%d" % h)
        def _(h=h):
            part = halves[h]
            normed = (R.RES[part, :] - R.RN[part, 0:1]) * R.RN[part, 1:2]
            cots = R.CA[at.p, part, :].astype(F32)
            R.GR[part, :] = cots + norm_back(R.U[part, :], normed, R.RN[part, 1:2], R.VV[4:5, :])
            grad_attn = R.GR[part, :].astype(BF16)
            left, right = out_weight()
            made = mm_nt(grad_attn[:, 0:512], left) + mm_nt(grad_attn[:, 512:1024], right)
            R.GM[at.l, part, :] = made.astype(BF16)

        gm = LatGather(post, at, lambda l, h=h: R.GM.at[l, halves[h]])
        getattr(do, "gm_a%d" % h)(gm.start)
        getattr(do, "gm_b%d" % h)(gm.relay)
        getattr(do, "gm_in%d" % h)(gm.last)

    @do.w_out
    def _():
        upstream = R.U[...]
        normed = (R.RES[...] - R.RN[:, 0:1]) * R.RN[:, 1:2]
        R.GS[...] = jnp.zeros_like(R.GS)
        R.GS[4:5, :] = jnp.sum(upstream * normed, axis=0, keepdims=True)
        R.GS[5:6, :] = jnp.sum(upstream, axis=0, keepdims=True)
        grad_attn = R.GR[...].astype(BF16)
        made = mm_tn(R.MX[...], grad_attn[:, 0:512]).astype(BF16)
        R.gA[:, :, :, 0:16, cols(GOUT)] = made.reshape(4, 4, 2, 16, 512)
        made = mm_tn(R.MX[...], grad_attn[:, 512:1024]).astype(BF16)
        R.gA[:, :, :, 16:32, cols(GOUT)] = made.reshape(4, 4, 2, 16, 512)

    bufs = (R.WY, R.WX, R.W2)
    for name, made in (
        ("out", Collect(post, at, R.gA, R.RA, bufs, R.ZW, GOUT, OUT, OUT[0], planes[0:7])),
        ("value", Collect(post, at, R.gU, R.RK, bufs, R.ZW, (512, 512), VAL, VAL[0], planes[7:14])),
        ("key", Collect(post, at, R.gU, R.RK, bufs, R.ZW, (0, 512), KEY, KEY[0], planes[14:21])),
        ("query", Collect(post, at, R.gA, R.RA, bufs, R.ZW, QU, QU, QU[0], planes[21:28])),
        ("norms", CollectNorms(post, at, R.gA, R.RA, R.WY, R.WX, R.W2, R.ZW, GN, planes[28:32])),
    ):
        getattr(do, name + "_core")(made.start)
        getattr(do, name + "_plane")(made.into_plane)
        if name != "norms":
            getattr(do, name + "_relay")(made.relay)
        getattr(do, name + "_z")(made.into_z)
        span = {"out": OUT, "value": VAL, "key": KEY, "query": QU, "norms": GN}[name]
        height = 16 if name == "norms" else 32
        getattr(do, name + "_sum")(lambda made=made, span=span, height=height: made.total(
            R.grad_pack.at[pl.ds(0, height), cols(span)]
        ))

    def grad_probs(g, carry):
        for half in range(2):
            upper = pl.ds(512 + 256 * half, 256)
            wide = spread_heads(R.GM[:, lat_rows(g), pl.ds(256 * half, 256)], mask)
            made = mm_nt(R.PR[g, :, upper], wide)
            probs = R.PB[2 * g + half]
            R.S[2 * g + half] = made
            R.DL[at.l, pl.ds(2 * g + half, 1), :] = jnp.sum(probs.astype(F32) * made, axis=0, keepdims=True)
            R.gP[g, :, upper] = mm(probs, wide).astype(BF16)
        return carry

    def grad_scores(g, carry):
        for half in range(2):
            span = pl.ds(256 * half, 256)
            grads = R.PB[2 * g + half].astype(F32) * (R.S[2 * g + half] - R.LG[pl.ds(2 * g + half, 1), :])
            grads = grads.astype(BF16)
            wide = mm_tn(grads, R.PR[g, :, span]) * SCALE
            R.QP[:, lat_rows(g), span] = gather_heads(wide).reshape(4, per_lat, 256).astype(BF16)
            queries = spread_heads(R.QA[:, lat_rows(g), span], mask)
            R.gP[g, :, span] = (mm(grads, queries) * SCALE).astype(BF16)
        return carry

    def row_terms(span):
        R.LG[span, :] = R.DL[0, span, :] + R.DL[1, span, :] + R.DL[2, span, :] + R.DL[3, span, :]

    sums = []
    for h in range(2):
        here = (each * h, each * h + each)
        span = pl.ds(2 * each * h, 2 * each)
        post.spare = lat_keys[h]
        getattr(do, "probs_%d" % h)(lambda here=here: loop(here, grad_probs))
        dl = exchange(R.DL, span)
        getattr(do, "dl_%d" % h)(*[m.start for m in dl])
        getattr(do, "dl_in%d" % h)(*[m.arrived for m in dl], lambda span=span: row_terms(span))
        getattr(do, "scores_%d" % h)(lambda here=here: loop(here, grad_scores))
        gq = LatReduce(post, at, R.QP.at[:, halves[h]], R.Q1.at[:, halves[h]], R.Q2.at[halves[h]])
        getattr(do, "gq_a%d" % h)(gq.start)
        getattr(do, "gq_b%d" % h)(gq.relay)
        sums.append(gq)

    def kv_grads(n, carry):
        low_rows = R.X[:, :, span256(lax.rem(n, 4))].reshape(images * rows, 256)
        lanes = pl.ds(pl.multiple_of(lax.div(n, 4) * 512, 512), 512)
        made = mm_tn(low_rows, R.gP[:, :, lanes].reshape(images * rows, 512)).astype(BF16)
        R.gU[lax.rem(n, 4), :, :, :, lanes] = made.reshape(4, 2, 32, 512)
        return carry

    do.value_0(*[m.sent for m in gu_c], lambda: loop((4, 6), kv_grads))
    do.value_1(lambda: loop((6, 8), kv_grads))
    do.key_0(lambda: loop((0, 2), kv_grads))
    do.key_1(lambda: loop((2, 4), kv_grads))

    def media_copy(h):
        return pltpu.make_async_copy(R.MG, R.to_media.at[pl.ds(h * 2, 2)], R.local.at[9])

    def media_grads(h, carry):
        span = pl.ds(h * 2, 2)
        weight = R.G[:, :, :, :, cols(KV)].reshape(1024, 1024)
        upstream = mm_nt(R.gP[span].reshape(2 * rows, 1024), weight).reshape(2, rows, 1024)
        R.U[pl.ds(h * 2 * per_lat, 2 * per_lat)] = upstream[:, per_media:rows, :].reshape(2 * per_lat, 1024)
        upstream = upstream[:, 0:per_media, :]
        rstd = R.MR[span, 0:per_media, 1:2]
        normed = (R.MED[span].astype(F32) - R.MR[span, 0:per_media, 0:1]) * rstd
        made = norm_back(upstream, normed, rstd, R.VV[0:1, :]).astype(R.MG.dtype)
        pl.when(h >= 1)(lambda: media_copy(h - 1).wait())
        R.MG[...] = made
        media_copy(h).start()
        R.GS[0:1, :] += jnp.sum(flat(upstream * normed), axis=0, keepdims=True)
        R.GS[1:2, :] += jnp.sum(flat(upstream), axis=0, keepdims=True)
        return carry

    for k in range(4):
        getattr(do, "media_%d" % k)(lambda k=k: loop((k, k + 1), media_grads))

    @do.gq_in
    def _():
        for h in range(2):
            R.GQ[halves[h], :] = sums[h].total().astype(BF16)
        latent_low = flat(R.X[:, per_media:rows, :])
        R.gA[:, :, :, :, cols(QU)] = mm_tn(latent_low, R.GQ[...]).astype(BF16).reshape(4, 4, 2, 32, 512)

    def latent_terms():
        rstd = flat(R.MR[:, per_media:rows, 1:2])
        return (flat(R.latents[...]).astype(F32) - flat(R.MR[:, per_media:rows, 0:1])) * rstd, rstd

    @do.norms
    def _():
        R.U[...] += mm_nt(R.GQ[...], R.G[:, :, :, :, cols(QU)].reshape(1024, 512))
        normed, _ = latent_terms()
        R.GS[2:3, :] = jnp.sum(R.U[...] * normed, axis=0, keepdims=True)
        R.GS[3:4, :] = jnp.sum(R.U[...], axis=0, keepdims=True)
        for i in range(8):
            piece = R.GS[:, 128 * i : 128 * i + 128].astype(BF16)
            for p in (2 * (i % 2), 2 * (i % 2) + 1):
                for c in range(2):
                    R.gA[i // 2, p, c, 0:16, cols(GN)] = piece

    results = [
        pltpu.make_async_copy(src, dst, R.local.at[10 + k])
        for k, (src, dst) in enumerate(
            (
                (R.latents_out, R.to_out),
                (R.grad_latents, R.to_latents),
                (R.grad_down, R.to_down),
                (R.grad_up, R.to_up),
                (R.grad_pack, R.to_pack),
            )
        )
    ]

    @do.grad_latents
    def _():
        normed, rstd = latent_terms()
        R.grad_latents[...] = (R.GR[...] + norm_back(R.U[...], normed, rstd, R.VV[2:3, :])).reshape(
            images, per_lat, 1024
        )
        results[1].start()

    do.sum_d(lambda: gd_z.total(R.grad_down), results[2].start)
    post.spare = [m.key for m in up]
    back_up = [
        post.msg(R.SU.at[there], R.AU.at[at.p], dev, R.AU.at[there])
        for there, dev in ((at.px, at.xn), (at.py, at.yn), (at.pd, at.diag))
    ]

    @do.sum_u
    def _():
        gu_z.total(R.SF)
        R.SU[...] = R.SF[...].astype(BF16)
        R.AU[at.p] = R.SU[at.p]
        for m in back_up:
            m.start()

    @do.up_out
    def _():
        for m in back_up:
            m.arrived()
        for p in range(4):
            for zz in range(4):
                for cc in range(2):
                    R.grad_up[:, 128 * (8 * zz + 2 * p + cc) : 128 * (8 * zz + 2 * p + cc) + 128] = R.AU[
                        p, :, 128 * (2 * zz + cc) : 128 * (2 * zz + cc) + 128
                    ].astype(F32)
        results[3].start()

    @do.out_in
    def _():
        R.latents_out[...] = (R.RES[...] + out.total()).astype(BF16).reshape(images, per_lat, 1024)
        results[0].start()

    names = order(Names())
    assert sorted(names) == sorted(do.made), set(names) ^ set(do.made)
    for name in names:
        with jax.named_scope(name):
            for action in do.made[name]:
                action()
    results[4].start()
    media_copy(images // 2 - 1).wait()
    for c in results:
        c.wait()


def loop(bounds, action):
    first, last = bounds if isinstance(bounds, tuple) else (0, bounds)
    lax.fori_loop(first, last, action, 0)


def place_of(name):
    if name == "bucket":
        return pltpu.SMEM
    return pl.ANY if name.startswith(("in_", "to_")) else pltpu.VMEM


class Refs:
    def __init__(self, names, refs):
        for name, ref in zip(names, refs):
            setattr(self, name, ref)


def build(kernel_body, inputs, outputs, scratch, messages, cid, name):
    in_names = [n for n, _ in inputs]
    out_names = [n for n, _, _ in outputs]
    scratch_names = [n for n, _, _ in scratch]

    def kernel(*refs):
        R = Refs(in_names + out_names + scratch_names, refs)
        at = Place()
        R.local = refs[-3]
        post = Post(refs[-2], refs[-1])
        kernel_body(at, post, R)
        with jax.named_scope('drain'):
            post.drain()
        assert (post.most, post.keys) == messages, (post.most, post.keys)

    specs = [
        pl.BlockSpec(memory_space=place_of(n)) for n in in_names
    ]
    return pl.pallas_call(
        kernel,
        out_shape=[jax.ShapeDtypeStruct(s, d) for _, s, d in outputs],
        in_specs=specs,
        out_specs=[
            pl.BlockSpec(memory_space=place_of(n)) for n, _, _ in outputs
        ],
        scratch_shapes=[pltpu.VMEM(s, d) for _, s, d in scratch]
        + [pltpu.SemaphoreType.DMA((15,))] + [pltpu.SemaphoreType.DMA((n,)) for n in messages],
        compiler_params=pltpu.CompilerParams(
            collective_id=cid, has_side_effects=True, vmem_limit_bytes=62 << 20
        ),
        name=name,
    )(*[v for _, v in inputs])


def layer(media, latents, bucket, cotangent, n0, n1, n2, n3, n4, n5, w_query, w_keyvalue, w_output, w_up, w_down):
    images, per_media, _ = media.shape
    per_lat = latents.shape[1]
    rows = per_media + per_lat
    tokens = images * per_lat
    inputs = [
        ("in_media", media),
        ("in_latents", latents),
        ("in_cotangent", cotangent),
        ("bucket", bucket),
        ("n0", n0),
        ("n1", n1),
        ("n2", n2),
        ("n3", n3),
        ("n4", n4),
        ("n5", n5),
        ("in_query", w_query),
        ("in_keyvalue", w_keyvalue),
        ("in_output", w_output),
        ("in_up", w_up),
        ("in_down", w_down),
    ]
    outputs = [
        ("to_out", (images, per_lat, 1024), BF16),
        ("to_media", (images, per_media, 1024), BF16),
        ("to_latents", (images, per_lat, 1024), F32),
        ("to_pack", (32, WIDE), F32),
        ("to_up", (32, 4096), F32),
        ("to_down", (128, 1024), F32),
    ]
    scratch = [
        ("MED", (images, per_media, 1024), BF16),
        ("X", (images, rows, 1024), BF16),
        ("MR", (images, rows, 2), F32),
        ("PR", (images, rows, 1024), BF16),
        ("S", (2 * images, rows, 256), F32),
        ("PB", (2 * images, rows, 256), BF16),
        ("QA", (4, tokens, 512), BF16),
        ("MX", (tokens, 512), BF16),
        ("RES", (tokens, 1024), F32),
        ("MA", (4, tokens, 1024), BF16),
        ("CA", (4, tokens, 1024), BF16),
        ("UD", (4, 2, 128, 1024), BF16),
        ("UU", (4, 4, 2, 32, 1024), BF16),
        ("G", (4, 4, 2, 32, WIDE), BF16),
        ("VV", (16, 1024), F32),
        ("WS", (4, 32, 1024), BF16),
        ("LS", (4, 2 * images, 256), F32),
        ("LG", (2 * images, 256), F32),
        ("OP", (4, tokens, 512), BF16),
        ("O1", (2, tokens, 512), BF16),
        ("O2", (tokens, 512), BF16),
        ("MG", (2, per_media, 1024), BF16),
        ("RN", (tokens, 2), F32),
        ("latents", (images, per_lat, 1024), BF16),
        ("cotangent", (images, per_lat, 1024), BF16),
        ("w_up", (32, 4096), BF16),
        ("latents_out", (images, per_lat, 1024), BF16),
        ("grad_latents", (images, per_lat, 1024), F32),
        ("grad_pack", (32, WIDE), F32),
        ("grad_up", (32, 4096), F32),
        ("grad_down", (128, 1024), F32),
        ("ACT", (4, tokens, 1024), BF16),
        ("GG", (4, tokens, 1024), BF16),
        ("PT", (4, tokens, 1024), BF16),
        ("PY", (2, tokens // 2, 1024), BF16),
        ("PX", (2, tokens // 2, 1024), BF16),
        ("P2", (2, tokens // 2, 1024), BF16),
        ("OX", (2, tokens, 1024), BF16),
        ("OY", (tokens, 1024), BF16),
        ("gD", (4, 2, 128, 1024), BF16),
        ("gU", (4, 4, 2, 32, 1024), BF16),
        ("RD", (4, 128, 1024), BF16),
        ("RU", (4, 4, 32, 1024), BF16),
        ("ZD", (4, 128, 1024), BF16),
        ("ZU", (4, 4, 32, 1024), BF16),
        ("U", (tokens, 1024), F32),
        ("GR", (tokens, 1024), F32),
        ("GS", (16, 1024), F32),
        ("GM", (4, tokens, 512), BF16),
        ("gP", (images, rows, 1024), BF16),
        ("DL", (4, 2 * images, 256), F32),
        ("QP", (4, tokens, 512), BF16),
        ("Q1", (2, tokens, 512), BF16),
        ("Q2", (tokens, 512), BF16),
        ("GQ", (tokens, 512), BF16),
        ("gA", (4, 4, 2, 32, NARROW), BF16),
        ("RA", (4, 4, 32, NARROW), BF16),
        ("RK", (4, 4, 32, 1024), BF16),
        ("WY", (2, 4, 16, WIDE), BF16),
        ("WX", (2, 4, 16, WIDE), BF16),
        ("W2", (2, 4, 16, WIDE), BF16),
        ("ZW", (3, 32, WIDE), BF16),
        ("SF", (4, 32, 1024), F32),
        ("SU", (4, 32, 1024), BF16),
        ("AU", (4, 32, 1024), BF16),
    ]
    return build(kernel_body, inputs, outputs, scratch, MESSAGES, 1, "resampler")


def finish_body(
    out_in, media_in, latents_in, pack, up_in, down_in, out, media, latents, n0, n1, n2, n3, n4, n5, wq, wkv, wo, wu, wd
):
    rows = wo.shape[0]
    media[...] = media_in[...].astype(F32)

    @pl.when(pl.program_id(0) == 0)
    def _():
        out[...] = out_in[...]
        latents[...] = latents_in[...]
        wu[...] = up_in[...]
        wd[...] = down_in[...]
        wq[...] = pack[:, cols(QU)]
        wkv[...] = pack[:, cols(KV)]
        wo[:, 0:512] = pack[0:rows, cols(OUT)]
        wo[:, 512:1024] = pack[rows : 2 * rows, cols(OUT)]
        mine = pltpu.roll(pack[0:8, cols(GN)], lax.rem(128 - 32 * lax.axis_index("lat"), 128), 1)
        for k, ref in enumerate((n0, n1, n2, n3, n4, n5)):
            ref[...] = mine[k, 0:32]


def finish(latents_out, grad_media, grad_latents, grad_pack, grad_up, grad_down):
    images, per_media, width = grad_media.shape
    block = pl.BlockSpec((images // 2, per_media, width), lambda g: (g, 0, 0))

    def whole(shape):
        return pl.BlockSpec(shape, lambda g: (0,) * len(shape))

    shapes = [
        jax.ShapeDtypeStruct(latents_out.shape, BF16),
        jax.ShapeDtypeStruct(grad_media.shape, F32),
        jax.ShapeDtypeStruct(grad_latents.shape, F32),
    ] + [
        jax.ShapeDtypeStruct(shape, F32)
        for shape in ((32,),) * 6 + ((32, 512), (32, 1024), (16, 1024), grad_up.shape, grad_down.shape)
    ]
    values = (latents_out, grad_media, grad_latents, grad_pack, grad_up, grad_down)
    return pl.pallas_call(
        finish_body,
        grid=(2,),
        out_shape=shapes,
        in_specs=[block if k == 1 else whole(v.shape) for k, v in enumerate(values)],
        out_specs=[block if k == 1 else whole(v.shape) for k, v in enumerate(shapes)],
        compiler_params=pltpu.CompilerParams(vmem_limit_bytes=60 << 20),
        name="finish",
    )(*values)


def solution(mesh):
    sizes = dict(mesh.shape)
    blocks = sizes["img"] // BLOCK
    names = ("img", "lat")

    def block_shard(weight):
        if blocks == 1:
            return weight
        whole = lax.all_gather(weight, names, axis=0, tiled=True)
        each = whole.shape[0] // (BLOCK * sizes["lat"])
        mine = lax.rem(lax.axis_index("img"), BLOCK) * sizes["lat"] + lax.axis_index("lat")
        return lax.dynamic_slice_in_dim(whole, mine * each, each, 0)

    def own_shard(gradient):
        if blocks == 1:
            return gradient
        each = gradient.shape[0]
        mine = lax.rem(lax.axis_index("img"), BLOCK) * sizes["lat"] + lax.axis_index("lat")
        whole = jnp.zeros((each * BLOCK * sizes["lat"],) + gradient.shape[1:], gradient.dtype)
        whole = lax.dynamic_update_slice_in_dim(whole, gradient, mine * each, 0)
        return lax.psum_scatter(whole, names, scatter_dimension=0, tiled=True)

    def on_device(
        media,
        latents,
        bucket,
        gain_media,
        shift_media,
        gain_latent,
        shift_latent,
        gain_mlp,
        shift_mlp,
        w_query,
        w_keyvalue,
        w_output,
        w_up,
        w_down,
        cotangent,
    ):
        norms = (gain_media, shift_media, gain_latent, shift_latent, gain_mlp, shift_mlp)
        weights = (w_query, w_keyvalue, w_output, w_up, w_down)
        made = layer(media, latents, bucket, cotangent, *[block_shard(v) for v in norms + weights])
        made = finish(*made)
        return (*made[:3], *[own_shard(v) for v in made[3:]])

    rows = P("img", "lat", None)
    shard = P(names)
    wide = P(names, None)
    return jax.shard_map(
        on_device,
        mesh=mesh,
        in_specs=(rows, rows, P("img")) + (shard,) * 6 + (wide,) * 5 + (rows,),
        out_specs=(rows, rows, rows) + (shard,) * 6 + (wide,) * 5,
        check_vma=False,
    )
```

```python
import jax
import jax.numpy as jnp
from jax import lax
from jax.experimental import pallas as pl
from jax.experimental.pallas import tpu as pltpu
from jax.sharding import PartitionSpec as P

MESH = pl.DeviceIdType.MESH
BF16 = jnp.bfloat16
F32 = jnp.float32

SHORT = 256
LONG = 576
HEADS = 8
EPS = 1e-05
SCALE = 0.125
NEG = -1e30

BLOCK = 8

QU = (0, 512)
GN = (512, 128)
KEY = (640, 512)
VAL = (1152, 512)
KV = (640, 1024)
OUT = (1664, 512)
WIDE = 2176
GOUT = (640, 512)
NARROW = 1152
MESSAGES = (106, 132)


def mm(a, b):
    return lax.dot_general(a, b, (((1,), (0,)), ((), ())), preferred_element_type=F32)


def mm_nt(a, b):
    return lax.dot_general(a, b, (((1,), (1,)), ((), ())), preferred_element_type=F32)


def mm_tn(a, b):
    return lax.dot_general(a, b, (((0,), (0,)), ((), ())), preferred_element_type=F32)


def cols(span):
    return pl.ds(span[0], span[1])


def flat(values):
    return values.reshape(-1, values.shape[-1])


def normal(values):
    mean = jnp.mean(values, axis=-1, keepdims=True)
    centred = values - mean
    spread = jnp.mean(centred * centred, axis=-1, keepdims=True)
    return mean, lax.rsqrt(spread + EPS)


def norm_back(upstream, normed, rstd, gain):
    scaled = upstream * gain
    first = jnp.mean(scaled, axis=-1, keepdims=True)
    second = jnp.mean(scaled * normed, axis=-1, keepdims=True)
    return (scaled - first - normed * second) * rstd


class Place:
    def __init__(self):
        img = lax.axis_index("img")
        lat = lax.axis_index("lat")
        self.i = lax.rem(img, BLOCK)
        self.base = img - self.i
        self.z = lax.div(self.i, 2)
        self.x = lax.rem(self.i, 2)
        self.l = lat
        self.y = lax.div(lat, 2)
        self.c = lax.rem(lat, 2)
        self.z1 = self.z + 1 - 2 * lax.rem(self.z, 2)
        self.z2 = lax.rem(self.z + 2, 4)
        self.z3 = 3 - self.z
        self.mid = jnp.logical_or(self.z == 1, self.z == 2)
        self.zs = (self.z, self.z1, self.z2, self.z3)
        self.end = jnp.logical_or(self.z == 0, self.z == 3)
        self.p = self.x * 2 + self.y
        self.q = self.z * 4 + self.p
        self.px = (1 - self.x) * 2 + self.y
        self.py = self.x * 2 + 1 - self.y
        self.pd = 3 - self.p
        self.lc = self.y * 2 + 1 - self.c
        self.ly = (1 - self.y) * 2 + self.c
        self.ld = 3 - self.l
        self.core = self.dev(self.z, self.x, self.y, 1 - self.c)
        self.xn = self.dev(self.z, 1 - self.x, self.y, self.c)
        self.yn = self.dev(self.z, self.x, 1 - self.y, self.c)
        self.diag = self.dev(self.z, 1 - self.x, 1 - self.y, self.c)
        self.ycore = self.dev(self.z, self.x, 1 - self.y, 1 - self.c)
        self.zn1 = self.dev(self.z1, self.x, self.y, self.c)
        self.zn2 = self.dev(self.z2, self.x, self.y, self.c)
        self.zn3 = self.dev(self.z3, self.x, self.y, self.c)

    def dev(self, z, x, y, c):
        return (self.base + z * 2 + x, y * 2 + c)

    def greet(self):
        barrier = pltpu.get_barrier_semaphore()
        peers = (self.core, self.xn, self.yn, self.diag, self.ycore, self.zn1, self.zn2, self.zn3)
        for peer in peers:
            pl.semaphore_signal(barrier, inc=1, device_id=peer, device_id_type=MESH)
        pl.semaphore_wait(barrier, len(peers))


def guarded(when, action):
    if when is None:
        action()
    else:
        pl.when(when)(action)


class Msg:
    def __init__(self, post, src, dst, dev, into, key=None, when=None):
        self.k = post.sends
        post.sends += 1
        self.key = post.key() if key is None else key
        self.when = when
        self.post, self.src, self.dst, self.dev, self.into = post, src, dst, dev, into
        self.done = False
        post.group.append(self)

    def copy(self, src, dst):
        return pltpu.make_async_remote_copy(
            src_ref=src,
            dst_ref=dst,
            send_sem=self.post.send.at[self.k],
            recv_sem=self.post.recv.at[self.key],
            device_id=self.dev,
            device_id_type=MESH,
        )

    def start(self):
        guarded(self.when, lambda: self.copy(self.src, self.dst).start())

    def arrived(self):
        self.copy(self.into, self.into).wait_recv()

    def sent(self):
        if self.done:
            return
        self.done = True
        guarded(self.when, lambda: self.copy(self.src, self.dst).wait_send())


class Post:
    def __init__(self, send, recv):
        self.send, self.recv = send, recv
        self.sends = self.most = self.keys = 0
        self.group, self.spare = [], []

    def key(self):
        if self.spare:
            return self.spare.pop(0)
        self.keys += 1
        return self.keys - 1

    def msg(self, *a, **k):
        return Msg(self, *a, **k)

    def recycle(self):
        group, self.group = self.group, []
        self.most, self.sends = max(self.most, self.sends), 0
        return group

    def drain(self):
        for m in self.recycle():
            m.sent()


class ZGather:
    def __init__(self, post, at, view, core):
        own = view(at.z)
        self.at = at
        self.m1 = post.msg(own, own, at.zn1, view(at.z1))
        self.m2 = post.msg(own, own, at.zn2, view(at.z2))
        self.m3 = post.msg(own, own, at.zn3, view(at.z3), when=at.mid)
        self.relay = post.msg(view(at.z2), view(at.z2), at.zn1, view(at.z3), key=self.m3.key, when=at.mid)
        early = jnp.where(at.mid, at.z2, at.z1)
        late = jnp.where(at.mid, at.z1, at.z2)
        self.core = [core(zz) for zz in (at.z, early, late, at.z3)]

    def start(self):
        pl.when(self.at.mid)(self.m1.start)
        pl.when(self.at.end)(self.m2.start)
        self.core[0].start()

    def far(self):
        @pl.when(self.at.mid)
        def _():
            self.m2.arrived()
            self.relay.start()
            self.m3.start()
            self.m2.start()

        pl.when(self.at.end)(self.m1.start)

    def early(self):
        pl.when(self.at.end)(self.m1.arrived)
        self.core[1].start()

    def last(self):
        pl.when(self.at.mid)(self.m1.arrived)
        pl.when(self.at.end)(self.m2.arrived)
        self.core[2].start()
        self.m3.arrived()
        self.core[3].start()

    def all(self):
        for m in self.core:
            m.arrived()


class PlaneGather:
    def __init__(self, post, at, view, half):
        own = view(at.x, at.y)
        ox, oy = 1 - at.x, 1 - at.y
        self.mx = post.msg(own, own, at.xn, view(ox, at.y))
        self.my = post.msg(own, own, at.yn, view(at.x, oy))
        self.hy = post.msg(half(ox, at.y, 0), half(ox, at.y, 0), at.yn, half(ox, oy, 0))
        self.hx = post.msg(half(at.x, oy, 1), half(at.x, oy, 1), at.xn, half(ox, oy, 1))

    def start(self):
        self.mx.start()
        self.my.start()

    def relay(self):
        self.mx.arrived()
        self.hy.start()
        self.my.arrived()
        self.hx.start()

    def last(self):
        self.hy.arrived()
        self.hx.arrived()


class HalfGather:
    def __init__(self, post, at, half):
        x, y = at.x, at.y
        ox, oy = 1 - x, 1 - y

        def msg(part, dev, into):
            return post.msg(part, part, dev, into)

        self.x0 = msg(half(x, y, 0), at.xn, half(ox, y, 0))
        self.y1 = msg(half(x, y, 1), at.yn, half(x, oy, 1))
        self.x1 = msg(half(x, y, 1), at.xn, half(ox, y, 1))
        self.y0 = msg(half(x, y, 0), at.yn, half(x, oy, 0))
        self.hy = msg(half(ox, y, 0), at.yn, half(ox, oy, 0))
        self.hx = msg(half(x, oy, 1), at.xn, half(ox, oy, 1))

    def start(self):
        self.x0.start()
        self.y1.start()

    def relay0(self):
        self.x0.arrived()
        self.hy.start()

    def relay1(self):
        self.y1.arrived()
        self.hx.start()

    def relay(self):
        self.relay0()
        self.relay1()

    def rest(self):
        self.y0.start()
        self.x1.start()

    def last0(self):
        self.y0.arrived()
        self.hy.arrived()

    def last1(self):
        self.x1.arrived()
        self.hx.arrived()

    def last(self):
        self.last0()
        self.last1()


class Spread:
    def __init__(self, post, at, G, span):
        lanes = cols(span)

        def view(zz, x, y):
            return G.at[zz, x * 2 + y, at.c, :, lanes]

        def half(zz, x, y, h):
            return G.at[zz, x * 2 + y, at.c, pl.ds(16 * h, 16), lanes]

        own = view(at.z, at.x, at.y)
        self.z = [
            post.msg(own, own, dev, view(zz, at.x, at.y))
            for zz, dev in ((at.z1, at.zn1), (at.z2, at.zn2), (at.z3, at.zn3))
        ]
        self.plane = [
            PlaneGather(
                post, at, lambda x, y, zz=zz: view(zz, x, y), lambda x, y, h, zz=zz: half(zz, x, y, h)
            )
            for zz in at.zs
        ]
        self.core = [
            post.msg(
                G.at[zz, :, at.c, :, lanes], G.at[zz, :, at.c, :, lanes], at.core, G.at[zz, :, 1 - at.c, :, lanes]
            )
            for zz in at.zs
        ]

    def start(self):
        for m in self.z:
            m.start()

    def into_plane(self):
        for k in range(3):
            self.z[k].arrived()
            self.plane[k + 1].start()

    def relay(self):
        for g in self.plane:
            g.relay()

    def to_core(self):
        for g, m in zip(self.plane, self.core):
            g.last()
            m.start()

    def arrived(self):
        for m in self.core:
            m.arrived()


class SpreadWide:
    def __init__(self, post, at, G, span, along_x):
        lanes = cols(span)

        def block(zz):
            return G.at[zz, at.p, at.c, :, lanes]

        def column(p):
            return G.at[:, p, at.c, :, lanes]

        own = block(at.z)
        self.z = [
            post.msg(own, own, dev, block(zz))
            for zz, dev in ((at.z1, at.zn1), (at.z2, at.zn2), (at.z3, at.zn3))
        ]
        near, far = ((at.px, at.xn), (at.py, at.yn)) if along_x else ((at.py, at.yn), (at.px, at.xn))
        self.one = post.msg(column(at.p), column(at.p), near[1], column(near[0]))
        self.two = post.msg(column(at.p), column(at.p), far[1], column(far[0]))
        self.on = post.msg(column(near[0]), column(near[0]), far[1], column(at.pd))
        self.core = post.msg(
            G.at[:, :, at.c, :, lanes], G.at[:, :, at.c, :, lanes], at.core, G.at[:, :, 1 - at.c, :, lanes]
        )

    def start(self):
        for m in self.z:
            m.start()

    def along_z(self):
        for m in self.z:
            m.arrived()

    def relay(self):
        self.one.arrived()
        self.on.start()

    def to_core(self):
        self.two.arrived()
        self.on.arrived()
        self.core.start()

    def arrived(self):
        self.core.arrived()


class LatGather:
    def __init__(self, post, at, view):
        self.mc = post.msg(view(at.l), view(at.l), at.core, view(at.lc))
        self.my = post.msg(view(at.l), view(at.l), at.yn, view(at.ly))
        self.fc = post.msg(view(at.ly), view(at.ly), at.core, view(at.ld))

    def start(self):
        self.my.start()
        self.mc.start()

    def relay(self):
        self.my.arrived()
        self.fc.start()

    def last(self):
        self.mc.arrived()
        self.fc.arrived()


class LatReduce:
    def __init__(self, post, at, parts, first, second):
        self.at, self.parts, self.first, self.second = at, parts, first, second
        self.m0 = post.msg(parts.at[at.lc], first.at[0], at.core, first.at[0])
        self.m1 = post.msg(parts.at[at.ld], first.at[1], at.core, first.at[1])
        self.m2 = post.msg(parts.at[at.ly], second, at.yn, second)

    def start(self):
        self.m1.start()
        self.m0.start()

    def relay(self):
        self.m1.arrived()
        ly = self.at.ly
        self.parts[ly] = (self.parts[ly].astype(F32) + self.first[1].astype(F32)).astype(BF16)
        self.m2.start()

    def total(self):
        self.m0.arrived()
        self.m2.arrived()
        near = self.parts[self.at.l].astype(F32) + self.first[0].astype(F32)
        return near + self.second[...].astype(F32)


class HalfReduce:
    def __init__(self, post, at, half, part, near, other, last):
        x, y = at.x, at.y
        ox, oy = 1 - x, 1 - y
        self.near, self.other, self.end = near, other, last
        self.own = part(x, y)
        first, second = (at.yn, at.xn) if half == 0 else (at.xn, at.yn)
        self.there = part(ox, y) if half == 0 else part(x, oy)
        beside = part(x, oy) if half == 0 else part(ox, y)
        self.m1 = post.msg(part(ox, oy), other, first, other)
        self.m0 = post.msg(beside, near, first, near)
        self.f = post.msg(self.there, last, second, last)

    def start(self):
        self.m1.start()
        self.m0.start()

    def relay(self):
        self.m1.arrived()
        self.there[...] = (self.there[...].astype(F32) + self.other[...].astype(F32)).astype(BF16)
        self.f.start()

    def total(self):
        self.m0.arrived()
        self.f.arrived()
        return self.own[...].astype(F32) + self.near[...].astype(F32) + self.end[...].astype(F32)


class PlaneReduceX:
    def __init__(self, post, at, part, mine, other, last, pieces):
        ox, oy = 1 - at.x, 1 - at.y
        self.mine, self.other, self.end = mine, other, last
        self.own, self.there = part(at.x, at.y), part(at.x, oy)
        self.m1 = post.msg(part(ox, oy), other, at.xn, other)
        self.m0 = post.msg(part(ox, at.y), mine, at.xn, mine)
        size = self.there.shape[0] // pieces
        self.f = []
        for k in range(pieces):
            piece = last.at[pl.ds(k * size, size)]
            self.f.append(post.msg(self.there.at[pl.ds(k * size, size)], piece, at.yn, piece))

    def start(self):
        self.m1.start()
        self.m0.start()

    def relay(self):
        self.m1.arrived()
        self.there[...] = (self.there[...].astype(F32) + self.other[...].astype(F32)).astype(BF16)
        self.f[0].start()

    def rest(self):
        self.f[1].start()

    def total(self):
        self.m0.arrived()
        for m in self.f:
            m.arrived()
        total = self.own[...].astype(F32) + self.mine[...].astype(F32)
        return total + self.end[...].astype(F32)


class ZReduce:
    def __init__(self, post, at, term, buf):
        self.at, self.term, self.buf = at, term, buf
        self.m1 = post.msg(term(at.z1), buf(0), at.zn1, buf(0))
        self.m2 = post.msg(term(at.z2), buf(1), at.zn2, buf(1))
        self.m3 = post.msg(term(at.z3), buf(2), at.zn3, buf(2), when=at.mid)
        self.rel = post.msg(term(at.z3), buf(3), at.zn1, buf(3), when=at.end)

    def start_last(self):
        self.rel.start()
        self.m3.start()

    def start_far(self):
        pl.when(self.at.end)(self.m2.start)

    def start_near(self):
        self.m1.start()

    def relay(self):
        @pl.when(self.at.mid)
        def _():
            self.rel.arrived()
            there = self.term(self.at.z2)
            there[...] = (there[...].astype(F32) + self.buf(3)[...].astype(F32)).astype(BF16)
            self.m2.start()

    def total(self, out):
        self.m1.arrived()
        self.m2.arrived()
        value = self.term(self.at.z)[...].astype(F32) + self.buf(0)[...].astype(F32)
        out[...] = value + self.buf(1)[...].astype(F32)

        @pl.when(self.at.mid)
        def _():
            self.m3.arrived()
            out[...] += self.buf(2)[...].astype(F32)


class ZDirect:
    def __init__(self, post, at, term, buf):
        self.at, self.term, self.buf = at, term, buf
        self.msgs = [
            post.msg(term(zz), buf(k), dev, buf(k))
            for k, (zz, dev) in enumerate(((at.z1, at.zn1), (at.z2, at.zn2), (at.z3, at.zn3)))
        ]

    def start(self):
        for m in self.msgs[::-1]:
            m.start()

    def total(self, out):
        value = self.term(self.at.z)[...].astype(F32)
        for k, m in enumerate(self.msgs):
            m.arrived()
            value = value + self.buf(k)[...].astype(F32)
        out[...] = value


class Collect:
    def __init__(self, post, at, grads, near, bufs, bz, src, dst, buf, spare):
        self.at, self.grads, self.near, self.src = at, grads, near, src
        post.spare = list(spare)
        self.lanes, self.there = cols(src), cols(dst)
        into = pl.ds(buf, src[1])
        self.core = post.msg(
            grads.at[:, :, 1 - at.c, :, self.lanes], near.at[:, :, :, self.lanes], at.core,
            near.at[:, :, :, self.lanes],
        )
        self.plane = [
            HalfReduce(
                post,
                at,
                h,
                lambda x, y, h=h: near.at[:, x * 2 + y, pl.ds(16 * h, 16), self.lanes],
                *[b.at[h, :, :, into] for b in bufs],
            )
            for h in range(2)
        ]
        post.spare = []
        self.z = ZDirect(
            post, at, lambda zz: near.at[zz, at.p, :, self.lanes], lambda k: bz.at[k, :, self.there]
        )

    def start(self):
        self.core.start()

    def into_plane(self):
        self.core.arrived()

        def add(zz, carry):
            mine = self.grads[zz, :, self.at.c, :, self.lanes].astype(F32)
            self.near[zz, :, :, self.lanes] = (self.near[zz, :, :, self.lanes].astype(F32) + mine).astype(BF16)
            return carry

        lax.fori_loop(0, 4, add, 0)
        for h in self.plane:
            h.start()

    def relay(self):
        for h in self.plane:
            h.relay()

    def into_z(self):
        for k, h in enumerate(self.plane):
            self.near[:, self.at.p, 16 * k : 16 * k + 16, self.lanes] = h.total().astype(BF16)
        self.z.start()

    def total(self, out):
        self.z.total(out)


class CollectNorms:
    def __init__(self, post, at, grads, near, by, bx, b2, bz, span, spare):
        self.at, self.grads, self.near, self.lanes = at, grads, near, cols(span)
        post.spare = list(spare)
        low = pl.ds(0, 16)

        def part(p):
            return near.at[:, p, low, self.lanes]

        theirs = grads.at[:, :, 1 - at.c, low, self.lanes]
        here = near.at[:, :, low, self.lanes]
        self.core = post.msg(theirs, here, at.core, here)
        self.bufs = [b.at[0, :, :, self.lanes] for b in (bx, by, b2)]
        self.plane = [
            post.msg(part(p), buf, dev, buf)
            for p, buf, dev in zip((at.px, at.py, at.pd), self.bufs, (at.xn, at.yn, at.diag))
        ]
        post.spare = []
        self.z = ZDirect(
            post, at, lambda zz: near.at[zz, at.p, low, self.lanes], lambda k: bz.at[k, low, self.lanes]
        )

    def start(self):
        self.core.start()

    def into_plane(self):
        self.core.arrived()
        mine = self.grads[:, :, self.at.c, 0:16, self.lanes].astype(F32)
        self.near[:, :, 0:16, self.lanes] = (self.near[:, :, 0:16, self.lanes].astype(F32) + mine).astype(BF16)
        for m in self.plane:
            m.start()

    def into_z(self):
        total = self.near[:, self.at.p, 0:16, self.lanes].astype(F32)
        for m, buf in zip(self.plane, self.bufs):
            m.arrived()
            total = total + buf[...].astype(F32)
        self.near[:, self.at.p, 0:16, self.lanes] = total.astype(BF16)
        self.z.start()

    def total(self, out):
        self.z.total(out)


def head_mask():
    rows = lax.div(lax.broadcasted_iota(jnp.int32, (256, 256), 0), 64)
    lanes = lax.div(lax.broadcasted_iota(jnp.int32, (256, 256), 1), 64)
    return (rows == lanes).astype(F32).astype(BF16)


def spread_heads(part, mask):
    rows = part.reshape(64, 256)
    return jnp.concatenate([rows, rows, rows, rows], axis=0) * mask


def gather_heads(wide):
    lane = lax.div(lax.broadcasted_iota(jnp.int32, (64, 256), 1), 64)
    out = jnp.where(lane == 0, wide[0:64], 0.0)
    for h in range(1, 4):
        out = out + jnp.where(lane == h, wide[64 * h : 64 * h + 64], 0.0)
    return out


def pick(values, k):
    out = values[-1]
    for i in range(len(values) - 2, -1, -1):
        out = jnp.where(k == i, values[i], out)
    return out


def span256(n):
    return pl.ds(pl.multiple_of(n * 256, 256), 256)


class Names:
    def __getattr__(self, name):
        return name


class Steps:
    def __init__(self):
        self.made = {}

    def __getattr__(self, name):
        def keep(*actions):
            assert name not in self.made, name
            self.made[name] = actions

        return keep


def order(s):
    return (
        s.load, s.greet, s.staged, s.first_z, s.first_0, s.keys_0, s.up_a, s.stats, s.keys_z, s.first_1, s.first_2,
        s.first_3, s.second_z, s.first_r0, s.first_r1, s.first_r2, s.first_r3, s.keys_1, s.keys_2, s.keys_3,
        s.third_z, s.first_c0, s.first_c1, s.first_c2, s.first_c3, s.down_a, s.up_in, s.up_z, s.keys_r0, s.keys_r1,
        s.keys_r2, s.keys_r3, s.cot_a, s.first_in, s.query, s.q_a, s.second_in, s.second_a, s.keys_c0, s.keys_c1,
        s.keys_c2, s.keys_c3, s.low, s.second_b, s.keys_in, s.pairs_k, s.q_b, s.second_r, s.q_in, s.down_far,
        s.up_far, s.third_in, s.score_0, s.ls_0, s.cot_r, s.score_1, s.ls_1, s.second_c, s.third_a, s.third_b,
        s.second_done, s.pairs_v, s.ls_in0, s.cot_b, s.mix_0, s.third_r, s.mixed_a0, s.ls_in1, s.mix_1, s.mixed_a1,
        s.mixed_b0, s.mixed_b1, s.third_c, s.third_done, s.mixed_in0, s.mixed_in1, s.resid, s.mlp_a, s.mlp_b,
        s.mlp_r0, s.mlp_r1, s.cot_in, s.down_early, s.up_early, s.down_last, s.up_mid, s.up_end, s.down_done,
        s.cot_back, s.up_done, s.mlp_in0, s.mlp_in1, s.gates_0, s.gates_1, s.parts_0, s.recycle, s.back_a0,
        s.parts_1, s.back_a1, s.grad_d3, s.grad_u3, s.grad_d2, s.add_d3, s.grad_u2, s.add_u3, s.back_r0, s.grad_d1,
        s.grad_d0, s.back_r1, s.add_d2, s.add_u2, s.grad_u1, s.grad_u0, s.add_d1, s.add_d0, s.out_parts, s.add_u1,
        s.add_u0, s.back_in0, s.norm_0, s.gm_a0, s.back_in1, s.norm_1, s.gm_a1, s.out_a, s.w_out, s.out_core,
        s.gm_b0, s.gm_in0, s.gm_b1, s.probs_0, s.dl_0, s.gm_in1, s.probs_1, s.dl_1, s.value_0, s.dl_in0, s.out_plane,
        s.scores_0, s.gq_a0, s.dl_in1, s.scores_1, s.gq_a1, s.value_1, s.value_core, s.far_d, s.far_u, s.gq_b0,
        s.gq_b1, s.key_0, s.value_plane, s.out_relay, s.key_1, s.key_core, s.key_plane, s.media_0, s.value_relay,
        s.media_1, s.key_relay, s.media_2, s.out_r, s.gq_in, s.query_core, s.media_3, s.norms, s.norms_core,
        s.query_plane, s.out_z, s.value_z, s.grad_latents, s.norms_plane, s.key_z, s.query_relay, s.out_b, s.sum_d,
        s.sum_u, s.norms_z, s.query_z, s.out_sum, s.value_sum, s.key_sum, s.norms_sum, s.up_out, s.out_in,
        s.query_sum,
    )


def kernel_body(at, post, R):
    images, per_media, _ = R.MED.shape
    per_lat = R.latents.shape[1]
    rows = per_media + per_lat
    tokens = images * per_lat
    half_rows = tokens // 2
    each = images // 2
    zs = at.zs
    halves = (pl.ds(0, half_rows), pl.ds(half_rows, half_rows))
    do = Steps()

    own = R.G.at[at.z, at.p, at.c]
    loads = [
        pltpu.make_async_copy(src, dst, R.local.at[k])
        for k, (src, dst) in enumerate(
            (
                (R.in_media, R.MED),
                (R.in_latents, R.latents),
                (R.in_cotangent, R.cotangent),
                (R.in_query, own.at[:, cols(QU)]),
                (R.in_keyvalue, own.at[:, cols(KV)]),
                (R.in_output.at[:, pl.ds(0, 512)], own.at[pl.ds(0, 16), cols(OUT)]),
                (R.in_output.at[:, pl.ds(512, 512)], own.at[pl.ds(16, 16), cols(OUT)]),
                (R.in_up, R.w_up),
                (R.in_down, R.UD.at[at.z, at.c]),
            )
        )
    ]

    @do.load
    def _():
        for c in loads[3:] + loads[2:3] + loads[:2]:
            c.start()
        norms = [ref[...].astype(F32).reshape(1, 32) for ref in (R.n0, R.n1, R.n2, R.n3, R.n4, R.n5)]
        norms = jnp.concatenate(norms + [jnp.zeros((10, 32), F32)], axis=0)
        norms = jnp.concatenate([norms, norms, norms, norms], axis=1)
        lanes = lax.div(lax.broadcasted_iota(jnp.int32, (16, 128), 1), 32)
        R.G[at.z, at.p, at.c, 0:16, cols(GN)] = jnp.where(lanes == at.l, norms, 0.0).astype(BF16)
        R.G[at.z, at.p, at.c, 16:32, cols(GN)] = jnp.zeros((16, 128), BF16)

    do.greet(at.greet)

    @do.staged
    def _():
        for c in loads[3:]:
            c.wait()
        for p in range(4):
            for zz in range(4):
                for cc in range(2):
                    R.WS[p, :, 128 * (2 * zz + cc) : 128 * (2 * zz + cc) + 128] = R.w_up[
                        :, 128 * (8 * zz + 2 * p + cc) : 128 * (8 * zz + 2 * p + cc) + 128
                    ]
        R.UU[at.z, at.p, at.c] = R.WS[at.p]
        loads[2].wait()
        R.CA[at.p] = R.cotangent[...].reshape(tokens, 1024)

    first = Spread(post, at, R.G, (0, 640))
    keys = Spread(post, at, R.G, KEY)
    second = SpreadWide(post, at, R.G, VAL, True)
    third = SpreadWide(post, at, R.G, OUT, False)
    for name, stream in (("first", first), ("keys", keys)):
        getattr(do, name + "_z")(stream.start)
        getattr(do, name + "_0")(stream.plane[0].start)
        for k in range(1, 4):
            getattr(do, "%s_%d" % (name, k))(stream.z[k - 1].arrived, stream.plane[k].start)
        for k in range(4):
            getattr(do, "%s_r%d" % (name, k))(stream.plane[k].relay)
            getattr(do, "%s_c%d" % (name, k))(stream.plane[k].last, stream.core[k].start)
        getattr(do, name + "_in")(stream.arrived)
    for name, stream in (("second", second), ("third", third)):
        getattr(do, name + "_z")(stream.start)
        getattr(do, name + "_in")(stream.along_z)
        getattr(do, name + "_a")(stream.one.start)
        getattr(do, name + "_b")(stream.two.start)
        getattr(do, name + "_r")(stream.relay)
        getattr(do, name + "_c")(stream.to_core)
        getattr(do, name + "_done")(stream.arrived)

    up = [
        post.msg(R.WS.at[there], R.UU.at[at.z, at.p, at.c], dev, R.UU.at[at.z, there, at.c])
        for there, dev in ((at.px, at.xn), (at.py, at.yn), (at.pd, at.diag))
    ]
    do.up_a(*[m.start for m in up])
    do.up_in(*[m.arrived for m in up])
    d_z = ZGather(
        post,
        at,
        lambda zz: R.UD.at[zz, at.c],
        lambda zz: post.msg(R.UD.at[zz, at.c], R.UD.at[zz, at.c], at.core, R.UD.at[zz, 1 - at.c]),
    )
    u_z = ZGather(
        post,
        at,
        lambda zz: R.UU.at[zz, :, at.c],
        lambda zz: post.msg(R.UU.at[zz, :, at.c], R.UU.at[zz, :, at.c], at.core, R.UU.at[zz, :, 1 - at.c]),
    )
    do.down_a(d_z.start)
    do.down_far(d_z.far)
    do.down_early(d_z.early)
    do.down_last(d_z.last)
    do.down_done(d_z.all)
    do.up_z(u_z.start)
    do.up_far(u_z.far)
    do.up_early(u_z.early)
    do.up_mid(lambda: pl.when(at.mid)(u_z.last))
    do.up_end(lambda: pl.when(at.end)(u_z.last))
    do.up_done(u_z.all)

    cot = HalfGather(post, at, lambda x, y, h: R.CA.at[x * 2 + y, halves[h]])
    do.cot_a(cot.start)
    do.cot_b(cot.rest)
    do.cot_r(cot.relay)
    do.cot_in(cot.last)

    @do.stats
    def _():
        def stats(g, carry):
            mean, rstd = normal(R.MED[g].astype(F32))
            R.MR[g, 0:per_media, 0:1] = mean
            R.MR[g, 0:per_media, 1:2] = rstd
            mean, rstd = normal(R.latents[g].astype(F32))
            R.MR[g, per_media:rows, 0:1] = mean
            R.MR[g, per_media:rows, 1:2] = rstd
            return carry

        loads[0].wait()
        loads[1].wait()
        loop(images, stats)

    @do.query
    def _():
        for i in range(8):
            total = jnp.zeros((16, 128), F32)
            for p in (2 * (i % 2), 2 * (i % 2) + 1):
                for c in range(2):
                    total = total + R.G[i // 2, p, c, 0:16, cols(GN)].astype(F32)
            R.VV[:, 128 * i : 128 * i + 128] = total
        latents = flat(R.latents[...]).astype(F32)
        normed = (latents - flat(R.MR[:, per_media:rows, 0:1])) * flat(R.MR[:, per_media:rows, 1:2])
        latent_low = (normed * R.VV[2:3, :] + R.VV[3:4, :]).astype(BF16)
        R.X[:, per_media:rows, :] = latent_low.reshape(images, per_lat, 1024)
        R.QA[at.l] = mm(latent_low, R.G[:, :, :, :, cols(QU)].reshape(1024, 512)).astype(BF16)

    q_all = LatGather(post, at, lambda l: R.QA.at[l])
    do.q_a(q_all.start)
    do.q_b(q_all.relay)
    do.q_in(q_all.last)

    @do.low
    def _():
        def low(g, carry):
            normed = (R.MED[g].astype(F32) - R.MR[g, 0:per_media, 0:1]) * R.MR[g, 0:per_media, 1:2]
            R.X[g, 0:per_media, :] = (normed * R.VV[0:1, :] + R.VV[1:2, :]).astype(BF16)
            return carry

        loop(images, low)

    def pairs(n, carry):
        weight = R.G[:, :, :, :, pl.ds(pl.multiple_of(KV[0] + n * 256, 128), 256)].reshape(1024, 256)
        made = mm(R.X[...].reshape(images * rows, 1024), weight).astype(BF16)
        R.PR[:, :, span256(n)] = made.reshape(images, rows, 256)
        return carry

    do.pairs_k(lambda: loop((0, 2), pairs))
    do.pairs_v(lambda: loop((2, 4), pairs))

    mask = head_mask()

    def lat_rows(g):
        return pl.ds(pl.multiple_of(g * per_lat, per_lat), per_lat)

    def score(g, carry):
        limit = SHORT + (LONG - SHORT) * R.bucket[g] - at.l * per_media
        row = lax.broadcasted_iota(jnp.int32, (rows, 256), 0)
        valid = jnp.logical_or(row >= per_media, row < limit)
        for half in range(2):
            span = pl.ds(256 * half, 256)
            raw = mm_nt(R.PR[g, :, span], spread_heads(R.QA[:, lat_rows(g), span], mask)) * SCALE
            raw = jnp.where(valid, raw, NEG)
            top = jnp.max(raw, axis=0, keepdims=True)
            total = jnp.sum(jnp.exp(raw - top), axis=0, keepdims=True)
            R.S[2 * g + half] = raw
            R.LS[at.l, pl.ds(2 * g + half, 1), :] = top + jnp.log(total)
        return carry

    def mix(g, carry):
        for half in range(2):
            probs = jnp.exp(R.S[2 * g + half] - R.LG[pl.ds(2 * g + half, 1), :]).astype(BF16)
            R.PB[2 * g + half] = probs
            wide = mm_tn(probs, R.PR[g, :, pl.ds(512 + 256 * half, 256)])
            R.OP[:, lat_rows(g), pl.ds(256 * half, 256)] = (
                gather_heads(wide).reshape(4, per_lat, 256).astype(BF16)
            )
        return carry

    def exchange(ref, span):
        return [
            post.msg(ref.at[at.l, span], ref.at[at.l, span], dev, ref.at[there, span])
            for there, dev in ((at.ly, at.yn), (at.ld, at.ycore), (at.lc, at.core))
        ]

    def log_total(span):
        parts = [R.LS[l, span, :] for l in range(4)]
        top = jnp.maximum(jnp.maximum(parts[0], parts[1]), jnp.maximum(parts[2], parts[3]))
        total = sum(jnp.exp(part - top) for part in parts)
        R.LG[span, :] = top + jnp.log(total)

    lat_keys = []
    for h in range(2):
        here = (each * h, each * h + each)
        span = pl.ds(2 * each * h, 2 * each)
        getattr(do, "score_%d" % h)(lambda here=here: loop(here, score))
        ls = exchange(R.LS, span)
        getattr(do, "ls_%d" % h)(*[m.start for m in ls])
        getattr(do, "ls_in%d" % h)(*[m.arrived for m in ls], lambda span=span: log_total(span))
        getattr(do, "mix_%d" % h)(lambda here=here: loop(here, mix))
        mixed = LatReduce(post, at, R.OP.at[:, halves[h]], R.O1.at[:, halves[h]], R.O2.at[halves[h]])
        lat_keys.append([m.key for m in ls + [mixed.m0, mixed.m1, mixed.m2]])
        getattr(do, "mixed_a%d" % h)(mixed.start)
        getattr(do, "mixed_b%d" % h)(mixed.relay)

        @getattr(do, "mixed_in%d" % h)
        def _(mixed=mixed, h=h):
            R.MX[halves[h], :] = mixed.total().astype(BF16)

    def out_weight():
        left = R.G[:, :, :, 0:16, cols(OUT)].reshape(512, 512)
        return left, R.G[:, :, :, 16:32, cols(OUT)].reshape(512, 512)

    @do.resid
    def _():
        left, right = out_weight()
        latents = flat(R.latents[...]).astype(F32)
        R.RES[:, 0:512] = latents[:, 0:512] + mm(R.MX[...], left)
        R.RES[:, 512:1024] = latents[:, 512:1024] + mm(R.MX[...], right)
        mean, rstd = normal(R.RES[...])
        R.RN[:, 0:1] = mean
        R.RN[:, 1:2] = rstd
        R.MA[at.p] = ((R.RES[...] - mean) * rstd * R.VV[4:5, :] + R.VV[5:6, :]).astype(BF16)

    mlp = HalfGather(post, at, lambda x, y, h: R.MA.at[x * 2 + y, halves[h]])
    do.mlp_a(mlp.start)
    do.mlp_b(mlp.rest)
    do.mlp_r0(mlp.relay0)
    do.mlp_r1(mlp.relay1)
    do.mlp_in0(mlp.last0)
    do.mlp_in1(mlp.last1)

    do.recycle(*[m.sent for m in post.recycle()])
    planes = [m.key for w in (first, keys) for g in w.plane for m in (g.mx, g.my, g.hy, g.hx)]
    cores = [m.key for w in (first, keys) for m in w.core]

    @do.cot_back
    def _():
        def cot_back(f, carry):
            made = mm_nt(R.CA[...].reshape(4 * tokens, 1024), R.UD[f].reshape(256, 1024))
            R.S[pl.ds(4 * f, 4), 0:tokens, :] = made.reshape(4, tokens, 256)
            return carry

        loop(4, cot_back)

    def gates(h):
        part = halves[h]

        def gates(f, carry):
            weight = R.UU[:, :, :, :, span256(f)].reshape(1024, 256)
            gate = mm(R.MA[...].reshape(4 * tokens, 1024), weight)
            back = R.S[pl.ds(4 * f, 4), 0:tokens, :].reshape(4 * tokens, 256)
            phi = 0.5 * (1.0 + lax.erf(gate * 0.7071067811865476))
            R.ACT[:, :, span256(f)] = (gate * phi).astype(BF16).reshape(4, tokens, 256)
            slope = phi + gate * jnp.exp(-0.5 * gate * gate) * 0.3989422804014327
            R.GG[:, :, span256(f)] = (back * slope).astype(BF16).reshape(4, tokens, 256)
            return carry

        loop(4, gates)

    def norm_parts(h):
        part = halves[h]

        def norm_parts(n, carry):
            made = mm_nt(R.GG[:, part, :].reshape(4 * half_rows, 1024), R.UU[n].reshape(256, 1024))
            R.PT[:, part, span256(n)] = made.astype(BF16).reshape(4, half_rows, 256)
            return carry

        loop(4, norm_parts)

    post.spare = [m.key for w in (second, third) for m in (w.one, w.two, w.on)]
    for h in range(2):
        getattr(do, "gates_%d" % h)(*([lambda h=h: gates(h)] if h == 0 else []))
        getattr(do, "parts_%d" % h)(lambda h=h: norm_parts(h))
        back = HalfReduce(
            post, at, h, lambda x, y, h=h: R.PT.at[x * 2 + y, halves[h]], R.PY.at[h], R.PX.at[h], R.P2.at[h]
        )
        getattr(do, "back_a%d" % h)(back.start)
        getattr(do, "back_r%d" % h)(back.relay)

        @getattr(do, "back_in%d" % h)
        def _(back=back, h=h):
            R.U[halves[h], :] = back.total()

    def down_grads(k, carry):
        f = pick(zs, k)
        act = R.ACT[:, :, span256(f)].reshape(4 * tokens, 256)
        R.gD[f] = mm_tn(act, R.CA[...].reshape(4 * tokens, 1024)).astype(BF16).reshape(2, 128, 1024)
        return carry

    def up_grads(k, carry):
        n = pick(zs, k)
        low_rows = R.MA[:, :, span256(n)].reshape(4 * tokens, 256)
        made = mm_tn(low_rows, R.GG[...].reshape(4 * tokens, 1024)).astype(BF16)
        R.gU[n] = made.reshape(4, 2, 32, 1024)
        return carry

    gd_z = ZReduce(post, at, lambda zz: R.RD.at[zz], lambda k: R.ZD.at[k])
    gu_z = ZReduce(post, at, lambda zz: R.RU.at[zz], lambda k: R.ZU.at[k])
    nothing = lambda: None
    gu_c = []
    post.spare = cores
    for k in range(4):
        zz = zs[k]
        gd = post.msg(R.gD.at[zz, 1 - at.c], R.RD.at[zz], at.core, R.RD.at[zz])
        gu = post.msg(R.gU.at[zz, :, 1 - at.c], R.RU.at[zz], at.core, R.RU.at[zz])
        gu_c.append(gu)
        getattr(do, "grad_d%d" % k)(lambda k=k: loop((k, k + 1), down_grads), gd.start)
        getattr(do, "grad_u%d" % k)(lambda k=k: loop((k, k + 1), up_grads), gu.start)

        def add_d(zz=zz):
            R.RD[zz] = (R.RD[zz].astype(F32) + R.gD[zz, at.c].astype(F32)).astype(BF16)

        def add_u(zz=zz):
            R.RU[zz] = (R.RU[zz].astype(F32) + R.gU[zz, :, at.c].astype(F32)).astype(BF16)

        send = (nothing, "start_near", "start_far", "start_last")[k]
        getattr(do, "add_d%d" % k)(gd.arrived, add_d, getattr(gd_z, send) if k else nothing)
        getattr(do, "add_u%d" % k)(gu.arrived, add_u, getattr(gu_z, send) if k else nothing)
    do.far_d(gd_z.relay)
    do.far_u(gu_z.relay)

    @do.out_parts
    def _():
        def out_parts(n, carry):
            made = mm(R.ACT[...].reshape(4 * tokens, 1024), R.UD[:, :, :, span256(n)].reshape(1024, 256))
            R.GG[:, :, span256(n)] = made.astype(BF16).reshape(4, tokens, 256)
            return carry

        loop(4, out_parts)

    out = PlaneReduceX(post, at, lambda x, y: R.GG.at[x * 2 + y], R.OX.at[0], R.OX.at[1], R.OY, 2)
    do.out_a(out.start)
    do.out_r(out.relay)
    do.out_b(out.rest)

    post.spare = [m.key for m in (q_all.mc, q_all.my, q_all.fc, second.core, third.core)]
    for h in range(2):

        @getattr(do, "norm_%d" % h)
        def _(h=h):
            part = halves[h]
            normed = (R.RES[part, :] - R.RN[part, 0:1]) * R.RN[part, 1:2]
            cots = R.CA[at.p, part, :].astype(F32)
            R.GR[part, :] = cots + norm_back(R.U[part, :], normed, R.RN[part, 1:2], R.VV[4:5, :])
            grad_attn = R.GR[part, :].astype(BF16)
            left, right = out_weight()
            made = mm_nt(grad_attn[:, 0:512], left) + mm_nt(grad_attn[:, 512:1024], right)
            R.GM[at.l, part, :] = made.astype(BF16)

        gm = LatGather(post, at, lambda l, h=h: R.GM.at[l, halves[h]])
        getattr(do, "gm_a%d" % h)(gm.start)
        getattr(do, "gm_b%d" % h)(gm.relay)
        getattr(do, "gm_in%d" % h)(gm.last)

    @do.w_out
    def _():
        upstream = R.U[...]
        normed = (R.RES[...] - R.RN[:, 0:1]) * R.RN[:, 1:2]
        R.GS[...] = jnp.zeros_like(R.GS)
        R.GS[4:5, :] = jnp.sum(upstream * normed, axis=0, keepdims=True)
        R.GS[5:6, :] = jnp.sum(upstream, axis=0, keepdims=True)
        grad_attn = R.GR[...].astype(BF16)
        made = mm_tn(R.MX[...], grad_attn[:, 0:512]).astype(BF16)
        R.gA[:, :, :, 0:16, cols(GOUT)] = made.reshape(4, 4, 2, 16, 512)
        made = mm_tn(R.MX[...], grad_attn[:, 512:1024]).astype(BF16)
        R.gA[:, :, :, 16:32, cols(GOUT)] = made.reshape(4, 4, 2, 16, 512)

    bufs = (R.WY, R.WX, R.W2)
    for name, made in (
        ("out", Collect(post, at, R.gA, R.RA, bufs, R.ZW, GOUT, OUT, OUT[0], planes[0:7])),
        ("value", Collect(post, at, R.gU, R.RK, bufs, R.ZW, (512, 512), VAL, VAL[0], planes[7:14])),
        ("key", Collect(post, at, R.gU, R.RK, bufs, R.ZW, (0, 512), KEY, KEY[0], planes[14:21])),
        ("query", Collect(post, at, R.gA, R.RA, bufs, R.ZW, QU, QU, QU[0], planes[21:28])),
        ("norms", CollectNorms(post, at, R.gA, R.RA, R.WY, R.WX, R.W2, R.ZW, GN, planes[28:32])),
    ):
        getattr(do, name + "_core")(made.start)
        getattr(do, name + "_plane")(made.into_plane)
        if name != "norms":
            getattr(do, name + "_relay")(made.relay)
        getattr(do, name + "_z")(made.into_z)
        span = {"out": OUT, "value": VAL, "key": KEY, "query": QU, "norms": GN}[name]
        height = 16 if name == "norms" else 32
        getattr(do, name + "_sum")(lambda made=made, span=span, height=height: made.total(
            R.grad_pack.at[pl.ds(0, height), cols(span)]
        ))

    def grad_probs(g, carry):
        for half in range(2):
            upper = pl.ds(512 + 256 * half, 256)
            wide = spread_heads(R.GM[:, lat_rows(g), pl.ds(256 * half, 256)], mask)
            made = mm_nt(R.PR[g, :, upper], wide)
            probs = R.PB[2 * g + half]
            R.S[2 * g + half] = made
            R.DL[at.l, pl.ds(2 * g + half, 1), :] = jnp.sum(probs.astype(F32) * made, axis=0, keepdims=True)
            R.gP[g, :, upper] = mm(probs, wide).astype(BF16)
        return carry

    def grad_scores(g, carry):
        for half in range(2):
            span = pl.ds(256 * half, 256)
            grads = R.PB[2 * g + half].astype(F32) * (R.S[2 * g + half] - R.LG[pl.ds(2 * g + half, 1), :])
            grads = grads.astype(BF16)
            wide = mm_tn(grads, R.PR[g, :, span]) * SCALE
            R.QP[:, lat_rows(g), span] = gather_heads(wide).reshape(4, per_lat, 256).astype(BF16)
            queries = spread_heads(R.QA[:, lat_rows(g), span], mask)
            R.gP[g, :, span] = (mm(grads, queries) * SCALE).astype(BF16)
        return carry

    def row_terms(span):
        R.LG[span, :] = R.DL[0, span, :] + R.DL[1, span, :] + R.DL[2, span, :] + R.DL[3, span, :]

    sums = []
    for h in range(2):
        here = (each * h, each * h + each)
        span = pl.ds(2 * each * h, 2 * each)
        post.spare = lat_keys[h]
        getattr(do, "probs_%d" % h)(lambda here=here: loop(here, grad_probs))
        dl = exchange(R.DL, span)
        getattr(do, "dl_%d" % h)(*[m.start for m in dl])
        getattr(do, "dl_in%d" % h)(*[m.arrived for m in dl], lambda span=span: row_terms(span))
        getattr(do, "scores_%d" % h)(lambda here=here: loop(here, grad_scores))
        gq = LatReduce(post, at, R.QP.at[:, halves[h]], R.Q1.at[:, halves[h]], R.Q2.at[halves[h]])
        getattr(do, "gq_a%d" % h)(gq.start)
        getattr(do, "gq_b%d" % h)(gq.relay)
        sums.append(gq)

    def kv_grads(n, carry):
        low_rows = R.X[:, :, span256(lax.rem(n, 4))].reshape(images * rows, 256)
        lanes = pl.ds(pl.multiple_of(lax.div(n, 4) * 512, 512), 512)
        made = mm_tn(low_rows, R.gP[:, :, lanes].reshape(images * rows, 512)).astype(BF16)
        R.gU[lax.rem(n, 4), :, :, :, lanes] = made.reshape(4, 2, 32, 512)
        return carry

    do.value_0(*[m.sent for m in gu_c], lambda: loop((4, 6), kv_grads))
    do.value_1(lambda: loop((6, 8), kv_grads))
    do.key_0(lambda: loop((0, 2), kv_grads))
    do.key_1(lambda: loop((2, 4), kv_grads))

    def media_copy(h):
        return pltpu.make_async_copy(R.MG, R.to_media.at[pl.ds(h * 2, 2)], R.local.at[9])

    def media_grads(h, carry):
        span = pl.ds(h * 2, 2)
        weight = R.G[:, :, :, :, cols(KV)].reshape(1024, 1024)
        upstream = mm_nt(R.gP[span].reshape(2 * rows, 1024), weight).reshape(2, rows, 1024)
        R.U[pl.ds(h * 2 * per_lat, 2 * per_lat)] = upstream[:, per_media:rows, :].reshape(2 * per_lat, 1024)
        upstream = upstream[:, 0:per_media, :]
        rstd = R.MR[span, 0:per_media, 1:2]
        normed = (R.MED[span].astype(F32) - R.MR[span, 0:per_media, 0:1]) * rstd
        made = norm_back(upstream, normed, rstd, R.VV[0:1, :]).astype(R.MG.dtype)
        pl.when(h >= 1)(lambda: media_copy(h - 1).wait())
        R.MG[...] = made
        media_copy(h).start()
        R.GS[0:1, :] += jnp.sum(flat(upstream * normed), axis=0, keepdims=True)
        R.GS[1:2, :] += jnp.sum(flat(upstream), axis=0, keepdims=True)
        return carry

    for k in range(4):
        getattr(do, "media_%d" % k)(lambda k=k: loop((k, k + 1), media_grads))

    @do.gq_in
    def _():
        for h in range(2):
            R.GQ[halves[h], :] = sums[h].total().astype(BF16)
        latent_low = flat(R.X[:, per_media:rows, :])
        R.gA[:, :, :, :, cols(QU)] = mm_tn(latent_low, R.GQ[...]).astype(BF16).reshape(4, 4, 2, 32, 512)

    def latent_terms():
        rstd = flat(R.MR[:, per_media:rows, 1:2])
        return (flat(R.latents[...]).astype(F32) - flat(R.MR[:, per_media:rows, 0:1])) * rstd, rstd

    @do.norms
    def _():
        R.U[...] += mm_nt(R.GQ[...], R.G[:, :, :, :, cols(QU)].reshape(1024, 512))
        normed, _ = latent_terms()
        R.GS[2:3, :] = jnp.sum(R.U[...] * normed, axis=0, keepdims=True)
        R.GS[3:4, :] = jnp.sum(R.U[...], axis=0, keepdims=True)
        for i in range(8):
            piece = R.GS[:, 128 * i : 128 * i + 128].astype(BF16)
            for p in (2 * (i % 2), 2 * (i % 2) + 1):
                for c in range(2):
                    R.gA[i // 2, p, c, 0:16, cols(GN)] = piece

    results = [
        pltpu.make_async_copy(src, dst, R.local.at[10 + k])
        for k, (src, dst) in enumerate(
            (
                (R.latents_out, R.to_out),
                (R.grad_latents, R.to_latents),
                (R.grad_down, R.to_down),
                (R.grad_up, R.to_up),
                (R.grad_pack, R.to_pack),
            )
        )
    ]

    @do.grad_latents
    def _():
        normed, rstd = latent_terms()
        R.grad_latents[...] = (R.GR[...] + norm_back(R.U[...], normed, rstd, R.VV[2:3, :])).reshape(
            images, per_lat, 1024
        )
        results[1].start()

    do.sum_d(lambda: gd_z.total(R.grad_down), results[2].start)
    post.spare = [m.key for m in up]
    back_up = [
        post.msg(R.SU.at[there], R.AU.at[at.p], dev, R.AU.at[there])
        for there, dev in ((at.px, at.xn), (at.py, at.yn), (at.pd, at.diag))
    ]

    @do.sum_u
    def _():
        gu_z.total(R.SF)
        R.SU[...] = R.SF[...].astype(BF16)
        R.AU[at.p] = R.SU[at.p]
        for m in back_up:
            m.start()

    @do.up_out
    def _():
        for m in back_up:
            m.arrived()
        for p in range(4):
            for zz in range(4):
                for cc in range(2):
                    R.grad_up[:, 128 * (8 * zz + 2 * p + cc) : 128 * (8 * zz + 2 * p + cc) + 128] = R.AU[
                        p, :, 128 * (2 * zz + cc) : 128 * (2 * zz + cc) + 128
                    ].astype(F32)
        results[3].start()

    @do.out_in
    def _():
        R.latents_out[...] = (R.RES[...] + out.total()).astype(BF16).reshape(images, per_lat, 1024)
        results[0].start()

    names = order(Names())
    assert sorted(names) == sorted(do.made), set(names) ^ set(do.made)
    for name in names:
        with jax.named_scope(name):
            for action in do.made[name]:
                action()
    results[4].start()
    media_copy(images // 2 - 1).wait()
    for c in results:
        c.wait()


def loop(bounds, action):
    first, last = bounds if isinstance(bounds, tuple) else (0, bounds)
    lax.fori_loop(first, last, action, 0)


def place_of(name):
    if name == "bucket":
        return pltpu.SMEM
    return pl.ANY if name.startswith(("in_", "to_")) else pltpu.VMEM


class Refs:
    def __init__(self, names, refs):
        for name, ref in zip(names, refs):
            setattr(self, name, ref)


def build(kernel_body, inputs, outputs, scratch, messages, cid, name):
    in_names = [n for n, _ in inputs]
    out_names = [n for n, _, _ in outputs]
    scratch_names = [n for n, _, _ in scratch]

    def kernel(*refs):
        R = Refs(in_names + out_names + scratch_names, refs)
        at = Place()
        R.local = refs[-3]
        post = Post(refs[-2], refs[-1])
        kernel_body(at, post, R)
        with jax.named_scope('drain'):
            post.drain()
        assert (post.most, post.keys) == messages, (post.most, post.keys)

    specs = [
        pl.BlockSpec(memory_space=place_of(n)) for n in in_names
    ]
    return pl.pallas_call(
        kernel,
        out_shape=[jax.ShapeDtypeStruct(s, d) for _, s, d in outputs],
        in_specs=specs,
        out_specs=[
            pl.BlockSpec(memory_space=place_of(n)) for n, _, _ in outputs
        ],
        scratch_shapes=[pltpu.VMEM(s, d) for _, s, d in scratch]
        + [pltpu.SemaphoreType.DMA((15,))] + [pltpu.SemaphoreType.DMA((n,)) for n in messages],
        compiler_params=pltpu.CompilerParams(
            collective_id=cid, has_side_effects=True, vmem_limit_bytes=62 << 20
        ),
        name=name,
    )(*[v for _, v in inputs])


def layer(media, latents, bucket, cotangent, n0, n1, n2, n3, n4, n5, w_query, w_keyvalue, w_output, w_up, w_down):
    images, per_media, _ = media.shape
    per_lat = latents.shape[1]
    rows = per_media + per_lat
    tokens = images * per_lat
    inputs = [
        ("in_media", media),
        ("in_latents", latents),
        ("in_cotangent", cotangent),
        ("bucket", bucket),
        ("n0", n0),
        ("n1", n1),
        ("n2", n2),
        ("n3", n3),
        ("n4", n4),
        ("n5", n5),
        ("in_query", w_query),
        ("in_keyvalue", w_keyvalue),
        ("in_output", w_output),
        ("in_up", w_up),
        ("in_down", w_down),
    ]
    outputs = [
        ("to_out", (images, per_lat, 1024), BF16),
        ("to_media", (images, per_media, 1024), BF16),
        ("to_latents", (images, per_lat, 1024), F32),
        ("to_pack", (32, WIDE), F32),
        ("to_up", (32, 4096), F32),
        ("to_down", (128, 1024), F32),
    ]
    scratch = [
        ("MED", (images, per_media, 1024), BF16),
        ("X", (images, rows, 1024), BF16),
        ("MR", (images, rows, 2), F32),
        ("PR", (images, rows, 1024), BF16),
        ("S", (2 * images, rows, 256), F32),
        ("PB", (2 * images, rows, 256), BF16),
        ("QA", (4, tokens, 512), BF16),
        ("MX", (tokens, 512), BF16),
        ("RES", (tokens, 1024), F32),
        ("MA", (4, tokens, 1024), BF16),
        ("CA", (4, tokens, 1024), BF16),
        ("UD", (4, 2, 128, 1024), BF16),
        ("UU", (4, 4, 2, 32, 1024), BF16),
        ("G", (4, 4, 2, 32, WIDE), BF16),
        ("VV", (16, 1024), F32),
        ("WS", (4, 32, 1024), BF16),
        ("LS", (4, 2 * images, 256), F32),
        ("LG", (2 * images, 256), F32),
        ("OP", (4, tokens, 512), BF16),
        ("O1", (2, tokens, 512), BF16),
        ("O2", (tokens, 512), BF16),
        ("MG", (2, per_media, 1024), BF16),
        ("RN", (tokens, 2), F32),
        ("latents", (images, per_lat, 1024), BF16),
        ("cotangent", (images, per_lat, 1024), BF16),
        ("w_up", (32, 4096), BF16),
        ("latents_out", (images, per_lat, 1024), BF16),
        ("grad_latents", (images, per_lat, 1024), F32),
        ("grad_pack", (32, WIDE), F32),
        ("grad_up", (32, 4096), F32),
        ("grad_down", (128, 1024), F32),
        ("ACT", (4, tokens, 1024), BF16),
        ("GG", (4, tokens, 1024), BF16),
        ("PT", (4, tokens, 1024), BF16),
        ("PY", (2, tokens // 2, 1024), BF16),
        ("PX", (2, tokens // 2, 1024), BF16),
        ("P2", (2, tokens // 2, 1024), BF16),
        ("OX", (2, tokens, 1024), BF16),
        ("OY", (tokens, 1024), BF16),
        ("gD", (4, 2, 128, 1024), BF16),
        ("gU", (4, 4, 2, 32, 1024), BF16),
        ("RD", (4, 128, 1024), BF16),
        ("RU", (4, 4, 32, 1024), BF16),
        ("ZD", (4, 128, 1024), BF16),
        ("ZU", (4, 4, 32, 1024), BF16),
        ("U", (tokens, 1024), F32),
        ("GR", (tokens, 1024), F32),
        ("GS", (16, 1024), F32),
        ("GM", (4, tokens, 512), BF16),
        ("gP", (images, rows, 1024), BF16),
        ("DL", (4, 2 * images, 256), F32),
        ("QP", (4, tokens, 512), BF16),
        ("Q1", (2, tokens, 512), BF16),
        ("Q2", (tokens, 512), BF16),
        ("GQ", (tokens, 512), BF16),
        ("gA", (4, 4, 2, 32, NARROW), BF16),
        ("RA", (4, 4, 32, NARROW), BF16),
        ("RK", (4, 4, 32, 1024), BF16),
        ("WY", (2, 4, 16, WIDE), BF16),
        ("WX", (2, 4, 16, WIDE), BF16),
        ("W2", (2, 4, 16, WIDE), BF16),
        ("ZW", (3, 32, WIDE), BF16),
        ("SF", (4, 32, 1024), F32),
        ("SU", (4, 32, 1024), BF16),
        ("AU", (4, 32, 1024), BF16),
    ]
    return build(kernel_body, inputs, outputs, scratch, MESSAGES, 1, "resampler")


def finish_body(
    out_in, media_in, latents_in, pack, up_in, down_in, out, media, latents, n0, n1, n2, n3, n4, n5, wq, wkv, wo, wu, wd
):
    rows = wo.shape[0]
    media[...] = media_in[...].astype(F32)

    @pl.when(pl.program_id(0) == 0)
    def _():
        out[...] = out_in[...]
        latents[...] = latents_in[...]
        wu[...] = up_in[...]
        wd[...] = down_in[...]
        wq[...] = pack[:, cols(QU)]
        wkv[...] = pack[:, cols(KV)]
        wo[:, 0:512] = pack[0:rows, cols(OUT)]
        wo[:, 512:1024] = pack[rows : 2 * rows, cols(OUT)]
        mine = pltpu.roll(pack[0:8, cols(GN)], lax.rem(128 - 32 * lax.axis_index("lat"), 128), 1)
        for k, ref in enumerate((n0, n1, n2, n3, n4, n5)):
            ref[...] = mine[k, 0:32]


def finish(latents_out, grad_media, grad_latents, grad_pack, grad_up, grad_down):
    images, per_media, width = grad_media.shape
    block = pl.BlockSpec((images // 2, per_media, width), lambda g: (g, 0, 0))

    def whole(shape):
        return pl.BlockSpec(shape, lambda g: (0,) * len(shape))

    shapes = [
        jax.ShapeDtypeStruct(latents_out.shape, BF16),
        jax.ShapeDtypeStruct(grad_media.shape, F32),
        jax.ShapeDtypeStruct(grad_latents.shape, F32),
    ] + [
        jax.ShapeDtypeStruct(shape, F32)
        for shape in ((32,),) * 6 + ((32, 512), (32, 1024), (16, 1024), grad_up.shape, grad_down.shape)
    ]
    values = (latents_out, grad_media, grad_latents, grad_pack, grad_up, grad_down)
    return pl.pallas_call(
        finish_body,
        grid=(2,),
        out_shape=shapes,
        in_specs=[block if k == 1 else whole(v.shape) for k, v in enumerate(values)],
        out_specs=[block if k == 1 else whole(v.shape) for k, v in enumerate(shapes)],
        compiler_params=pltpu.CompilerParams(vmem_limit_bytes=60 << 20),
        name="finish",
    )(*values)


def solution(mesh):
    sizes = dict(mesh.shape)
    blocks = sizes["img"] // BLOCK
    names = ("img", "lat")

    def block_shard(weight):
        if blocks == 1:
            return weight
        whole = lax.all_gather(weight, names, axis=0, tiled=True)
        each = whole.shape[0] // (BLOCK * sizes["lat"])
        mine = lax.rem(lax.axis_index("img"), BLOCK) * sizes["lat"] + lax.axis_index("lat")
        return lax.dynamic_slice_in_dim(whole, mine * each, each, 0)

    def own_shard(gradient):
        if blocks == 1:
            return gradient
        each = gradient.shape[0]
        mine = lax.rem(lax.axis_index("img"), BLOCK) * sizes["lat"] + lax.axis_index("lat")
        whole = jnp.zeros((each * BLOCK * sizes["lat"],) + gradient.shape[1:], gradient.dtype)
        whole = lax.dynamic_update_slice_in_dim(whole, gradient, mine * each, 0)
        return lax.psum_scatter(whole, names, scatter_dimension=0, tiled=True)

    def on_device(
        media,
        latents,
        bucket,
        gain_media,
        shift_media,
        gain_latent,
        shift_latent,
        gain_mlp,
        shift_mlp,
        w_query,
        w_keyvalue,
        w_output,
        w_up,
        w_down,
        cotangent,
    ):
        norms = (gain_media, shift_media, gain_latent, shift_latent, gain_mlp, shift_mlp)
        weights = (w_query, w_keyvalue, w_output, w_up, w_down)
        made = layer(media, latents, bucket, cotangent, *[block_shard(v) for v in norms + weights])
        made = finish(*made)
        return (*made[:3], *[own_shard(v) for v in made[3:]])

    rows = P("img", "lat", None)
    shard = P(names)
    wide = P(names, None)
    return jax.shard_map(
        on_device,
        mesh=mesh,
        in_specs=(rows, rows, P("img")) + (shard,) * 6 + (wide,) * 5 + (rows,),
        out_specs=(rows, rows, rows) + (shard,) * 6 + (wide,) * 5,
        check_vma=False,
    )
```

```python
import jax
import jax.numpy as jnp
from jax import lax
from jax.experimental import pallas as pl
from jax.experimental.pallas import tpu as pltpu
from jax.sharding import PartitionSpec as P

MESH = pl.DeviceIdType.MESH
BF16 = jnp.bfloat16
F32 = jnp.float32

SHORT = 256
LONG = 576
HEADS = 8
EPS = 1e-05
SCALE = 0.125
NEG = -1e30

BLOCK = 8

QU = (0, 512)
GN = (512, 128)
KEY = (640, 512)
VAL = (1152, 512)
KV = (640, 1024)
OUT = (1664, 512)
WIDE = 2176
GOUT = (640, 512)
NARROW = 1152
MESSAGES = (106, 132)


def mm(a, b):
    return lax.dot_general(a, b, (((1,), (0,)), ((), ())), preferred_element_type=F32)


def mm_nt(a, b):
    return lax.dot_general(a, b, (((1,), (1,)), ((), ())), preferred_element_type=F32)


def mm_tn(a, b):
    return lax.dot_general(a, b, (((0,), (0,)), ((), ())), preferred_element_type=F32)


def cols(span):
    return pl.ds(span[0], span[1])


def flat(values):
    return values.reshape(-1, values.shape[-1])


def normal(values):
    mean = jnp.mean(values, axis=-1, keepdims=True)
    centred = values - mean
    spread = jnp.mean(centred * centred, axis=-1, keepdims=True)
    return mean, lax.rsqrt(spread + EPS)


def norm_back(upstream, normed, rstd, gain):
    scaled = upstream * gain
    first = jnp.mean(scaled, axis=-1, keepdims=True)
    second = jnp.mean(scaled * normed, axis=-1, keepdims=True)
    return (scaled - first - normed * second) * rstd


class Place:
    def __init__(self):
        img = lax.axis_index("img")
        lat = lax.axis_index("lat")
        self.i = lax.rem(img, BLOCK)
        self.base = img - self.i
        self.z = lax.div(self.i, 2)
        self.x = lax.rem(self.i, 2)
        self.l = lat
        self.y = lax.div(lat, 2)
        self.c = lax.rem(lat, 2)
        self.z1 = self.z + 1 - 2 * lax.rem(self.z, 2)
        self.z2 = lax.rem(self.z + 2, 4)
        self.z3 = 3 - self.z
        self.mid = jnp.logical_or(self.z == 1, self.z == 2)
        self.zs = (self.z, self.z1, self.z2, self.z3)
        self.end = jnp.logical_or(self.z == 0, self.z == 3)
        self.p = self.x * 2 + self.y
        self.q = self.z * 4 + self.p
        self.px = (1 - self.x) * 2 + self.y
        self.py = self.x * 2 + 1 - self.y
        self.pd = 3 - self.p
        self.lc = self.y * 2 + 1 - self.c
        self.ly = (1 - self.y) * 2 + self.c
        self.ld = 3 - self.l
        self.core = self.dev(self.z, self.x, self.y, 1 - self.c)
        self.xn = self.dev(self.z, 1 - self.x, self.y, self.c)
        self.yn = self.dev(self.z, self.x, 1 - self.y, self.c)
        self.diag = self.dev(self.z, 1 - self.x, 1 - self.y, self.c)
        self.ycore = self.dev(self.z, self.x, 1 - self.y, 1 - self.c)
        self.zn1 = self.dev(self.z1, self.x, self.y, self.c)
        self.zn2 = self.dev(self.z2, self.x, self.y, self.c)
        self.zn3 = self.dev(self.z3, self.x, self.y, self.c)

    def dev(self, z, x, y, c):
        return (self.base + z * 2 + x, y * 2 + c)

    def greet(self):
        barrier = pltpu.get_barrier_semaphore()
        peers = (self.core, self.xn, self.yn, self.diag, self.ycore, self.zn1, self.zn2, self.zn3)
        for peer in peers:
            pl.semaphore_signal(barrier, inc=1, device_id=peer, device_id_type=MESH)
        pl.semaphore_wait(barrier, len(peers))


def guarded(when, action):
    if when is None:
        action()
    else:
        pl.when(when)(action)


class Msg:
    def __init__(self, post, src, dst, dev, into, key=None, when=None):
        self.k = post.sends
        post.sends += 1
        self.key = post.key() if key is None else key
        self.when = when
        self.post, self.src, self.dst, self.dev, self.into = post, src, dst, dev, into
        self.done = False
        post.group.append(self)

    def copy(self, src, dst):
        return pltpu.make_async_remote_copy(
            src_ref=src,
            dst_ref=dst,
            send_sem=self.post.send.at[self.k],
            recv_sem=self.post.recv.at[self.key],
            device_id=self.dev,
            device_id_type=MESH,
        )

    def start(self):
        guarded(self.when, lambda: self.copy(self.src, self.dst).start())

    def arrived(self):
        self.copy(self.into, self.into).wait_recv()

    def sent(self):
        if self.done:
            return
        self.done = True
        guarded(self.when, lambda: self.copy(self.src, self.dst).wait_send())


class Post:
    def __init__(self, send, recv):
        self.send, self.recv = send, recv
        self.sends = self.most = self.keys = 0
        self.group, self.spare = [], []

    def key(self):
        if self.spare:
            return self.spare.pop(0)
        self.keys += 1
        return self.keys - 1

    def msg(self, *a, **k):
        return Msg(self, *a, **k)

    def recycle(self):
        group, self.group = self.group, []
        self.most, self.sends = max(self.most, self.sends), 0
        return group

    def drain(self):
        for m in self.recycle():
            m.sent()


class ZGather:
    def __init__(self, post, at, view, core):
        own = view(at.z)
        self.at = at
        self.m1 = post.msg(own, own, at.zn1, view(at.z1))
        self.m2 = post.msg(own, own, at.zn2, view(at.z2))
        self.m3 = post.msg(own, own, at.zn3, view(at.z3), when=at.mid)
        self.relay = post.msg(view(at.z2), view(at.z2), at.zn1, view(at.z3), key=self.m3.key, when=at.mid)
        early = jnp.where(at.mid, at.z2, at.z1)
        late = jnp.where(at.mid, at.z1, at.z2)
        self.core = [core(zz) for zz in (at.z, early, late, at.z3)]

    def start(self):
        pl.when(self.at.mid)(self.m1.start)
        pl.when(self.at.end)(self.m2.start)
        self.core[0].start()

    def far(self):
        @pl.when(self.at.mid)
        def _():
            self.m2.arrived()
            self.relay.start()
            self.m3.start()
            self.m2.start()

        pl.when(self.at.end)(self.m1.start)

    def early(self):
        pl.when(self.at.end)(self.m1.arrived)
        self.core[1].start()

    def last(self):
        pl.when(self.at.mid)(self.m1.arrived)
        pl.when(self.at.end)(self.m2.arrived)
        self.core[2].start()
        self.m3.arrived()
        self.core[3].start()

    def all(self):
        for m in self.core:
            m.arrived()


class PlaneGather:
    def __init__(self, post, at, view, half):
        own = view(at.x, at.y)
        ox, oy = 1 - at.x, 1 - at.y
        self.mx = post.msg(own, own, at.xn, view(ox, at.y))
        self.my = post.msg(own, own, at.yn, view(at.x, oy))
        self.hy = post.msg(half(ox, at.y, 0), half(ox, at.y, 0), at.yn, half(ox, oy, 0))
        self.hx = post.msg(half(at.x, oy, 1), half(at.x, oy, 1), at.xn, half(ox, oy, 1))

    def start(self):
        self.mx.start()
        self.my.start()

    def relay(self):
        self.mx.arrived()
        self.hy.start()
        self.my.arrived()
        self.hx.start()

    def last(self):
        self.hy.arrived()
        self.hx.arrived()


class HalfGather:
    def __init__(self, post, at, half):
        x, y = at.x, at.y
        ox, oy = 1 - x, 1 - y

        def msg(part, dev, into):
            return post.msg(part, part, dev, into)

        self.x0 = msg(half(x, y, 0), at.xn, half(ox, y, 0))
        self.y1 = msg(half(x, y, 1), at.yn, half(x, oy, 1))
        self.x1 = msg(half(x, y, 1), at.xn, half(ox, y, 1))
        self.y0 = msg(half(x, y, 0), at.yn, half(x, oy, 0))
        self.hy = msg(half(ox, y, 0), at.yn, half(ox, oy, 0))
        self.hx = msg(half(x, oy, 1), at.xn, half(ox, oy, 1))

    def start(self):
        self.x0.start()
        self.y1.start()

    def relay0(self):
        self.x0.arrived()
        self.hy.start()

    def relay1(self):
        self.y1.arrived()
        self.hx.start()

    def relay(self):
        self.relay0()
        self.relay1()

    def rest(self):
        self.y0.start()
        self.x1.start()

    def last0(self):
        self.y0.arrived()
        self.hy.arrived()

    def last1(self):
        self.x1.arrived()
        self.hx.arrived()

    def last(self):
        self.last0()
        self.last1()


class Spread:
    def __init__(self, post, at, G, span):
        lanes = cols(span)

        def view(zz, x, y):
            return G.at[zz, x * 2 + y, at.c, :, lanes]

        def half(zz, x, y, h):
            return G.at[zz, x * 2 + y, at.c, pl.ds(16 * h, 16), lanes]

        own = view(at.z, at.x, at.y)
        self.z = [
            post.msg(own, own, dev, view(zz, at.x, at.y))
            for zz, dev in ((at.z1, at.zn1), (at.z2, at.zn2), (at.z3, at.zn3))
        ]
        self.plane = [
            PlaneGather(
                post, at, lambda x, y, zz=zz: view(zz, x, y), lambda x, y, h, zz=zz: half(zz, x, y, h)
            )
            for zz in at.zs
        ]
        self.core = [
            post.msg(
                G.at[zz, :, at.c, :, lanes], G.at[zz, :, at.c, :, lanes], at.core, G.at[zz, :, 1 - at.c, :, lanes]
            )
            for zz in at.zs
        ]

    def start(self):
        for m in self.z:
            m.start()

    def into_plane(self):
        for k in range(3):
            self.z[k].arrived()
            self.plane[k + 1].start()

    def relay(self):
        for g in self.plane:
            g.relay()

    def to_core(self):
        for g, m in zip(self.plane, self.core):
            g.last()
            m.start()

    def arrived(self):
        for m in self.core:
            m.arrived()


class SpreadWide:
    def __init__(self, post, at, G, span, along_x):
        lanes = cols(span)

        def block(zz):
            return G.at[zz, at.p, at.c, :, lanes]

        def column(p):
            return G.at[:, p, at.c, :, lanes]

        own = block(at.z)
        self.z = [
            post.msg(own, own, dev, block(zz))
            for zz, dev in ((at.z1, at.zn1), (at.z2, at.zn2), (at.z3, at.zn3))
        ]
        near, far = ((at.px, at.xn), (at.py, at.yn)) if along_x else ((at.py, at.yn), (at.px, at.xn))
        self.one = post.msg(column(at.p), column(at.p), near[1], column(near[0]))
        self.two = post.msg(column(at.p), column(at.p), far[1], column(far[0]))
        self.on = post.msg(column(near[0]), column(near[0]), far[1], column(at.pd))
        self.core = post.msg(
            G.at[:, :, at.c, :, lanes], G.at[:, :, at.c, :, lanes], at.core, G.at[:, :, 1 - at.c, :, lanes]
        )

    def start(self):
        for m in self.z:
            m.start()

    def along_z(self):
        for m in self.z:
            m.arrived()

    def relay(self):
        self.one.arrived()
        self.on.start()

    def to_core(self):
        self.two.arrived()
        self.on.arrived()
        self.core.start()

    def arrived(self):
        self.core.arrived()


class LatGather:
    def __init__(self, post, at, view):
        self.mc = post.msg(view(at.l), view(at.l), at.core, view(at.lc))
        self.my = post.msg(view(at.l), view(at.l), at.yn, view(at.ly))
        self.fc = post.msg(view(at.ly), view(at.ly), at.core, view(at.ld))

    def start(self):
        self.my.start()
        self.mc.start()

    def relay(self):
        self.my.arrived()
        self.fc.start()

    def last(self):
        self.mc.arrived()
        self.fc.arrived()


class LatReduce:
    def __init__(self, post, at, parts, first, second):
        self.at, self.parts, self.first, self.second = at, parts, first, second
        self.m0 = post.msg(parts.at[at.lc], first.at[0], at.core, first.at[0])
        self.m1 = post.msg(parts.at[at.ld], first.at[1], at.core, first.at[1])
        self.m2 = post.msg(parts.at[at.ly], second, at.yn, second)

    def start(self):
        self.m1.start()
        self.m0.start()

    def relay(self):
        self.m1.arrived()
        ly = self.at.ly
        self.parts[ly] = (self.parts[ly].astype(F32) + self.first[1].astype(F32)).astype(BF16)
        self.m2.start()

    def total(self):
        self.m0.arrived()
        self.m2.arrived()
        near = self.parts[self.at.l].astype(F32) + self.first[0].astype(F32)
        return near + self.second[...].astype(F32)


class HalfReduce:
    def __init__(self, post, at, half, part, near, other, last):
        x, y = at.x, at.y
        ox, oy = 1 - x, 1 - y
        self.near, self.other, self.end = near, other, last
        self.own = part(x, y)
        first, second = (at.yn, at.xn) if half == 0 else (at.xn, at.yn)
        self.there = part(ox, y) if half == 0 else part(x, oy)
        beside = part(x, oy) if half == 0 else part(ox, y)
        self.m1 = post.msg(part(ox, oy), other, first, other)
        self.m0 = post.msg(beside, near, first, near)
        self.f = post.msg(self.there, last, second, last)

    def start(self):
        self.m1.start()
        self.m0.start()

    def relay(self):
        self.m1.arrived()
        self.there[...] = (self.there[...].astype(F32) + self.other[...].astype(F32)).astype(BF16)
        self.f.start()

    def total(self):
        self.m0.arrived()
        self.f.arrived()
        return self.own[...].astype(F32) + self.near[...].astype(F32) + self.end[...].astype(F32)


class PlaneReduceX:
    def __init__(self, post, at, part, mine, other, last, pieces):
        ox, oy = 1 - at.x, 1 - at.y
        self.mine, self.other, self.end = mine, other, last
        self.own, self.there = part(at.x, at.y), part(at.x, oy)
        self.m1 = post.msg(part(ox, oy), other, at.xn, other)
        self.m0 = post.msg(part(ox, at.y), mine, at.xn, mine)
        size = self.there.shape[0] // pieces
        self.f = []
        for k in range(pieces):
            piece = last.at[pl.ds(k * size, size)]
            self.f.append(post.msg(self.there.at[pl.ds(k * size, size)], piece, at.yn, piece))

    def start(self):
        self.m1.start()
        self.m0.start()

    def relay(self):
        self.m1.arrived()
        self.there[...] = (self.there[...].astype(F32) + self.other[...].astype(F32)).astype(BF16)
        self.f[0].start()

    def rest(self):
        self.f[1].start()

    def total(self):
        self.m0.arrived()
        for m in self.f:
            m.arrived()
        total = self.own[...].astype(F32) + self.mine[...].astype(F32)
        return total + self.end[...].astype(F32)


class ZReduce:
    def __init__(self, post, at, term, buf):
        self.at, self.term, self.buf = at, term, buf
        self.m1 = post.msg(term(at.z1), buf(0), at.zn1, buf(0))
        self.m2 = post.msg(term(at.z2), buf(1), at.zn2, buf(1))
        self.m3 = post.msg(term(at.z3), buf(2), at.zn3, buf(2), when=at.mid)
        self.rel = post.msg(term(at.z3), buf(3), at.zn1, buf(3), when=at.end)

    def start_last(self):
        self.rel.start()
        self.m3.start()

    def start_far(self):
        pl.when(self.at.end)(self.m2.start)

    def start_near(self):
        self.m1.start()

    def relay(self):
        @pl.when(self.at.mid)
        def _():
            self.rel.arrived()
            there = self.term(self.at.z2)
            there[...] = (there[...].astype(F32) + self.buf(3)[...].astype(F32)).astype(BF16)
            self.m2.start()

    def total(self, out):
        self.m1.arrived()
        self.m2.arrived()
        value = self.term(self.at.z)[...].astype(F32) + self.buf(0)[...].astype(F32)
        out[...] = value + self.buf(1)[...].astype(F32)

        @pl.when(self.at.mid)
        def _():
            self.m3.arrived()
            out[...] += self.buf(2)[...].astype(F32)


class ZDirect:
    def __init__(self, post, at, term, buf):
        self.at, self.term, self.buf = at, term, buf
        self.msgs = [
            post.msg(term(zz), buf(k), dev, buf(k))
            for k, (zz, dev) in enumerate(((at.z1, at.zn1), (at.z2, at.zn2), (at.z3, at.zn3)))
        ]

    def start(self):
        for m in self.msgs[::-1]:
            m.start()

    def total(self, out):
        value = self.term(self.at.z)[...].astype(F32)
        for k, m in enumerate(self.msgs):
            m.arrived()
            value = value + self.buf(k)[...].astype(F32)
        out[...] = value


class Collect:
    def __init__(self, post, at, grads, near, bufs, bz, src, dst, buf, spare):
        self.at, self.grads, self.near, self.src = at, grads, near, src
        post.spare = list(spare)
        self.lanes, self.there = cols(src), cols(dst)
        into = pl.ds(buf, src[1])
        self.core = post.msg(
            grads.at[:, :, 1 - at.c, :, self.lanes], near.at[:, :, :, self.lanes], at.core,
            near.at[:, :, :, self.lanes],
        )
        self.plane = [
            HalfReduce(
                post,
                at,
                h,
                lambda x, y, h=h: near.at[:, x * 2 + y, pl.ds(16 * h, 16), self.lanes],
                *[b.at[h, :, :, into] for b in bufs],
            )
            for h in range(2)
        ]
        post.spare = []
        self.z = ZDirect(
            post, at, lambda zz: near.at[zz, at.p, :, self.lanes], lambda k: bz.at[k, :, self.there]
        )

    def start(self):
        self.core.start()

    def into_plane(self):
        self.core.arrived()

        def add(zz, carry):
            mine = self.grads[zz, :, self.at.c, :, self.lanes].astype(F32)
            self.near[zz, :, :, self.lanes] = (self.near[zz, :, :, self.lanes].astype(F32) + mine).astype(BF16)
            return carry

        lax.fori_loop(0, 4, add, 0)
        for h in self.plane:
            h.start()

    def relay(self):
        for h in self.plane:
            h.relay()

    def into_z(self):
        for k, h in enumerate(self.plane):
            self.near[:, self.at.p, 16 * k : 16 * k + 16, self.lanes] = h.total().astype(BF16)
        self.z.start()

    def total(self, out):
        self.z.total(out)


class CollectNorms:
    def __init__(self, post, at, grads, near, by, bx, b2, bz, span, spare):
        self.at, self.grads, self.near, self.lanes = at, grads, near, cols(span)
        post.spare = list(spare)
        low = pl.ds(0, 16)

        def part(p):
            return near.at[:, p, low, self.lanes]

        theirs = grads.at[:, :, 1 - at.c, low, self.lanes]
        here = near.at[:, :, low, self.lanes]
        self.core = post.msg(theirs, here, at.core, here)
        self.bufs = [b.at[0, :, :, self.lanes] for b in (bx, by, b2)]
        self.plane = [
            post.msg(part(p), buf, dev, buf)
            for p, buf, dev in zip((at.px, at.py, at.pd), self.bufs, (at.xn, at.yn, at.diag))
        ]
        post.spare = []
        self.z = ZDirect(
            post, at, lambda zz: near.at[zz, at.p, low, self.lanes], lambda k: bz.at[k, low, self.lanes]
        )

    def start(self):
        self.core.start()

    def into_plane(self):
        self.core.arrived()
        mine = self.grads[:, :, self.at.c, 0:16, self.lanes].astype(F32)
        self.near[:, :, 0:16, self.lanes] = (self.near[:, :, 0:16, self.lanes].astype(F32) + mine).astype(BF16)
        for m in self.plane:
            m.start()

    def into_z(self):
        total = self.near[:, self.at.p, 0:16, self.lanes].astype(F32)
        for m, buf in zip(self.plane, self.bufs):
            m.arrived()
            total = total + buf[...].astype(F32)
        self.near[:, self.at.p, 0:16, self.lanes] = total.astype(BF16)
        self.z.start()

    def total(self, out):
        self.z.total(out)


def head_mask():
    rows = lax.div(lax.broadcasted_iota(jnp.int32, (256, 256), 0), 64)
    lanes = lax.div(lax.broadcasted_iota(jnp.int32, (256, 256), 1), 64)
    return (rows == lanes).astype(F32).astype(BF16)


def spread_heads(part, mask):
    rows = part.reshape(64, 256)
    return jnp.concatenate([rows, rows, rows, rows], axis=0) * mask


def gather_heads(wide):
    lane = lax.div(lax.broadcasted_iota(jnp.int32, (64, 256), 1), 64)
    out = jnp.where(lane == 0, wide[0:64], 0.0)
    for h in range(1, 4):
        out = out + jnp.where(lane == h, wide[64 * h : 64 * h + 64], 0.0)
    return out


def pick(values, k):
    out = values[-1]
    for i in range(len(values) - 2, -1, -1):
        out = jnp.where(k == i, values[i], out)
    return out


def span256(n):
    return pl.ds(pl.multiple_of(n * 256, 256), 256)


class Names:
    def __getattr__(self, name):
        return name


class Steps:
    def __init__(self):
        self.made = {}

    def __getattr__(self, name):
        def keep(*actions):
            assert name not in self.made, name
            self.made[name] = actions

        return keep


def order(s):
    return (
        s.load, s.greet, s.staged, s.first_z, s.first_0, s.keys_0, s.up_a, s.stats, s.keys_z, s.first_1, s.first_2,
        s.first_3, s.second_z, s.first_r0, s.first_r1, s.first_r2, s.first_r3, s.keys_1, s.keys_2, s.third_z,
        s.keys_3, s.first_c0, s.first_c1, s.first_c2, s.first_c3, s.down_a, s.up_in, s.up_z, s.keys_r0, s.keys_r1,
        s.keys_r2, s.keys_r3, s.cot_a, s.first_in, s.query, s.q_a, s.second_in, s.second_a, s.keys_c0, s.keys_c1,
        s.keys_c2, s.keys_c3, s.low, s.second_b, s.keys_in, s.pairs_k, s.q_b, s.second_r, s.q_in, s.down_far,
        s.up_far, s.score_0, s.ls_0, s.cot_r, s.score_1, s.ls_1, s.second_c, s.third_in, s.third_a, s.third_b,
        s.second_done, s.pairs_v, s.ls_in0, s.cot_b, s.mix_0, s.third_r, s.mixed_a0, s.ls_in1, s.mix_1, s.mixed_a1,
        s.mixed_b0, s.mixed_b1, s.third_c, s.third_done, s.mixed_in0, s.mixed_in1, s.resid, s.mlp_a, s.mlp_b,
        s.mlp_r0, s.mlp_r1, s.cot_in, s.down_early, s.up_early, s.down_last, s.up_mid, s.up_end, s.down_done,
        s.cot_back, s.up_done, s.mlp_in0, s.mlp_in1, s.gates_0, s.gates_1, s.parts_0, s.recycle, s.back_a0,
        s.parts_1, s.back_a1, s.grad_d3, s.grad_u3, s.grad_d2, s.add_d3, s.grad_u2, s.add_u3, s.back_r0, s.grad_d1,
        s.grad_d0, s.back_r1, s.add_d2, s.add_u2, s.grad_u1, s.grad_u0, s.add_d1, s.add_d0, s.out_parts, s.add_u1,
        s.add_u0, s.back_in0, s.norm_0, s.gm_a0, s.back_in1, s.norm_1, s.gm_a1, s.out_a, s.w_out, s.out_core,
        s.gm_b0, s.gm_in0, s.gm_b1, s.probs_0, s.dl_0, s.gm_in1, s.probs_1, s.dl_1, s.value_0, s.dl_in0, s.out_plane,
        s.scores_0, s.gq_a0, s.dl_in1, s.scores_1, s.gq_a1, s.value_1, s.value_core, s.far_d, s.far_u, s.gq_b0,
        s.gq_b1, s.key_0, s.value_plane, s.out_relay, s.key_1, s.key_core, s.key_plane, s.media_0, s.value_relay,
        s.media_1, s.media_2, s.key_relay, s.out_r, s.gq_in, s.query_core, s.media_3, s.norms, s.norms_core,
        s.query_plane, s.out_z, s.value_z, s.grad_latents, s.norms_plane, s.key_z, s.query_relay, s.out_b, s.sum_d,
        s.sum_u, s.norms_z, s.query_z, s.out_sum, s.value_sum, s.key_sum, s.norms_sum, s.up_out, s.out_in,
        s.query_sum,
    )


def kernel_body(at, post, R):
    images, per_media, _ = R.MED.shape
    per_lat = R.latents.shape[1]
    rows = per_media + per_lat
    tokens = images * per_lat
    half_rows = tokens // 2
    each = images // 2
    zs = at.zs
    halves = (pl.ds(0, half_rows), pl.ds(half_rows, half_rows))
    do = Steps()

    own = R.G.at[at.z, at.p, at.c]
    loads = [
        pltpu.make_async_copy(src, dst, R.local.at[k])
        for k, (src, dst) in enumerate(
            (
                (R.in_media, R.MED),
                (R.in_latents, R.latents),
                (R.in_cotangent, R.cotangent),
                (R.in_query, own.at[:, cols(QU)]),
                (R.in_keyvalue, own.at[:, cols(KV)]),
                (R.in_output.at[:, pl.ds(0, 512)], own.at[pl.ds(0, 16), cols(OUT)]),
                (R.in_output.at[:, pl.ds(512, 512)], own.at[pl.ds(16, 16), cols(OUT)]),
                (R.in_up, R.w_up),
                (R.in_down, R.UD.at[at.z, at.c]),
            )
        )
    ]

    @do.load
    def _():
        for c in loads[3:] + loads[2:3] + loads[:2]:
            c.start()
        norms = [ref[...].astype(F32).reshape(1, 32) for ref in (R.n0, R.n1, R.n2, R.n3, R.n4, R.n5)]
        norms = jnp.concatenate(norms + [jnp.zeros((10, 32), F32)], axis=0)
        norms = jnp.concatenate([norms, norms, norms, norms], axis=1)
        lanes = lax.div(lax.broadcasted_iota(jnp.int32, (16, 128), 1), 32)
        R.G[at.z, at.p, at.c, 0:16, cols(GN)] = jnp.where(lanes == at.l, norms, 0.0).astype(BF16)
        R.G[at.z, at.p, at.c, 16:32, cols(GN)] = jnp.zeros((16, 128), BF16)

    do.greet(at.greet)

    @do.staged
    def _():
        for c in loads[3:]:
            c.wait()
        for p in range(4):
            for zz in range(4):
                for cc in range(2):
                    R.WS[p, :, 128 * (2 * zz + cc) : 128 * (2 * zz + cc) + 128] = R.w_up[
                        :, 128 * (8 * zz + 2 * p + cc) : 128 * (8 * zz + 2 * p + cc) + 128
                    ]
        R.UU[at.z, at.p, at.c] = R.WS[at.p]
        loads[2].wait()
        R.CA[at.p] = R.cotangent[...].reshape(tokens, 1024)

    first = Spread(post, at, R.G, (0, 640))
    keys = Spread(post, at, R.G, KEY)
    second = SpreadWide(post, at, R.G, VAL, True)
    third = SpreadWide(post, at, R.G, OUT, False)
    for name, stream in (("first", first), ("keys", keys)):
        getattr(do, name + "_z")(stream.start)
        getattr(do, name + "_0")(stream.plane[0].start)
        for k in range(1, 4):
            getattr(do, "%s_%d" % (name, k))(stream.z[k - 1].arrived, stream.plane[k].start)
        for k in range(4):
            getattr(do, "%s_r%d" % (name, k))(stream.plane[k].relay)
            getattr(do, "%s_c%d" % (name, k))(stream.plane[k].last, stream.core[k].start)
        getattr(do, name + "_in")(stream.arrived)
    for name, stream in (("second", second), ("third", third)):
        getattr(do, name + "_z")(stream.start)
        getattr(do, name + "_in")(stream.along_z)
        getattr(do, name + "_a")(stream.one.start)
        getattr(do, name + "_b")(stream.two.start)
        getattr(do, name + "_r")(stream.relay)
        getattr(do, name + "_c")(stream.to_core)
        getattr(do, name + "_done")(stream.arrived)

    up = [
        post.msg(R.WS.at[there], R.UU.at[at.z, at.p, at.c], dev, R.UU.at[at.z, there, at.c])
        for there, dev in ((at.px, at.xn), (at.py, at.yn), (at.pd, at.diag))
    ]
    do.up_a(*[m.start for m in up])
    do.up_in(*[m.arrived for m in up])
    d_z = ZGather(
        post,
        at,
        lambda zz: R.UD.at[zz, at.c],
        lambda zz: post.msg(R.UD.at[zz, at.c], R.UD.at[zz, at.c], at.core, R.UD.at[zz, 1 - at.c]),
    )
    u_z = ZGather(
        post,
        at,
        lambda zz: R.UU.at[zz, :, at.c],
        lambda zz: post.msg(R.UU.at[zz, :, at.c], R.UU.at[zz, :, at.c], at.core, R.UU.at[zz, :, 1 - at.c]),
    )
    do.down_a(d_z.start)
    do.down_far(d_z.far)
    do.down_early(d_z.early)
    do.down_last(d_z.last)
    do.down_done(d_z.all)
    do.up_z(u_z.start)
    do.up_far(u_z.far)
    do.up_early(u_z.early)
    do.up_mid(lambda: pl.when(at.mid)(u_z.last))
    do.up_end(lambda: pl.when(at.end)(u_z.last))
    do.up_done(u_z.all)

    cot = HalfGather(post, at, lambda x, y, h: R.CA.at[x * 2 + y, halves[h]])
    do.cot_a(cot.start)
    do.cot_b(cot.rest)
    do.cot_r(cot.relay)
    do.cot_in(cot.last)

    @do.stats
    def _():
        def stats(g, carry):
            mean, rstd = normal(R.MED[g].astype(F32))
            R.MR[g, 0:per_media, 0:1] = mean
            R.MR[g, 0:per_media, 1:2] = rstd
            mean, rstd = normal(R.latents[g].astype(F32))
            R.MR[g, per_media:rows, 0:1] = mean
            R.MR[g, per_media:rows, 1:2] = rstd
            return carry

        loads[0].wait()
        loads[1].wait()
        loop(images, stats)

    @do.query
    def _():
        for i in range(8):
            total = jnp.zeros((16, 128), F32)
            for p in (2 * (i % 2), 2 * (i % 2) + 1):
                for c in range(2):
                    total = total + R.G[i // 2, p, c, 0:16, cols(GN)].astype(F32)
            R.VV[:, 128 * i : 128 * i + 128] = total
        latents = flat(R.latents[...]).astype(F32)
        normed = (latents - flat(R.MR[:, per_media:rows, 0:1])) * flat(R.MR[:, per_media:rows, 1:2])
        latent_low = (normed * R.VV[2:3, :] + R.VV[3:4, :]).astype(BF16)
        R.X[:, per_media:rows, :] = latent_low.reshape(images, per_lat, 1024)
        R.QA[at.l] = mm(latent_low, R.G[:, :, :, :, cols(QU)].reshape(1024, 512)).astype(BF16)

    q_all = LatGather(post, at, lambda l: R.QA.at[l])
    do.q_a(q_all.start)
    do.q_b(q_all.relay)
    do.q_in(q_all.last)

    @do.low
    def _():
        def low(g, carry):
            normed = (R.MED[g].astype(F32) - R.MR[g, 0:per_media, 0:1]) * R.MR[g, 0:per_media, 1:2]
            R.X[g, 0:per_media, :] = (normed * R.VV[0:1, :] + R.VV[1:2, :]).astype(BF16)
            return carry

        loop(images, low)

    def pairs(n, carry):
        weight = R.G[:, :, :, :, pl.ds(pl.multiple_of(KV[0] + n * 256, 128), 256)].reshape(1024, 256)
        made = mm(R.X[...].reshape(images * rows, 1024), weight).astype(BF16)
        R.PR[:, :, span256(n)] = made.reshape(images, rows, 256)
        return carry

    do.pairs_k(lambda: loop((0, 2), pairs))
    do.pairs_v(lambda: loop((2, 4), pairs))

    mask = head_mask()

    def lat_rows(g):
        return pl.ds(pl.multiple_of(g * per_lat, per_lat), per_lat)

    def score(g, carry):
        limit = SHORT + (LONG - SHORT) * R.bucket[g] - at.l * per_media
        row = lax.broadcasted_iota(jnp.int32, (rows, 256), 0)
        valid = jnp.logical_or(row >= per_media, row < limit)
        for half in range(2):
            span = pl.ds(256 * half, 256)
            raw = mm_nt(R.PR[g, :, span], spread_heads(R.QA[:, lat_rows(g), span], mask)) * SCALE
            raw = jnp.where(valid, raw, NEG)
            top = jnp.max(raw, axis=0, keepdims=True)
            total = jnp.sum(jnp.exp(raw - top), axis=0, keepdims=True)
            R.S[2 * g + half] = raw
            R.LS[at.l, pl.ds(2 * g + half, 1), :] = top + jnp.log(total)
        return carry

    def mix(g, carry):
        for half in range(2):
            probs = jnp.exp(R.S[2 * g + half] - R.LG[pl.ds(2 * g + half, 1), :]).astype(BF16)
            R.PB[2 * g + half] = probs
            wide = mm_tn(probs, R.PR[g, :, pl.ds(512 + 256 * half, 256)])
            R.OP[:, lat_rows(g), pl.ds(256 * half, 256)] = (
                gather_heads(wide).reshape(4, per_lat, 256).astype(BF16)
            )
        return carry

    def exchange(ref, span):
        return [
            post.msg(ref.at[at.l, span], ref.at[at.l, span], dev, ref.at[there, span])
            for there, dev in ((at.ly, at.yn), (at.ld, at.ycore), (at.lc, at.core))
        ]

    def log_total(span):
        parts = [R.LS[l, span, :] for l in range(4)]
        top = jnp.maximum(jnp.maximum(parts[0], parts[1]), jnp.maximum(parts[2], parts[3]))
        total = sum(jnp.exp(part - top) for part in parts)
        R.LG[span, :] = top + jnp.log(total)

    lat_keys = []
    for h in range(2):
        here = (each * h, each * h + each)
        span = pl.ds(2 * each * h, 2 * each)
        getattr(do, "score_%d" % h)(lambda here=here: loop(here, score))
        ls = exchange(R.LS, span)
        getattr(do, "ls_%d" % h)(*[m.start for m in ls])
        getattr(do, "ls_in%d" % h)(*[m.arrived for m in ls], lambda span=span: log_total(span))
        getattr(do, "mix_%d" % h)(lambda here=here: loop(here, mix))
        mixed = LatReduce(post, at, R.OP.at[:, halves[h]], R.O1.at[:, halves[h]], R.O2.at[halves[h]])
        lat_keys.append([m.key for m in ls + [mixed.m0, mixed.m1, mixed.m2]])
        getattr(do, "mixed_a%d" % h)(mixed.start)
        getattr(do, "mixed_b%d" % h)(mixed.relay)

        @getattr(do, "mixed_in%d" % h)
        def _(mixed=mixed, h=h):
            R.MX[halves[h], :] = mixed.total().astype(BF16)

    def out_weight():
        left = R.G[:, :, :, 0:16, cols(OUT)].reshape(512, 512)
        return left, R.G[:, :, :, 16:32, cols(OUT)].reshape(512, 512)

    @do.resid
    def _():
        left, right = out_weight()
        latents = flat(R.latents[...]).astype(F32)
        R.RES[:, 0:512] = latents[:, 0:512] + mm(R.MX[...], left)
        R.RES[:, 512:1024] = latents[:, 512:1024] + mm(R.MX[...], right)
        mean, rstd = normal(R.RES[...])
        R.RN[:, 0:1] = mean
        R.RN[:, 1:2] = rstd
        R.MA[at.p] = ((R.RES[...] - mean) * rstd * R.VV[4:5, :] + R.VV[5:6, :]).astype(BF16)

    mlp = HalfGather(post, at, lambda x, y, h: R.MA.at[x * 2 + y, halves[h]])
    do.mlp_a(mlp.start)
    do.mlp_b(mlp.rest)
    do.mlp_r0(mlp.relay0)
    do.mlp_r1(mlp.relay1)
    do.mlp_in0(mlp.last0)
    do.mlp_in1(mlp.last1)

    do.recycle(*[m.sent for m in post.recycle()])
    planes = [m.key for w in (first, keys) for g in w.plane for m in (g.mx, g.my, g.hy, g.hx)]
    cores = [m.key for w in (first, keys) for m in w.core]

    @do.cot_back
    def _():
        def cot_back(f, carry):
            made = mm_nt(R.CA[...].reshape(4 * tokens, 1024), R.UD[f].reshape(256, 1024))
            R.S[pl.ds(4 * f, 4), 0:tokens, :] = made.reshape(4, tokens, 256)
            return carry

        loop(4, cot_back)

    def gates(h):
        part = halves[h]

        def gates(f, carry):
            weight = R.UU[:, :, :, :, span256(f)].reshape(1024, 256)
            gate = mm(R.MA[...].reshape(4 * tokens, 1024), weight)
            back = R.S[pl.ds(4 * f, 4), 0:tokens, :].reshape(4 * tokens, 256)
            phi = 0.5 * (1.0 + lax.erf(gate * 0.7071067811865476))
            R.ACT[:, :, span256(f)] = (gate * phi).astype(BF16).reshape(4, tokens, 256)
            slope = phi + gate * jnp.exp(-0.5 * gate * gate) * 0.3989422804014327
            R.GG[:, :, span256(f)] = (back * slope).astype(BF16).reshape(4, tokens, 256)
            return carry

        loop(4, gates)

    def norm_parts(h):
        part = halves[h]

        def norm_parts(n, carry):
            made = mm_nt(R.GG[:, part, :].reshape(4 * half_rows, 1024), R.UU[n].reshape(256, 1024))
            R.PT[:, part, span256(n)] = made.astype(BF16).reshape(4, half_rows, 256)
            return carry

        loop(4, norm_parts)

    post.spare = [m.key for w in (second, third) for m in (w.one, w.two, w.on)]
    for h in range(2):
        getattr(do, "gates_%d" % h)(*([lambda h=h: gates(h)] if h == 0 else []))
        getattr(do, "parts_%d" % h)(lambda h=h: norm_parts(h))
        back = HalfReduce(
            post, at, h, lambda x, y, h=h: R.PT.at[x * 2 + y, halves[h]], R.PY.at[h], R.PX.at[h], R.P2.at[h]
        )
        getattr(do, "back_a%d" % h)(back.start)
        getattr(do, "back_r%d" % h)(back.relay)

        @getattr(do, "back_in%d" % h)
        def _(back=back, h=h):
            R.U[halves[h], :] = back.total()

    def down_grads(k, carry):
        f = pick(zs, k)
        act = R.ACT[:, :, span256(f)].reshape(4 * tokens, 256)
        R.gD[f] = mm_tn(act, R.CA[...].reshape(4 * tokens, 1024)).astype(BF16).reshape(2, 128, 1024)
        return carry

    def up_grads(k, carry):
        n = pick(zs, k)
        low_rows = R.MA[:, :, span256(n)].reshape(4 * tokens, 256)
        made = mm_tn(low_rows, R.GG[...].reshape(4 * tokens, 1024)).astype(BF16)
        R.gU[n] = made.reshape(4, 2, 32, 1024)
        return carry

    gd_z = ZReduce(post, at, lambda zz: R.RD.at[zz], lambda k: R.ZD.at[k])
    gu_z = ZReduce(post, at, lambda zz: R.RU.at[zz], lambda k: R.ZU.at[k])
    nothing = lambda: None
    gu_c = []
    post.spare = cores
    for k in range(4):
        zz = zs[k]
        gd = post.msg(R.gD.at[zz, 1 - at.c], R.RD.at[zz], at.core, R.RD.at[zz])
        gu = post.msg(R.gU.at[zz, :, 1 - at.c], R.RU.at[zz], at.core, R.RU.at[zz])
        gu_c.append(gu)
        getattr(do, "grad_d%d" % k)(lambda k=k: loop((k, k + 1), down_grads), gd.start)
        getattr(do, "grad_u%d" % k)(lambda k=k: loop((k, k + 1), up_grads), gu.start)

        def add_d(zz=zz):
            R.RD[zz] = (R.RD[zz].astype(F32) + R.gD[zz, at.c].astype(F32)).astype(BF16)

        def add_u(zz=zz):
            R.RU[zz] = (R.RU[zz].astype(F32) + R.gU[zz, :, at.c].astype(F32)).astype(BF16)

        send = (nothing, "start_near", "start_far", "start_last")[k]
        getattr(do, "add_d%d" % k)(gd.arrived, add_d, getattr(gd_z, send) if k else nothing)
        getattr(do, "add_u%d" % k)(gu.arrived, add_u, getattr(gu_z, send) if k else nothing)
    do.far_d(gd_z.relay)
    do.far_u(gu_z.relay)

    @do.out_parts
    def _():
        def out_parts(n, carry):
            made = mm(R.ACT[...].reshape(4 * tokens, 1024), R.UD[:, :, :, span256(n)].reshape(1024, 256))
            R.GG[:, :, span256(n)] = made.astype(BF16).reshape(4, tokens, 256)
            return carry

        loop(4, out_parts)

    out = PlaneReduceX(post, at, lambda x, y: R.GG.at[x * 2 + y], R.OX.at[0], R.OX.at[1], R.OY, 2)
    do.out_a(out.start)
    do.out_r(out.relay)
    do.out_b(out.rest)

    post.spare = [m.key for m in (q_all.mc, q_all.my, q_all.fc, second.core, third.core)]
    for h in range(2):

        @getattr(do, "norm_%d" % h)
        def _(h=h):
            part = halves[h]
            normed = (R.RES[part, :] - R.RN[part, 0:1]) * R.RN[part, 1:2]
            cots = R.CA[at.p, part, :].astype(F32)
            R.GR[part, :] = cots + norm_back(R.U[part, :], normed, R.RN[part, 1:2], R.VV[4:5, :])
            grad_attn = R.GR[part, :].astype(BF16)
            left, right = out_weight()
            made = mm_nt(grad_attn[:, 0:512], left) + mm_nt(grad_attn[:, 512:1024], right)
            R.GM[at.l, part, :] = made.astype(BF16)

        gm = LatGather(post, at, lambda l, h=h: R.GM.at[l, halves[h]])
        getattr(do, "gm_a%d" % h)(gm.start)
        getattr(do, "gm_b%d" % h)(gm.relay)
        getattr(do, "gm_in%d" % h)(gm.last)

    @do.w_out
    def _():
        upstream = R.U[...]
        normed = (R.RES[...] - R.RN[:, 0:1]) * R.RN[:, 1:2]
        R.GS[...] = jnp.zeros_like(R.GS)
        R.GS[4:5, :] = jnp.sum(upstream * normed, axis=0, keepdims=True)
        R.GS[5:6, :] = jnp.sum(upstream, axis=0, keepdims=True)
        grad_attn = R.GR[...].astype(BF16)
        made = mm_tn(R.MX[...], grad_attn[:, 0:512]).astype(BF16)
        R.gA[:, :, :, 0:16, cols(GOUT)] = made.reshape(4, 4, 2, 16, 512)
        made = mm_tn(R.MX[...], grad_attn[:, 512:1024]).astype(BF16)
        R.gA[:, :, :, 16:32, cols(GOUT)] = made.reshape(4, 4, 2, 16, 512)

    bufs = (R.WY, R.WX, R.W2)
    for name, made in (
        ("out", Collect(post, at, R.gA, R.RA, bufs, R.ZW, GOUT, OUT, OUT[0], planes[0:7])),
        ("value", Collect(post, at, R.gU, R.RK, bufs, R.ZW, (512, 512), VAL, VAL[0], planes[7:14])),
        ("key", Collect(post, at, R.gU, R.RK, bufs, R.ZW, (0, 512), KEY, KEY[0], planes[14:21])),
        ("query", Collect(post, at, R.gA, R.RA, bufs, R.ZW, QU, QU, QU[0], planes[21:28])),
        ("norms", CollectNorms(post, at, R.gA, R.RA, R.WY, R.WX, R.W2, R.ZW, GN, planes[28:32])),
    ):
        getattr(do, name + "_core")(made.start)
        getattr(do, name + "_plane")(made.into_plane)
        if name != "norms":
            getattr(do, name + "_relay")(made.relay)
        getattr(do, name + "_z")(made.into_z)
        span = {"out": OUT, "value": VAL, "key": KEY, "query": QU, "norms": GN}[name]
        height = 16 if name == "norms" else 32
        getattr(do, name + "_sum")(lambda made=made, span=span, height=height: made.total(
            R.grad_pack.at[pl.ds(0, height), cols(span)]
        ))

    def grad_probs(g, carry):
        for half in range(2):
            upper = pl.ds(512 + 256 * half, 256)
            wide = spread_heads(R.GM[:, lat_rows(g), pl.ds(256 * half, 256)], mask)
            made = mm_nt(R.PR[g, :, upper], wide)
            probs = R.PB[2 * g + half]
            R.S[2 * g + half] = made
            R.DL[at.l, pl.ds(2 * g + half, 1), :] = jnp.sum(probs.astype(F32) * made, axis=0, keepdims=True)
            R.gP[g, :, upper] = mm(probs, wide).astype(BF16)
        return carry

    def grad_scores(g, carry):
        for half in range(2):
            span = pl.ds(256 * half, 256)
            grads = R.PB[2 * g + half].astype(F32) * (R.S[2 * g + half] - R.LG[pl.ds(2 * g + half, 1), :])
            grads = grads.astype(BF16)
            wide = mm_tn(grads, R.PR[g, :, span]) * SCALE
            R.QP[:, lat_rows(g), span] = gather_heads(wide).reshape(4, per_lat, 256).astype(BF16)
            queries = spread_heads(R.QA[:, lat_rows(g), span], mask)
            R.gP[g, :, span] = (mm(grads, queries) * SCALE).astype(BF16)
        return carry

    def row_terms(span):
        R.LG[span, :] = R.DL[0, span, :] + R.DL[1, span, :] + R.DL[2, span, :] + R.DL[3, span, :]

    sums = []
    for h in range(2):
        here = (each * h, each * h + each)
        span = pl.ds(2 * each * h, 2 * each)
        post.spare = lat_keys[h]
        getattr(do, "probs_%d" % h)(lambda here=here: loop(here, grad_probs))
        dl = exchange(R.DL, span)
        getattr(do, "dl_%d" % h)(*[m.start for m in dl])
        getattr(do, "dl_in%d" % h)(*[m.arrived for m in dl], lambda span=span: row_terms(span))
        getattr(do, "scores_%d" % h)(lambda here=here: loop(here, grad_scores))
        gq = LatReduce(post, at, R.QP.at[:, halves[h]], R.Q1.at[:, halves[h]], R.Q2.at[halves[h]])
        getattr(do, "gq_a%d" % h)(gq.start)
        getattr(do, "gq_b%d" % h)(gq.relay)
        sums.append(gq)

    def kv_grads(n, carry):
        low_rows = R.X[:, :, span256(lax.rem(n, 4))].reshape(images * rows, 256)
        lanes = pl.ds(pl.multiple_of(lax.div(n, 4) * 512, 512), 512)
        made = mm_tn(low_rows, R.gP[:, :, lanes].reshape(images * rows, 512)).astype(BF16)
        R.gU[lax.rem(n, 4), :, :, :, lanes] = made.reshape(4, 2, 32, 512)
        return carry

    do.value_0(*[m.sent for m in gu_c], lambda: loop((4, 6), kv_grads))
    do.value_1(lambda: loop((6, 8), kv_grads))
    do.key_0(lambda: loop((0, 2), kv_grads))
    do.key_1(lambda: loop((2, 4), kv_grads))

    def media_copy(h):
        return pltpu.make_async_copy(R.MG, R.to_media.at[pl.ds(h * 2, 2)], R.local.at[9])

    def media_grads(h, carry):
        span = pl.ds(h * 2, 2)
        weight = R.G[:, :, :, :, cols(KV)].reshape(1024, 1024)
        upstream = mm_nt(R.gP[span].reshape(2 * rows, 1024), weight).reshape(2, rows, 1024)
        R.U[pl.ds(h * 2 * per_lat, 2 * per_lat)] = upstream[:, per_media:rows, :].reshape(2 * per_lat, 1024)
        upstream = upstream[:, 0:per_media, :]
        rstd = R.MR[span, 0:per_media, 1:2]
        normed = (R.MED[span].astype(F32) - R.MR[span, 0:per_media, 0:1]) * rstd
        made = norm_back(upstream, normed, rstd, R.VV[0:1, :]).astype(R.MG.dtype)
        pl.when(h >= 1)(lambda: media_copy(h - 1).wait())
        R.MG[...] = made
        media_copy(h).start()
        R.GS[0:1, :] += jnp.sum(flat(upstream * normed), axis=0, keepdims=True)
        R.GS[1:2, :] += jnp.sum(flat(upstream), axis=0, keepdims=True)
        return carry

    for k in range(4):
        getattr(do, "media_%d" % k)(lambda k=k: loop((k, k + 1), media_grads))

    @do.gq_in
    def _():
        for h in range(2):
            R.GQ[halves[h], :] = sums[h].total().astype(BF16)
        latent_low = flat(R.X[:, per_media:rows, :])
        R.gA[:, :, :, :, cols(QU)] = mm_tn(latent_low, R.GQ[...]).astype(BF16).reshape(4, 4, 2, 32, 512)

    def latent_terms():
        rstd = flat(R.MR[:, per_media:rows, 1:2])
        return (flat(R.latents[...]).astype(F32) - flat(R.MR[:, per_media:rows, 0:1])) * rstd, rstd

    @do.norms
    def _():
        R.U[...] += mm_nt(R.GQ[...], R.G[:, :, :, :, cols(QU)].reshape(1024, 512))
        normed, _ = latent_terms()
        R.GS[2:3, :] = jnp.sum(R.U[...] * normed, axis=0, keepdims=True)
        R.GS[3:4, :] = jnp.sum(R.U[...], axis=0, keepdims=True)
        for i in range(8):
            piece = R.GS[:, 128 * i : 128 * i + 128].astype(BF16)
            for p in (2 * (i % 2), 2 * (i % 2) + 1):
                for c in range(2):
                    R.gA[i // 2, p, c, 0:16, cols(GN)] = piece

    results = [
        pltpu.make_async_copy(src, dst, R.local.at[10 + k])
        for k, (src, dst) in enumerate(
            (
                (R.latents_out, R.to_out),
                (R.grad_latents, R.to_latents),
                (R.grad_down, R.to_down),
                (R.grad_up, R.to_up),
                (R.grad_pack, R.to_pack),
            )
        )
    ]

    @do.grad_latents
    def _():
        normed, rstd = latent_terms()
        R.grad_latents[...] = (R.GR[...] + norm_back(R.U[...], normed, rstd, R.VV[2:3, :])).reshape(
            images, per_lat, 1024
        )
        results[1].start()

    do.sum_d(lambda: gd_z.total(R.grad_down), results[2].start)
    post.spare = [m.key for m in up]
    back_up = [
        post.msg(R.SU.at[there], R.AU.at[at.p], dev, R.AU.at[there])
        for there, dev in ((at.px, at.xn), (at.py, at.yn), (at.pd, at.diag))
    ]

    @do.sum_u
    def _():
        gu_z.total(R.SF)
        R.SU[...] = R.SF[...].astype(BF16)
        R.AU[at.p] = R.SU[at.p]
        for m in back_up:
            m.start()

    @do.up_out
    def _():
        for m in back_up:
            m.arrived()
        for p in range(4):
            for zz in range(4):
                for cc in range(2):
                    R.grad_up[:, 128 * (8 * zz + 2 * p + cc) : 128 * (8 * zz + 2 * p + cc) + 128] = R.AU[
                        p, :, 128 * (2 * zz + cc) : 128 * (2 * zz + cc) + 128
                    ].astype(F32)
        results[3].start()

    @do.out_in
    def _():
        R.latents_out[...] = (R.RES[...] + out.total()).astype(BF16).reshape(images, per_lat, 1024)
        results[0].start()

    names = order(Names())
    assert sorted(names) == sorted(do.made), set(names) ^ set(do.made)
    for name in names:
        with jax.named_scope(name):
            for action in do.made[name]:
                action()
    results[4].start()
    media_copy(images // 2 - 1).wait()
    for c in results:
        c.wait()


def loop(bounds, action):
    first, last = bounds if isinstance(bounds, tuple) else (0, bounds)
    lax.fori_loop(first, last, action, 0)


def place_of(name):
    if name == "bucket":
        return pltpu.SMEM
    return pl.ANY if name.startswith(("in_", "to_")) else pltpu.VMEM


class Refs:
    def __init__(self, names, refs):
        for name, ref in zip(names, refs):
            setattr(self, name, ref)


def build(kernel_body, inputs, outputs, scratch, messages, cid, name):
    in_names = [n for n, _ in inputs]
    out_names = [n for n, _, _ in outputs]
    scratch_names = [n for n, _, _ in scratch]

    def kernel(*refs):
        R = Refs(in_names + out_names + scratch_names, refs)
        at = Place()
        R.local = refs[-3]
        post = Post(refs[-2], refs[-1])
        kernel_body(at, post, R)
        with jax.named_scope('drain'):
            post.drain()
        assert (post.most, post.keys) == messages, (post.most, post.keys)

    specs = [
        pl.BlockSpec(memory_space=place_of(n)) for n in in_names
    ]
    return pl.pallas_call(
        kernel,
        out_shape=[jax.ShapeDtypeStruct(s, d) for _, s, d in outputs],
        in_specs=specs,
        out_specs=[
            pl.BlockSpec(memory_space=place_of(n)) for n, _, _ in outputs
        ],
        scratch_shapes=[pltpu.VMEM(s, d) for _, s, d in scratch]
        + [pltpu.SemaphoreType.DMA((15,))] + [pltpu.SemaphoreType.DMA((n,)) for n in messages],
        compiler_params=pltpu.CompilerParams(
            collective_id=cid, has_side_effects=True, vmem_limit_bytes=62 << 20
        ),
        name=name,
    )(*[v for _, v in inputs])


def layer(media, latents, bucket, cotangent, n0, n1, n2, n3, n4, n5, w_query, w_keyvalue, w_output, w_up, w_down):
    images, per_media, _ = media.shape
    per_lat = latents.shape[1]
    rows = per_media + per_lat
    tokens = images * per_lat
    inputs = [
        ("in_media", media),
        ("in_latents", latents),
        ("in_cotangent", cotangent),
        ("bucket", bucket),
        ("n0", n0),
        ("n1", n1),
        ("n2", n2),
        ("n3", n3),
        ("n4", n4),
        ("n5", n5),
        ("in_query", w_query),
        ("in_keyvalue", w_keyvalue),
        ("in_output", w_output),
        ("in_up", w_up),
        ("in_down", w_down),
    ]
    outputs = [
        ("to_out", (images, per_lat, 1024), BF16),
        ("to_media", (images, per_media, 1024), BF16),
        ("to_latents", (images, per_lat, 1024), F32),
        ("to_pack", (32, WIDE), F32),
        ("to_up", (32, 4096), F32),
        ("to_down", (128, 1024), F32),
    ]
    scratch = [
        ("MED", (images, per_media, 1024), BF16),
        ("X", (images, rows, 1024), BF16),
        ("MR", (images, rows, 2), F32),
        ("PR", (images, rows, 1024), BF16),
        ("S", (2 * images, rows, 256), F32),
        ("PB", (2 * images, rows, 256), BF16),
        ("QA", (4, tokens, 512), BF16),
        ("MX", (tokens, 512), BF16),
        ("RES", (tokens, 1024), F32),
        ("MA", (4, tokens, 1024), BF16),
        ("CA", (4, tokens, 1024), BF16),
        ("UD", (4, 2, 128, 1024), BF16),
        ("UU", (4, 4, 2, 32, 1024), BF16),
        ("G", (4, 4, 2, 32, WIDE), BF16),
        ("VV", (16, 1024), F32),
        ("WS", (4, 32, 1024), BF16),
        ("LS", (4, 2 * images, 256), F32),
        ("LG", (2 * images, 256), F32),
        ("OP", (4, tokens, 512), BF16),
        ("O1", (2, tokens, 512), BF16),
        ("O2", (tokens, 512), BF16),
        ("MG", (2, per_media, 1024), BF16),
        ("RN", (tokens, 2), F32),
        ("latents", (images, per_lat, 1024), BF16),
        ("cotangent", (images, per_lat, 1024), BF16),
        ("w_up", (32, 4096), BF16),
        ("latents_out", (images, per_lat, 1024), BF16),
        ("grad_latents", (images, per_lat, 1024), F32),
        ("grad_pack", (32, WIDE), F32),
        ("grad_up", (32, 4096), F32),
        ("grad_down", (128, 1024), F32),
        ("ACT", (4, tokens, 1024), BF16),
        ("GG", (4, tokens, 1024), BF16),
        ("PT", (4, tokens, 1024), BF16),
        ("PY", (2, tokens // 2, 1024), BF16),
        ("PX", (2, tokens // 2, 1024), BF16),
        ("P2", (2, tokens // 2, 1024), BF16),
        ("OX", (2, tokens, 1024), BF16),
        ("OY", (tokens, 1024), BF16),
        ("gD", (4, 2, 128, 1024), BF16),
        ("gU", (4, 4, 2, 32, 1024), BF16),
        ("RD", (4, 128, 1024), BF16),
        ("RU", (4, 4, 32, 1024), BF16),
        ("ZD", (4, 128, 1024), BF16),
        ("ZU", (4, 4, 32, 1024), BF16),
        ("U", (tokens, 1024), F32),
        ("GR", (tokens, 1024), F32),
        ("GS", (16, 1024), F32),
        ("GM", (4, tokens, 512), BF16),
        ("gP", (images, rows, 1024), BF16),
        ("DL", (4, 2 * images, 256), F32),
        ("QP", (4, tokens, 512), BF16),
        ("Q1", (2, tokens, 512), BF16),
        ("Q2", (tokens, 512), BF16),
        ("GQ", (tokens, 512), BF16),
        ("gA", (4, 4, 2, 32, NARROW), BF16),
        ("RA", (4, 4, 32, NARROW), BF16),
        ("RK", (4, 4, 32, 1024), BF16),
        ("WY", (2, 4, 16, WIDE), BF16),
        ("WX", (2, 4, 16, WIDE), BF16),
        ("W2", (2, 4, 16, WIDE), BF16),
        ("ZW", (3, 32, WIDE), BF16),
        ("SF", (4, 32, 1024), F32),
        ("SU", (4, 32, 1024), BF16),
        ("AU", (4, 32, 1024), BF16),
    ]
    return build(kernel_body, inputs, outputs, scratch, MESSAGES, 1, "resampler")


def finish_body(
    out_in, media_in, latents_in, pack, up_in, down_in, out, media, latents, n0, n1, n2, n3, n4, n5, wq, wkv, wo, wu, wd
):
    rows = wo.shape[0]
    media[...] = media_in[...].astype(F32)

    @pl.when(pl.program_id(0) == 0)
    def _():
        out[...] = out_in[...]
        latents[...] = latents_in[...]
        wu[...] = up_in[...]
        wd[...] = down_in[...]
        wq[...] = pack[:, cols(QU)]
        wkv[...] = pack[:, cols(KV)]
        wo[:, 0:512] = pack[0:rows, cols(OUT)]
        wo[:, 512:1024] = pack[rows : 2 * rows, cols(OUT)]
        mine = pltpu.roll(pack[0:8, cols(GN)], lax.rem(128 - 32 * lax.axis_index("lat"), 128), 1)
        for k, ref in enumerate((n0, n1, n2, n3, n4, n5)):
            ref[...] = mine[k, 0:32]


def finish(latents_out, grad_media, grad_latents, grad_pack, grad_up, grad_down):
    images, per_media, width = grad_media.shape
    block = pl.BlockSpec((images // 2, per_media, width), lambda g: (g, 0, 0))

    def whole(shape):
        return pl.BlockSpec(shape, lambda g: (0,) * len(shape))

    shapes = [
        jax.ShapeDtypeStruct(latents_out.shape, BF16),
        jax.ShapeDtypeStruct(grad_media.shape, F32),
        jax.ShapeDtypeStruct(grad_latents.shape, F32),
    ] + [
        jax.ShapeDtypeStruct(shape, F32)
        for shape in ((32,),) * 6 + ((32, 512), (32, 1024), (16, 1024), grad_up.shape, grad_down.shape)
    ]
    values = (latents_out, grad_media, grad_latents, grad_pack, grad_up, grad_down)
    return pl.pallas_call(
        finish_body,
        grid=(2,),
        out_shape=shapes,
        in_specs=[block if k == 1 else whole(v.shape) for k, v in enumerate(values)],
        out_specs=[block if k == 1 else whole(v.shape) for k, v in enumerate(shapes)],
        compiler_params=pltpu.CompilerParams(vmem_limit_bytes=60 << 20),
        name="finish",
    )(*values)


def solution(mesh):
    sizes = dict(mesh.shape)
    blocks = sizes["img"] // BLOCK
    names = ("img", "lat")

    def block_shard(weight):
        if blocks == 1:
            return weight
        whole = lax.all_gather(weight, names, axis=0, tiled=True)
        each = whole.shape[0] // (BLOCK * sizes["lat"])
        mine = lax.rem(lax.axis_index("img"), BLOCK) * sizes["lat"] + lax.axis_index("lat")
        return lax.dynamic_slice_in_dim(whole, mine * each, each, 0)

    def own_shard(gradient):
        if blocks == 1:
            return gradient
        each = gradient.shape[0]
        mine = lax.rem(lax.axis_index("img"), BLOCK) * sizes["lat"] + lax.axis_index("lat")
        whole = jnp.zeros((each * BLOCK * sizes["lat"],) + gradient.shape[1:], gradient.dtype)
        whole = lax.dynamic_update_slice_in_dim(whole, gradient, mine * each, 0)
        return lax.psum_scatter(whole, names, scatter_dimension=0, tiled=True)

    def on_device(
        media,
        latents,
        bucket,
        gain_media,
        shift_media,
        gain_latent,
        shift_latent,
        gain_mlp,
        shift_mlp,
        w_query,
        w_keyvalue,
        w_output,
        w_up,
        w_down,
        cotangent,
    ):
        norms = (gain_media, shift_media, gain_latent, shift_latent, gain_mlp, shift_mlp)
        weights = (w_query, w_keyvalue, w_output, w_up, w_down)
        made = layer(media, latents, bucket, cotangent, *[block_shard(v) for v in norms + weights])
        made = finish(*made)
        return (*made[:3], *[own_shard(v) for v in made[3:]])

    rows = P("img", "lat", None)
    shard = P(names)
    wide = P(names, None)
    return jax.shard_map(
        on_device,
        mesh=mesh,
        in_specs=(rows, rows, P("img")) + (shard,) * 6 + (wide,) * 5 + (rows,),
        out_specs=(rows, rows, rows) + (shard,) * 6 + (wide,) * 5,
        check_vma=False,
    )
```
